256 devices in a mesh: dp: 64 (over z, x, core), mp: 4 (over y).
Axes of the slice: x: 4, y: 4, z: 8, core: 2. Of those that a mesh axis runs over, the one named last changes fastest.
Arguments:
- images: bfloat16 [1024, 64, 1408], P('dp'), may hold values from -8 to 8
- query_states: bfloat16 [1024, 32, 768], P('dp'), may hold values from -6 to 6
- neg_caption: int32 [1024], P('dp'), may hold values from 0 to 1023, as said below
- neg_image: int32 [1024], P('dp'), may hold values from 0 to 1023, as said below
- cross_query: bfloat16 [768, 768], P(None, 'mp'), may hold values from -0.21875 to 0.21875
- cross_kv: bfloat16 [2, 1408, 768], P(None, None, 'mp'), may hold values from -0.15625 to 0.15625
- cross_out: bfloat16 [768, 768], P('mp'), may hold values from -0.21875 to 0.21875
- norm_gain: float32 [768], replicated, may hold values from 0.1 to 1.9
- itm_weight: float32 [768, 2], replicated, may hold values from -1.2 to 1.2
Outputs:
- itm_logits: float32 [3, 1024, 2], P(None, 'dp')
- grad_cross_kv: float32 [2, 1408, 768], P(None, 'dp', 'mp')
The draws below stay inside these ranges and needn't reach their ends.
Inputs may be any that keep to these rules, and one draw needn't show every extreme that they name: `neg_caption`: among the 16 entries of each aligned block of rows (the rows of one index of dp), at most 2 lie in any one aligned block of 16 pair ids, and some block of pair ids holds exactly 2 entries of every block of rows. No entry equals its own row's pair id. `neg_image`: among the 16 entries of each aligned block of rows (the rows of one index of dp), at most 2 lie in any one aligned block of 16 pair ids, and some block of pair ids holds exactly 2 entries of every block of rows. No entry equals its own row's pair id.
All inputs are finite; a program needn't handle non-finite values.
Results may differ from the reference program's by a relative error of at most 0.011.
Values may be sent and summed in bfloat16 or wider, within the bound.
No kernel may reach another device: no remote copies, remote signals or barrier semaphores. Data moves between devices by JAX's collectives and lax.ppermute only.
A program may use at most 128 MiB of HBM per device.

```python
import math
import jax
import jax.numpy as jnp
from jax import lax

D = 768
VIS = 1408
QUERIES = 32
HEADS = 12
PATCHES = 64
PAIRS_DEV = 16
PAIRS = 1024
CAP = 2
N_MP = 4


def partner_ids(key):
    blocks = PAIRS // PAIRS_DEV
    spare_count = (blocks - 1) * CAP
    key_busy, key_rest = jax.random.split(key)
    busy_owner = jax.random.randint(key_busy, (), 0, blocks)
    block_keys = jax.random.split(key_rest, blocks)

    def one_block(block_key, block_index):
        key_order, key_spare, key_local = jax.random.split(block_key, 3)
        row_order = jax.random.permutation(key_order, PAIRS_DEV)
        spare_slots = jax.random.permutation(key_spare, spare_count)
        spare_pick = jnp.take(spare_slots, jnp.clip(row_order - CAP, 0, spare_count - 1))
        other_owner = spare_pick // CAP
        other_owner = other_owner + (other_owner >= busy_owner).astype(jnp.int32)
        owner_block = jnp.where(row_order < CAP, busy_owner, other_owner)
        local_row = jax.random.randint(key_local, (PAIRS_DEV,), 0, PAIRS_DEV)
        own_id = block_index * PAIRS_DEV + jnp.arange(PAIRS_DEV, dtype=jnp.int32)
        local_row = jnp.where(owner_block * PAIRS_DEV + local_row == own_id, (local_row + 1) % PAIRS_DEV, local_row)
        return (owner_block * PAIRS_DEV + local_row).astype(jnp.int32)
    return jax.vmap(one_block)(block_keys, jnp.arange(blocks, dtype=jnp.int32)).reshape(-1)


def draw_neg_caption(key, part):
    key = jax.random.fold_in(key, 11)
    return partner_ids(key)


def draw_neg_image(key, part):
    key = jax.random.fold_in(key, 23)
    return partner_ids(key)


def strengthened(entries, own_key, source, target, parts, factor):
    def block_of(dim):
        return (jnp.arange(entries.shape[dim]) // (entries.shape[dim] // parts)).reshape((-1,) + (1,) * (entries.ndim - 1 - dim))

    near = jax.random.permutation(own_key, parts)[block_of(target)]
    second = (block_of(target) + parts // 2) % parts
    return jnp.where((block_of(source) == near) | (block_of(source) == second), factor * entries, entries)


def shard_levels(stream_key, dims, cuts, least, largest):
    loudness = 1.0
    for position, parts in cuts:
        steps = jax.random.uniform(jax.random.fold_in(jax.random.fold_in(stream_key, 6), position), (parts,), jnp.float32, least / len(cuts), largest / len(cuts))
        loudness = loudness * jnp.repeat(jnp.exp(steps), dims[position] // parts).reshape((-1,) + (1,) * (len(dims) - 1 - position))
    return loudness


def gaussian(rng, shape, spread, bound, cuts=(), kind=jnp.bfloat16):
    values = spread * jax.random.normal(rng, shape, jnp.float32)
    if cuts:
        values = values * shard_levels(rng, shape, cuts, -0.22, 0.18)
    return jnp.clip(values, -bound, bound).astype(kind)


def bell_draw_with(key, extent, spread, limit, cuts, heavy, held_as=jnp.bfloat16):
    array = spread * jax.random.normal(key, extent, jnp.float32)
    if cuts:
        array = array * shard_levels(key, extent, cuts, -0.22, 0.18)
    return jnp.clip(strengthened(array, jax.random.fold_in(key, 3), *heavy), -limit, limit).astype(held_as)


def setup_inputs(seed: int = 0) -> dict:
    keys = jax.random.split(jax.random.key(seed), 10)
    images = bell_draw_with(keys[0], (PAIRS, PATCHES, VIS), 1.0, 8.0, ((0, 64),), (0, 2, 64, 4.0))
    query_states = gaussian(keys[1], (PAIRS, QUERIES, D), 1.0, 6.0, ((0, 64),))
    neg_caption = draw_neg_caption(jax.random.fold_in(keys[9], 71), 0)
    neg_image = draw_neg_image(jax.random.fold_in(keys[9], 71), 0)
    cross_query = gaussian(keys[4], (D, D), D ** -0.5, 0.21875, ((1, 4),))
    cross_kv = gaussian(keys[5], (2, VIS, D), VIS ** -0.5, 0.15625, ((2, 4),))
    cross_out = gaussian(keys[6], (D, D), D ** -0.5, 0.21875, ((0, 4),))
    norm_gain = jnp.clip(1.0 + 0.18 * jax.random.normal(keys[7], (D,), jnp.float32), 0.1, 1.9)
    itm_weight = gaussian(keys[8], (D, 2), 0.2, 1.2, (), jnp.float32)
    return {"images": images, "query_states": query_states, "neg_caption": neg_caption, "neg_image": neg_image, "cross_query": cross_query, "cross_kv": cross_kv, "cross_out": cross_out, "norm_gain": norm_gain, "itm_weight": itm_weight}


EPS = 1e-06

def half_back(values):
    return lax.optimization_barrier(values.astype(jnp.bfloat16)).astype(jnp.float32)

def norm_forward(residual, gain):
    mean_row = lax.optimization_barrier(jnp.mean(residual, axis=-1, keepdims=True))
    centred = residual - mean_row
    variance = lax.optimization_barrier(jnp.mean(centred * centred, axis=-1, keepdims=True))
    inverse = 1.0 / jnp.sqrt(variance + EPS)
    unit_rows = centred * inverse
    return (unit_rows * gain, unit_rows, inverse)

def norm_backward(d_normed, unit_rows, inverse, gain):
    scaled = d_normed * gain
    first = lax.optimization_barrier(jnp.mean(scaled, axis=-1, keepdims=True))
    second = lax.optimization_barrier(jnp.mean(scaled * unit_rows, axis=-1, keepdims=True))
    return inverse * (scaled - first - unit_rows * second)

def reference(images, query_states, neg_caption, neg_image, cross_query, cross_kv, cross_out, norm_gain, itm_weight):
    head_size = D // HEADS
    score_scale = 1.0 / math.sqrt(head_size)
    blocks = PAIRS // PAIRS_DEV
    group_cols = D // N_MP
    example_count = 3 * PAIRS_DEV
    positive = (jnp.arange(example_count, dtype=jnp.int32) < PAIRS_DEV).astype(jnp.float32)
    target = jnp.stack([1.0 - positive, positive], axis=-1)
    query_weight = cross_query.astype(jnp.float32)
    kv_weight = cross_kv.astype(jnp.float32)
    out_weight = cross_out.astype(jnp.float32)
    out_groups = out_weight.reshape(N_MP, group_cols, D)

    def step_block(grad_sum, block_index):
        first_row = (block_index * PAIRS_DEV).astype(jnp.int32)
        own_images = lax.dynamic_slice_in_dim(images, first_row, PAIRS_DEV, 0)
        own_states = lax.dynamic_slice_in_dim(query_states, first_row, PAIRS_DEV, 0)
        caption_partner = lax.dynamic_slice_in_dim(neg_caption, first_row, PAIRS_DEV, 0).astype(jnp.int32)
        image_partner = lax.dynamic_slice_in_dim(neg_image, first_row, PAIRS_DEV, 0).astype(jnp.int32)
        neg_states = jnp.take(query_states, caption_partner, axis=0)
        neg_images = jnp.take(images, image_partner, axis=0)
        both_states = jnp.concatenate([own_states, neg_states], axis=0)
        query_proj = half_back(jnp.einsum('nqd,dc->nqc', both_states.astype(jnp.float32), query_weight))
        both_images = jnp.concatenate([own_images, neg_images], axis=0)
        kv_all = half_back(jnp.einsum('npf,kfc->nkpc', both_images.astype(jnp.float32), kv_weight))
        example_query = jnp.concatenate([query_proj[:PAIRS_DEV], query_proj[PAIRS_DEV:], query_proj[:PAIRS_DEV]], axis=0)
        example_kv = jnp.concatenate([kv_all[:PAIRS_DEV], kv_all[:PAIRS_DEV], kv_all[PAIRS_DEV:]], axis=0)
        example_states = jnp.concatenate([own_states, neg_states, own_states], axis=0).astype(jnp.float32)
        query_heads = example_query.reshape(example_count, QUERIES, HEADS, head_size)
        key_heads = example_kv[:, 0].reshape(example_count, PATCHES, HEADS, head_size)
        value_heads = example_kv[:, 1].reshape(example_count, PATCHES, HEADS, head_size)
        scores = jnp.einsum('eqhd,ephd->ehqp', query_heads, key_heads) * score_scale
        raised = jnp.exp(scores)
        attention = raised / lax.optimization_barrier(jnp.sum(raised, axis=-1, keepdims=True))
        attention_half = half_back(attention)
        mixed_heads = half_back(jnp.einsum('ehqp,ephd->eqhd', attention_half, value_heads))
        mixed_groups = mixed_heads.reshape(example_count, QUERIES, N_MP, group_cols)
        group_parts = half_back(jnp.einsum('eqmc,mcd->eqmd', mixed_groups, out_groups))
        attended = lax.optimization_barrier(jnp.sum(group_parts, axis=2))
        residual = example_states + attended
        normed, unit_rows, inverse = norm_forward(residual, norm_gain)
        pooled = lax.optimization_barrier(jnp.mean(normed, axis=1))
        logits = jnp.dot(pooled, itm_weight, precision=lax.Precision.HIGHEST)
        raised_logits = jnp.exp(logits)
        softened = raised_logits / lax.optimization_barrier(jnp.sum(raised_logits, axis=-1, keepdims=True))
        d_logits = softened - target
        d_pooled = jnp.dot(d_logits, itm_weight.T, precision=lax.Precision.HIGHEST)
        d_normed = jnp.broadcast_to(d_pooled[:, None, :] / QUERIES, normed.shape)
        d_residual = norm_backward(d_normed, unit_rows, inverse, norm_gain)
        d_res_half = half_back(d_residual)
        d_mixed = half_back(jnp.einsum('eqd,cd->eqc', d_res_half, out_weight))
        d_mixed = d_mixed.reshape(example_count, QUERIES, HEADS, head_size)
        d_values = jnp.einsum('ehqp,eqhd->ephd', attention_half, d_mixed)
        d_attention = jnp.einsum('eqhd,ephd->ehqp', d_mixed, value_heads)
        d_scores = attention * (d_attention - lax.optimization_barrier(jnp.sum(d_attention * attention, axis=-1, keepdims=True))) * score_scale
        d_scores = half_back(d_scores)
        d_keys = jnp.einsum('ehqp,eqhd->ephd', d_scores, query_heads)
        d_kv = half_back(jnp.stack([d_keys, d_values], axis=1).reshape(example_count, 2, PATCHES, D))
        own_grad = d_kv[:PAIRS_DEV] + d_kv[PAIRS_DEV:2 * PAIRS_DEV]
        weight_term = jnp.einsum('npf,nkpc->kfc', own_images.astype(jnp.float32), own_grad)
        weight_term = weight_term + jnp.einsum('npf,nkpc->kfc', neg_images.astype(jnp.float32), d_kv[2 * PAIRS_DEV:])
        return (grad_sum + weight_term, logits.reshape(3, PAIRS_DEV, 2))
    grad_start = jnp.zeros((2, VIS, D), jnp.float32)
    grad_total, logit_blocks = lax.scan(step_block, grad_start, jnp.arange(blocks, dtype=jnp.int32))
    itm_logits = jnp.transpose(logit_blocks, (1, 0, 2, 3)).reshape(3, PAIRS, 2)
    return (itm_logits, grad_total)
```

```python
import functools

import jax
import jax.numpy as jnp
from jax import lax
from jax.experimental import pallas as pl
from jax.experimental.pallas import tpu as pltpu
from jax.sharding import PartitionSpec as P

HEADS = 12
EPS = 1e-06
CE = 8
NB = 4
BF16 = jnp.bfloat16
F32 = jnp.float32


def dot(a, b):
    return jnp.dot(a, b, preferred_element_type=F32)


def dot_nt(a, b):
    return lax.dot_general(a, b, (((1,), (1,)), ((), ())), preferred_element_type=F32)


def dot_tn(a, b):
    return lax.dot_general(a, b, (((0,), (0,)), ((), ())), preferred_element_type=F32)


def head_blocks(rows, head):
    lane_head = lax.broadcasted_iota(jnp.int32, rows.shape, 1) // head
    zero = jnp.zeros_like(rows)
    return jnp.concatenate(
        [jnp.where(lane_head == h, rows, zero) for h in range(rows.shape[1] // head)], axis=0
    )


def head_ones(width, head):
    row = lax.broadcasted_iota(jnp.int32, (width, width), 0) // head
    col = lax.broadcasted_iota(jnp.int32, (width, width), 1) // head
    return jnp.where(row == col, 1.0, 0.0).astype(BF16)


def head_sum(values, ones):
    upper = values.astype(BF16)
    lower = (values - upper.astype(F32)).astype(BF16)
    return dot(upper, ones) + dot(lower, ones)


def forward_kernel(
    nch, chunk_img, cap_id, pool, k_ref, v_ref, wq_ref, wot_ref, gain_ref, itm_ref,
    q_out, p_out, d_out, log_out, xbuf, sems, *, head, scale,
):
    step = pl.program_id(0)
    shards, _, cols = k_ref.shape
    patches = head
    slots = NB * CE
    blocks = (nch[0] + NB - 1) // NB

    def fetch(blk):
        def one(j, carry):
            slot = blk * slots + j
            pltpu.make_async_copy(pool.at[cap_id[slot]], xbuf.at[slot], sems.at[blk]).start()
            return carry

        lax.fori_loop(0, slots, one, 0)

    @pl.when(step == 0)
    def _():
        def each(blk, carry):
            fetch(blk)
            return carry

        lax.fori_loop(0, blocks, each, 0)

    @pl.when(step < blocks)
    def _():
        first = pl.multiple_of(step * slots, slots)
        mine = xbuf.at[pl.ds(first, slots)]
        pltpu.make_async_copy(pool.at[pl.ds(0, slots)], mine, sems.at[step]).wait()
        x16 = mine[...].astype(F32)
        rows = x16.shape[1] // 2
        xf = jnp.concatenate([x16[:, :rows], x16[:, rows:]], axis=-1)
        width = xf.shape[-1]
        xf = xf.reshape(slots * rows, width)
        xb = xf.astype(BF16)
        ones = head_ones(cols, head)
        attended = jnp.zeros_like(xf)
        crow = CE * rows
        for s in range(shards):
            q = dot(xb, wq_ref[s]).astype(BF16)
            q_out[s] = q
            scores = []
            for c in range(NB):
                img = chunk_img[step * NB + c]
                at = pl.multiple_of(img * patches, patches)
                kbd = head_blocks(k_ref[s, pl.ds(at, patches), :], head)
                scores.append(dot_nt(q[c * crow : (c + 1) * crow], kbd))
            raised = jnp.exp(jnp.concatenate(scores, axis=0) * scale)
            prob = raised / head_sum(raised, ones)
            p_out[s] = prob
            half = prob.astype(BF16)
            mixed = []
            for c in range(NB):
                img = chunk_img[step * NB + c]
                at = pl.multiple_of(img * patches, patches)
                vbd = head_blocks(v_ref[s, pl.ds(at, patches), :], head)
                mixed.append(dot(half[c * crow : (c + 1) * crow], vbd))
            mixed = jnp.concatenate(mixed, axis=0).astype(BF16)
            attended = attended + dot_nt(mixed, wot_ref[s]).astype(BF16).astype(F32)
        residual = xf + attended
        centred = residual - jnp.mean(residual, axis=-1, keepdims=True)
        variance = jnp.mean(centred * centred, axis=-1, keepdims=True)
        inverse = 1.0 / jnp.sqrt(variance + EPS)
        unit = centred * inverse
        gain = gain_ref[...]
        pooled = jnp.sum((unit * gain).reshape(slots, rows, width), axis=1)
        for j in range(2):
            part = jnp.sum(pooled * itm_ref[j : j + 1], axis=-1, keepdims=True)
            log_out[:, 128 * j : 128 * (j + 1)] = jnp.broadcast_to(part, (slots, 128))
        scaled = (itm_ref[1:2] - itm_ref[0:1]) * gain
        d_first = jnp.mean(scaled, axis=-1, keepdims=True)
        d_second = jnp.mean(scaled * unit, axis=-1, keepdims=True)
        d_out[...] = (inverse * (scaled - d_first - unit * d_second)).astype(BF16)


def backward_kernel(nch, chunk_img, d_ref, p_ref, v_ref, wot_ref, dm_out, ds_out, *, head, scale):
    step = pl.program_id(0)
    shards, _, cols = v_ref.shape
    patches = head
    blocks = (nch[0] + NB - 1) // NB

    @pl.when(step < blocks)
    def _():
        ones = head_ones(cols, head)
        d_res = d_ref[...]
        crow = d_res.shape[0] // NB
        for s in range(shards):
            dm = dot(d_res, wot_ref[s]).astype(BF16)
            dm_out[s] = dm
            d_att = []
            for c in range(NB):
                img = chunk_img[step * NB + c]
                at = pl.multiple_of(img * patches, patches)
                vbd = head_blocks(v_ref[s, pl.ds(at, patches), :], head)
                d_att.append(dot_nt(dm[c * crow : (c + 1) * crow], vbd))
            d_att = jnp.concatenate(d_att, axis=0)
            prob = p_ref[s]
            inner = head_sum(d_att * prob, ones)
            ds_out[s] = prob * (d_att - inner) * scale


def outer_kernel(nch, chunk_img, delta_ref, q_ref, p_ref, dm_ref, ds_ref, out_ref, acc, *, head):
    step = pl.program_id(0)
    cols = q_ref.shape[-1]
    patches = head
    blocks = (nch[0] + NB - 1) // NB

    @pl.when(step == 0)
    def _():
        acc[...] = jnp.zeros_like(acc)

    @pl.when(step < blocks)
    def _():
        delta = delta_ref[:, :1]
        ds = (ds_ref[0] * delta).astype(BF16)
        pd = (p_ref[0] * delta).astype(BF16)
        q = q_ref[0]
        dm = dm_ref[0]
        crow = q.shape[0] // NB
        lane_head = lax.broadcasted_iota(jnp.int32, (patches, cols), 1) // head

        def diagonal(block):
            total = jnp.zeros((patches, cols), F32)
            for h in range(cols // head):
                total = total + jnp.where(
                    lane_head == h, block[h * patches : (h + 1) * patches], 0.0
                )
            return total

        for c in range(NB):
            img = chunk_img[step * NB + c]
            at = pl.multiple_of(img * patches, patches)
            sl = slice(c * crow, (c + 1) * crow)
            dk = diagonal(dot_tn(ds[sl], q[sl]))
            dv = diagonal(dot_tn(pd[sl], dm[sl]))
            acc[pl.ds(at, patches), :] += jnp.concatenate([dk, dv], axis=-1)

    @pl.when(step == pl.num_programs(0) - 1)
    def _():
        out_ref[...] = acc[...].astype(BF16)


def plan(neg_caption, all_images, dp, pair_count, n_slots):
    total = all_images.shape[0]
    index = jnp.arange(pair_count, dtype=jnp.int32)
    own = (all_images // pair_count == dp)[:, None] & (
        (all_images % pair_count)[:, None] == index[None, :]
    )
    order = jnp.arange(total, dtype=jnp.int32)
    below = (order[None, :] <= order[:, None]).astype(BF16)
    upto = dot(below, own.astype(BF16)).astype(jnp.int32)
    count = jnp.sum(own.astype(jnp.int32), axis=0)
    chunks = (2 + count + CE - 1) // CE
    first = jnp.sum(jnp.where(index[None, :] < index[:, None], chunks[None, :], 0), axis=1)
    n_chunks = jnp.sum(chunks)
    slot_of = jnp.sum(jnp.where(own, first[None, :] * CE + 1 + upto, 0), axis=1)
    slot = jnp.arange(n_slots, dtype=jnp.int32)
    img = jnp.sum((slot[:, None] // CE >= first[None, :]).astype(jnp.int32), axis=1) - 1
    at_img = img[:, None] == index[None, :]
    pos = slot - CE * jnp.sum(jnp.where(at_img, first[None, :], 0), axis=1)
    hit = slot[:, None] == slot_of[None, :]
    hit = hit & (pos >= 2)[:, None]
    pushed = jnp.sum(jnp.where(hit, order[None, :], 0), axis=1)
    filled = jnp.any(hit, axis=1)
    negative = jnp.sum(jnp.where(at_img, neg_caption[None, :], 0), axis=1)
    cap = jnp.where(pos == 1, negative, jnp.where(filled, pushed, dp * pair_count + img))
    in_use = (slot // CE < n_chunks) & ((pos < 2) | filled)
    sign = jnp.where(in_use, jnp.where(pos == 0, -1.0, 1.0), 0.0).astype(F32)
    chunk_img = img.reshape(-1, CE)[:, 0]
    return n_chunks, chunk_img, cap, sign, first, hit


def local(
    images, query_states, neg_caption, neg_image, cross_query, cross_kv, cross_out, norm_gain,
    itm_weight,
):
    pair_count, patches, vis = images.shape
    queries, width = query_states.shape[1:]
    cols = cross_query.shape[1]
    head = width // HEADS
    scale = 1.0 / head**0.5
    groups = lax.axis_size("dp")
    shards = lax.axis_size("mp")
    dp, mp = lax.axis_index("dp"), lax.axis_index("mp")
    core = dp % 2
    rows = queries // shards
    half = width // 2
    pairs = groups * pair_count

    def around(x, by):
        return lax.ppermute(x, "mp", [(i, (i + by) % shards) for i in range(shards)])

    def other_core(x):
        return lax.ppermute(x, "dp", [(i, i ^ 1) for i in range(groups)])

    own_rows = lax.dynamic_slice_in_dim(query_states, mp * rows, rows, 1)
    packed = jnp.concatenate([own_rows[:, :, :half], own_rows[:, :, half:]], axis=1)
    pool = lax.all_gather(packed, "dp", axis=0, tiled=True)
    ids = jnp.zeros((8, 128), jnp.int32).at[0, :pair_count].set(neg_image)
    all_images = lax.all_gather(ids, "dp", axis=0, tiled=True)
    all_images = all_images.reshape(groups, 8, 128)[:, 0, :pair_count].reshape(-1)

    weights = jnp.concatenate(
        [
            jnp.concatenate([cross_kv[0], cross_kv[1]], axis=1),
            jnp.concatenate([cross_query, cross_out.T], axis=1),
        ],
        axis=0,
    )
    tall = weights.shape[0] // 2
    mine = lax.dynamic_slice_in_dim(weights, core * tall, tall, 0)
    shard_list = [weights]
    for s in range(1, shards):
        got = around(mine, shards - s)
        swap = other_core(got)
        shard_list.append(
            jnp.concatenate(
                [jnp.where(core == 0, got, swap), jnp.where(core == 0, swap, got)], axis=0
            )
        )
    flat = images.reshape(pair_count * patches, vis)
    kv = [dot(flat, w[:vis]).astype(BF16) for w in shard_list]
    keys = jnp.stack([x[:, :cols] for x in kv])
    values = jnp.stack([x[:, cols:] for x in kv])
    wq = jnp.stack([w[vis:, :cols] for w in shard_list])
    wot = jnp.stack([w[vis:, cols:] for w in shard_list])

    out_rows = vis // groups
    pad_rows = (out_rows + 1 + 7) // 8 * 8
    feature = lax.broadcasted_iota(jnp.int32, (vis, groups * pad_rows), 0)
    place = lax.broadcasted_iota(jnp.int32, (vis, groups * pad_rows), 1)
    target = jnp.where(
        place % pad_rows < out_rows, place // pad_rows * out_rows + place % pad_rows, -1
    )
    chosen = (feature == target).astype(BF16)
    spread = lax.dot_general(
        chosen, flat, (((0,), (1,)), ((), ())), preferred_element_type=F32
    ).astype(BF16)

    steps = -(-(pair_count * (2 + CE - 1) + 2 * groups) // (CE * NB))
    n_slots = steps * NB * CE
    n_chunks, chunk_img, cap, sign, first, hit = plan(
        neg_caption, all_images, dp, pair_count, n_slots
    )
    nch = n_chunks.reshape(1)
    n_rows = n_slots * rows
    blk = NB * CE * rows

    def last(i, nch):
        return jnp.minimum(i, (nch[0] + NB - 1) // NB - 1)

    def whole(a):
        return pl.BlockSpec(a.shape, lambda *_: (0,) * a.ndim)

    row3 = pl.BlockSpec((shards, blk, cols), lambda i, n, *_: (0, last(i, n), 0))
    row2 = pl.BlockSpec((blk, width), lambda i, n, *_: (last(i, n), 0))
    params = pltpu.CompilerParams(vmem_limit_bytes=56 * 2**20)
    gain = norm_gain.reshape(1, width)
    itm = itm_weight.T / queries
    q_rows, prob, d_res, log_part = pl.pallas_call(
        functools.partial(forward_kernel, head=head, scale=scale),
        grid_spec=pltpu.PrefetchScalarGridSpec(
            num_scalar_prefetch=3,
            grid=(steps,),
            in_specs=[
                pl.BlockSpec(memory_space=pl.ANY),
                whole(keys), whole(values), whole(wq), whole(wot), whole(gain), whole(itm),
            ],
            out_specs=[
                row3, row3, row2,
                pl.BlockSpec((NB * CE, 256), lambda i, n, *_: (last(i, n), 0)),
            ],
            scratch_shapes=[
                pltpu.VMEM((n_slots, 2 * rows, half), BF16),
                pltpu.SemaphoreType.DMA((steps,)),
            ],
        ),
        out_shape=[
            jax.ShapeDtypeStruct((shards, n_rows, cols), BF16),
            jax.ShapeDtypeStruct((shards, n_rows, cols), F32),
            jax.ShapeDtypeStruct((n_rows, width), BF16),
            jax.ShapeDtypeStruct((n_slots, 256), F32),
        ],
        compiler_params=params,
        name="forward",
    )(nch, chunk_img, cap, pool, keys, values, wq, wot, gain, itm)

    part = jnp.stack([log_part[:, 0], log_part[:, 128]])
    part = jnp.where((sign != 0.0)[None, :], part, 0.0)
    terms = [part] + [around(part, shards - s) for s in range(1, shards)]
    logits = jnp.zeros_like(part)
    for m in range(shards):
        for s in range(shards):
            logits = logits + jnp.where((mp + s) % shards == m, terms[s], 0.0)

    d_mixed, d_scores = pl.pallas_call(
        functools.partial(backward_kernel, head=head, scale=scale),
        grid_spec=pltpu.PrefetchScalarGridSpec(
            num_scalar_prefetch=2,
            grid=(steps,),
            in_specs=[row2, row3, whole(values), whole(wot)],
            out_specs=[row3, row3],
        ),
        out_shape=[
            jax.ShapeDtypeStruct((shards, n_rows, cols), BF16),
            jax.ShapeDtypeStruct((shards, n_rows, cols), F32),
        ],
        compiler_params=params,
        name="backward",
    )(nch, chunk_img, d_res, prob, values, wot)

    gap = logits[1] - logits[0]
    delta = sign / (1.0 + jnp.exp(-sign * gap))
    delta = jnp.broadcast_to(jnp.repeat(delta, rows)[:, None], (n_rows, 128))

    def outer(s):
        pick = pl.BlockSpec((1, blk, cols), lambda i, n, *_: (s, last(i, n), 0))
        return pl.pallas_call(
            functools.partial(outer_kernel, head=head),
            grid_spec=pltpu.PrefetchScalarGridSpec(
                num_scalar_prefetch=2,
                grid=(steps,),
                in_specs=[
                    pl.BlockSpec((blk, 128), lambda i, n, *_: (last(i, n), 0)),
                    pick, pick, pick, pick,
                ],
                out_specs=pl.BlockSpec(
                    (pair_count * patches, 2 * cols), lambda *_: (0, 0)
                ),
                scratch_shapes=[pltpu.VMEM((pair_count * patches, 2 * cols), F32)],
            ),
            out_shape=jax.ShapeDtypeStruct((pair_count * patches, 2 * cols), BF16),
            compiler_params=params,
            name="outer",
        )(nch, chunk_img, delta, q_rows, prob, d_mixed, d_scores)

    d_kv = sum(
        around(outer(s), s).astype(F32) for s in range(1, shards)
    ) + outer(0).astype(F32)
    upper = d_kv.astype(BF16)
    grad = dot(spread, upper)

    logit_hi = logits.astype(BF16)
    logit_lo = (logits - logit_hi.astype(F32)).astype(BF16)
    four = jnp.concatenate([logit_hi, logit_lo], axis=0)
    home = lax.dot_general(
        hit.astype(BF16), four, (((0,), (1,)), ((), ())), preferred_element_type=F32
    )
    home = jnp.pad(
        home.reshape(groups, 1, 4 * pair_count),
        ((0, 0), (out_rows, pad_rows - out_rows - 1), (0, 2 * cols - 4 * pair_count)),
    )
    leaving = (grad.reshape(groups, pad_rows, 2 * cols) + home).astype(BF16)
    arrived = lax.all_to_all(leaving, "dp", split_axis=0, concat_axis=0, tiled=True)
    summed = jnp.sum(arrived.astype(F32), axis=0)
    grad_part = jnp.transpose(summed[:out_rows].reshape(out_rows, 2, cols), (1, 0, 2))
    back = summed[out_rows, : 4 * pair_count].reshape(pair_count, 2, 2)
    pushed_logits = back[:, 0] + back[:, 1]
    slot = jnp.arange(n_slots, dtype=jnp.int32)[None, :]
    own_logits = []
    for j in range(2):
        here = (first[:, None] * CE + j == slot)[:, None, :]
        own_logits.append(jnp.sum(jnp.where(here, logits[None], 0.0), axis=-1))
    return (jnp.stack(own_logits + [pushed_logits]), grad_part)


def solution(mesh):
    return jax.shard_map(
        local,
        mesh=mesh,
        in_specs=(
            P("dp", None, None),
            P("dp", None, None),
            P("dp"),
            P("dp"),
            P(None, "mp"),
            P(None, None, "mp"),
            P("mp", None),
            P(),
            P(),
        ),
        out_specs=(P(None, "dp", None), P(None, "dp", "mp")),
        check_vma=False,
    )
```

```python
import functools

import jax
import jax.numpy as jnp
from jax import lax
from jax.experimental import pallas as pl
from jax.experimental.pallas import tpu as pltpu
from jax.sharding import PartitionSpec as P

HEADS = 12
EPS = 1e-06
CE = 8
NB = 8
NZ, NX, NC = 8, 4, 2
SPLIT = 9
BF16 = jnp.bfloat16
F32 = jnp.float32


def dot(a, b):
    return jnp.dot(a, b, preferred_element_type=F32)


def dot_nt(a, b):
    return lax.dot_general(a, b, (((1,), (1,)), ((), ())), preferred_element_type=F32)


def dot_tn(a, b):
    return lax.dot_general(a, b, (((0,), (0,)), ((), ())), preferred_element_type=F32)


def head_blocks(rows, head):
    lane_head = lax.broadcasted_iota(jnp.int32, rows.shape, 1) // head
    zero = jnp.zeros_like(rows)
    return jnp.concatenate(
        [jnp.where(lane_head == h, rows, zero) for h in range(rows.shape[1] // head)], axis=0
    )


def head_ones(width, head):
    row = lax.broadcasted_iota(jnp.int32, (width, width), 0) // head
    col = lax.broadcasted_iota(jnp.int32, (width, width), 1) // head
    return jnp.where(row == col, 1.0, 0.0).astype(BF16)


def head_sum(values, ones):
    upper = values.astype(BF16)
    lower = (values - upper.astype(F32)).astype(BF16)
    return dot(upper, ones) + dot(lower, ones)


def forward_kernel(
    nch, chunk_img, kind, row, pool, mine, other, k_ref, v_ref, wq_ref, wot_ref, gain_ref,
    itm_ref, q_out, p_out, d_out, log_out, xbuf, sems, *, head, scale,
):
    step = pl.program_id(0)
    shards, _, cols = k_ref.shape
    patches = head
    slots = NB * CE
    blocks = (nch[0] + NB - 1) // NB

    def fetch(blk):
        def one(j, carry):
            slot = blk * slots + j
            for at, source in enumerate((pool, mine, other)):

                @pl.when(kind[slot] == at)
                def _():
                    pltpu.make_async_copy(
                        source.at[row[slot]], xbuf.at[slot], sems.at[blk]
                    ).start()

            return carry

        lax.fori_loop(0, slots, one, 0)

    def settle(blk):
        def one(j, carry):
            slot = blk * slots + j

            @pl.when(kind[slot] >= 0)
            def _():
                pltpu.make_async_copy(pool.at[0], xbuf.at[slot], sems.at[blk]).wait()

            return carry

        lax.fori_loop(0, slots, one, 0)

    @pl.when(step == 0)
    def _():
        xbuf[...] = jnp.zeros_like(xbuf)
        fetch(0)

    @pl.when(step + 1 < blocks)
    def _():
        fetch(step + 1)

    @pl.when(step < blocks)
    def _():
        settle(step)

    @pl.when(step < blocks)
    def _():
        first = pl.multiple_of(step * slots, slots)
        x16 = xbuf[pl.ds(first, slots)].astype(F32)
        rows = x16.shape[1] // 2
        xf = jnp.concatenate([x16[:, :rows], x16[:, rows:]], axis=-1)
        width = xf.shape[-1]
        xf = xf.reshape(slots * rows, width)
        xb = xf.astype(BF16)
        ones = head_ones(cols, head)
        attended = jnp.zeros_like(xf)
        crow = CE * rows
        for s in range(shards):
            q = dot(xb, wq_ref[s]).astype(BF16)
            q_out[s] = q
            scores = []
            for c in range(NB):
                img = chunk_img[step * NB + c]
                at = pl.multiple_of(img * patches, patches)
                kbd = head_blocks(k_ref[s, pl.ds(at, patches), :], head)
                scores.append(dot_nt(q[c * crow : (c + 1) * crow], kbd))
            raised = jnp.exp(jnp.concatenate(scores, axis=0) * scale)
            prob = raised / head_sum(raised, ones)
            p_out[s] = prob
            half = prob.astype(BF16)
            mixed = []
            for c in range(NB):
                img = chunk_img[step * NB + c]
                at = pl.multiple_of(img * patches, patches)
                vbd = head_blocks(v_ref[s, pl.ds(at, patches), :], head)
                mixed.append(dot(half[c * crow : (c + 1) * crow], vbd))
            mixed = jnp.concatenate(mixed, axis=0).astype(BF16)
            attended = attended + dot_nt(mixed, wot_ref[s]).astype(BF16).astype(F32)
        residual = xf + attended
        centred = residual - jnp.mean(residual, axis=-1, keepdims=True)
        variance = jnp.mean(centred * centred, axis=-1, keepdims=True)
        inverse = 1.0 / jnp.sqrt(variance + EPS)
        unit = centred * inverse
        gain = gain_ref[...]
        pooled = jnp.sum((unit * gain).reshape(slots, rows, width), axis=1)
        for j in range(2):
            part = jnp.sum(pooled * itm_ref[j : j + 1], axis=-1, keepdims=True)
            log_out[:, 128 * j : 128 * (j + 1)] = jnp.broadcast_to(part, (slots, 128))
        scaled = (itm_ref[1:2] - itm_ref[0:1]) * gain
        d_first = jnp.mean(scaled, axis=-1, keepdims=True)
        d_second = jnp.mean(scaled * unit, axis=-1, keepdims=True)
        d_out[...] = (inverse * (scaled - d_first - unit * d_second)).astype(BF16)


def backward_kernel(
    nch, chunk_img, delta_ref, d_ref, q_ref, p_ref, v_ref, wot_ref, *rest, head, scale
):
    *arrived, out_ref, acc = rest
    step = pl.program_id(0)
    cols = q_ref.shape[-1]
    patches = head
    blocks = (nch[0] + NB - 1) // NB

    @pl.when(step == 0)
    def _():
        acc[...] = sum((a[...].astype(F32) for a in arrived), jnp.zeros_like(acc))

    @pl.when(step < blocks)
    def _():
        delta = delta_ref[:, :1]
        q = q_ref[0]
        prob = p_ref[0]
        dm = dot(d_ref[...], wot_ref[0]).astype(BF16)
        crow = q.shape[0] // NB
        parts = [slice(c * crow, (c + 1) * crow) for c in range(NB)]
        at = [pl.multiple_of(chunk_img[step * NB + c] * patches, patches) for c in range(NB)]
        d_att = jnp.concatenate(
            [
                dot_nt(dm[parts[c]], head_blocks(v_ref[0, pl.ds(at[c], patches), :], head))
                for c in range(NB)
            ],
            axis=0,
        )
        inner = head_sum(d_att * prob, head_ones(cols, head))
        weighted = prob * delta
        ds = (weighted * (d_att - inner) * scale).astype(BF16)
        pd = weighted.astype(BF16)
        lane_head = lax.broadcasted_iota(jnp.int32, (patches, cols), 1) // head

        def diagonal(block):
            total = jnp.zeros((patches, cols), F32)
            for h in range(cols // head):
                total = jnp.where(lane_head == h, block[h * patches : (h + 1) * patches], total)
            return total

        terms = []
        for c in range(NB):
            dk = diagonal(dot_tn(ds[parts[c]], q[parts[c]]))
            dv = diagonal(dot_tn(pd[parts[c]], dm[parts[c]]))
            terms.append(jnp.concatenate([dk, dv], axis=-1))
        for c in range(NB):
            acc[pl.ds(at[c], patches), :] += terms[c]

    @pl.when(step == pl.num_programs(0) - 1)
    def _():
        out_ref[...] = acc[...].astype(out_ref.dtype)


def plan(neg_caption, all_images, dp, pair_count, n_slots):
    total = all_images.shape[0]
    index = jnp.arange(pair_count, dtype=jnp.int32)
    own = (all_images // pair_count == dp)[:, None] & (
        (all_images % pair_count)[:, None] == index[None, :]
    )
    order = jnp.arange(total, dtype=jnp.int32)
    below = (order[None, :] <= order[:, None]).astype(BF16)
    upto = dot(below, own.astype(BF16)).astype(jnp.int32)
    count = jnp.sum(own.astype(jnp.int32), axis=0)
    chunks = (2 + count + CE - 1) // CE
    first = jnp.sum(jnp.where(index[None, :] < index[:, None], chunks[None, :], 0), axis=1)
    n_chunks = jnp.sum(chunks)
    slot_of = jnp.sum(jnp.where(own, first[None, :] * CE + 1 + upto, 0), axis=1)
    slot = jnp.arange(n_slots, dtype=jnp.int32)
    img = jnp.sum((slot[:, None] // CE >= first[None, :]).astype(jnp.int32), axis=1) - 1
    at_img = img[:, None] == index[None, :]
    pos = slot - CE * jnp.sum(jnp.where(at_img, first[None, :], 0), axis=1)
    hit = slot[:, None] == slot_of[None, :]
    hit = hit & (pos >= 2)[:, None]
    pushed = jnp.sum(jnp.where(hit, order[None, :], 0), axis=1)
    filled = jnp.any(hit, axis=1)
    negative = jnp.sum(jnp.where(at_img, neg_caption[None, :], 0), axis=1)
    cap = jnp.where(pos == 1, negative, jnp.where(filled, pushed, dp * pair_count + img))
    in_use = (slot // CE < n_chunks) & ((pos < 2) | filled)
    block, place = cap // pair_count, cap % pair_count
    far_z = (block // (NX * NC) - dp // (NX * NC)) % NZ
    far_x = (block // NC - dp // NC) % NX
    gathered = place < SPLIT
    row = jnp.where(
        gathered,
        block * SPLIT + place,
        (far_z * NX + far_x) * (pair_count - SPLIT + 1) + place - SPLIT,
    )
    kind = jnp.where(gathered, 0, jnp.where(block % NC == dp % NC, 1, 2))
    kind = jnp.where(in_use, kind, -1)
    sign = jnp.where(in_use, jnp.where(pos == 0, -1.0, 1.0), 0.0).astype(F32)
    chunk_img = img.reshape(-1, CE)[:, 0]
    return n_chunks, chunk_img, kind, row, sign, first, hit


def local(
    images, query_states, neg_caption, neg_image, cross_query, cross_kv, cross_out, norm_gain,
    itm_weight,
):
    pair_count, patches, vis = images.shape
    queries, width = query_states.shape[1:]
    cols = cross_query.shape[1]
    head = width // HEADS
    scale = 1.0 / head**0.5
    groups = lax.axis_size("dp")
    shards = lax.axis_size("mp")
    dp, mp = lax.axis_index("dp"), lax.axis_index("mp")
    core = dp % 2
    rows = queries // shards
    half = width // 2
    pairs = groups * pair_count

    def around(x, by):
        return lax.ppermute(x, "mp", [(i, (i + by) % shards) for i in range(shards)])

    def shift(x, by_z, by_x, by_core):
        pairs_ = []
        for i in range(groups):
            z, x_, c = i // (NX * NC), i // NC % NX, i % NC
            to = ((z + by_z) % NZ * NX + (x_ + by_x) % NX) * NC + (c + by_core) % NC
            pairs_.append((i, to))
        return lax.ppermute(x, "dp", pairs_)

    own_rows = lax.dynamic_slice_in_dim(query_states, mp * rows, rows, 1)
    packed = jnp.concatenate([own_rows[:, :, :half], own_rows[:, :, half:]], axis=1)
    pool = lax.all_gather(packed[:SPLIT], "dp", axis=0, tiled=True)
    number = jnp.stack([neg_image // 32, neg_image % 32], axis=-1).astype(BF16)
    number = jnp.pad(number, ((0, 2 * rows - pair_count), (0, half - 2)))
    part = jnp.concatenate([packed[SPLIT:], number[None]], axis=0)[None]
    by_x = [part] + [shift(part, 0, -d, 0) for d in range(1, NX)]
    line = jnp.concatenate(by_x, axis=0)
    up, down = [line], [line]
    for _ in range(NZ // 2 - 1):
        up.append(shift(up[-1], -1, 0, 0))
        down.append(shift(down[-1], 1, 0, 0))
    across = [shift(up[-1][: NX // 2], -1, 0, 0), shift(down[-1][NX // 2 :], 1, 0, 0)]
    mine = jnp.concatenate(up + across + down[:0:-1], axis=0)
    other = shift(mine, 0, 0, 1)
    near = mine[:, -1, :pair_count, :2].astype(jnp.int32)
    beside = other[:, -1, :pair_count, :2].astype(jnp.int32)
    both = jnp.where(
        core == 0, jnp.stack([near, beside], axis=1), jnp.stack([beside, near], axis=1)
    )
    both = (both[..., 0] * 32 + both[..., 1]).reshape(NZ, NX, NC * pair_count)
    both = jnp.roll(both, (dp // (NX * NC), dp // NC % NX), axis=(0, 1))
    all_images = both.reshape(-1)
    mine = mine.reshape(-1, 2 * rows, half)
    other = other.reshape(-1, 2 * rows, half)

    weights = jnp.concatenate(
        [
            jnp.concatenate([cross_kv[0], cross_kv[1]], axis=1),
            jnp.concatenate([cross_query, cross_out.T], axis=1),
        ],
        axis=0,
    )
    tall = weights.shape[0] // 2
    brought = lax.dynamic_slice_in_dim(weights, core * tall, tall, 0)
    shard_list = [weights]
    for s in range(1, shards):
        got = around(brought, shards - s)
        swap = shift(got, 0, 0, 1)
        shard_list.append(
            jnp.concatenate(
                [jnp.where(core == 0, got, swap), jnp.where(core == 0, swap, got)], axis=0
            )
        )
    flat = images.reshape(pair_count * patches, vis)
    kv = [dot(flat, w[:vis]).astype(BF16) for w in shard_list]
    keys = jnp.stack([x[:, :cols] for x in kv])
    values = jnp.stack([x[:, cols:] for x in kv])
    wq = jnp.stack([w[vis:, :cols] for w in shard_list])
    wot = jnp.stack([w[vis:, cols:] for w in shard_list])

    out_rows = vis // groups
    pad_rows = (out_rows + 1 + 7) // 8 * 8
    feature = lax.broadcasted_iota(jnp.int32, (vis, groups * pad_rows), 0)
    place = lax.broadcasted_iota(jnp.int32, (vis, groups * pad_rows), 1)
    target = jnp.where(
        place % pad_rows < out_rows, place // pad_rows * out_rows + place % pad_rows, -1
    )
    chosen = (feature == target).astype(BF16)
    spread = lax.dot_general(
        chosen, flat, (((0,), (1,)), ((), ())), preferred_element_type=F32
    ).astype(BF16)

    steps = -(-(pair_count * (2 + CE - 1) + 2 * groups) // (CE * NB))
    n_slots = steps * NB * CE
    n_chunks, chunk_img, kind, row, sign, first, hit = plan(
        neg_caption, all_images, dp, pair_count, n_slots
    )
    nch = n_chunks.reshape(1)
    n_rows = n_slots * rows
    blk = NB * CE * rows

    def last(i, nch):
        return jnp.minimum(i, (nch[0] + NB - 1) // NB - 1)

    def whole(a):
        return pl.BlockSpec(a.shape, lambda *_: (0,) * a.ndim)

    row3 = pl.BlockSpec((shards, blk, cols), lambda i, n, *_: (0, last(i, n), 0))
    row2 = pl.BlockSpec((blk, width), lambda i, n, *_: (last(i, n), 0))
    params = pltpu.CompilerParams(vmem_limit_bytes=56 * 2**20)
    gain = norm_gain.reshape(1, width)
    itm = itm_weight.T / queries
    q_rows, prob, d_res, log_part = pl.pallas_call(
        functools.partial(forward_kernel, head=head, scale=scale),
        grid_spec=pltpu.PrefetchScalarGridSpec(
            num_scalar_prefetch=4,
            grid=(steps,),
            in_specs=[
                pl.BlockSpec(memory_space=pl.ANY),
                pl.BlockSpec(memory_space=pl.ANY),
                pl.BlockSpec(memory_space=pl.ANY),
                whole(keys), whole(values), whole(wq), whole(wot), whole(gain), whole(itm),
            ],
            out_specs=[
                row3, row3, row2,
                pl.BlockSpec((NB * CE, 256), lambda i, n, *_: (last(i, n), 0)),
            ],
            scratch_shapes=[
                pltpu.VMEM((n_slots, 2 * rows, half), BF16),
                pltpu.SemaphoreType.DMA((steps,)),
            ],
        ),
        out_shape=[
            jax.ShapeDtypeStruct((shards, n_rows, cols), BF16),
            jax.ShapeDtypeStruct((shards, n_rows, cols), F32),
            jax.ShapeDtypeStruct((n_rows, width), BF16),
            jax.ShapeDtypeStruct((n_slots, 256), F32),
        ],
        compiler_params=params,
        name="forward",
    )(nch, chunk_img, kind, row, pool, mine, other, keys, values, wq, wot, gain, itm)

    part = jnp.stack([log_part[:, 0], log_part[:, 128]])
    part = jnp.where((sign != 0.0)[None, :], part, 0.0)
    terms = [part] + [around(part, shards - s) for s in range(1, shards)]
    logits = jnp.zeros_like(part)
    for m in range(shards):
        for s in range(shards):
            logits = logits + jnp.where((mp + s) % shards == m, terms[s], 0.0)

    gap = logits[1] - logits[0]
    delta = sign / (1.0 + jnp.exp(-sign * gap))
    delta = jnp.broadcast_to(jnp.repeat(delta, rows)[:, None], (n_rows, 128))

    def backward(s, arrived=(), kind=BF16):
        def rows_of(shape):
            return pl.BlockSpec((1,) + shape, lambda *_: (s, 0, 0))

        pick = pl.BlockSpec((1, blk, cols), lambda i, n, *_: (s, last(i, n), 0))
        return pl.pallas_call(
            functools.partial(backward_kernel, head=head, scale=scale),
            grid_spec=pltpu.PrefetchScalarGridSpec(
                num_scalar_prefetch=2,
                grid=(steps,),
                in_specs=[
                    pl.BlockSpec((blk, 128), lambda i, n, *_: (last(i, n), 0)),
                    row2, pick, pick, rows_of(values.shape[1:]), rows_of(wot.shape[1:]),
                ]
                + [whole(a) for a in arrived],
                out_specs=pl.BlockSpec(
                    (pair_count * patches, 2 * cols), lambda *_: (0, 0)
                ),
                scratch_shapes=[pltpu.VMEM((pair_count * patches, 2 * cols), F32)],
            ),
            out_shape=jax.ShapeDtypeStruct((pair_count * patches, 2 * cols), kind),
            compiler_params=params,
            cost_estimate=pl.CostEstimate(
                flops=10**6, bytes_accessed=10**4, transcendentals=0
            ),
            name="backward",
        )(nch, chunk_img, delta, d_res, q_rows, prob, values, wot, *arrived)

    terms = [around(backward(s), s) for s in range(1, shards)]
    d_kv = backward(0, terms[:2], F32)
    d_kv = (d_kv + sum(term.astype(F32) for term in terms[2:])).astype(BF16)
    grad = dot(spread, lax.optimization_barrier(d_kv))

    logit_hi = logits.astype(BF16)
    logit_lo = (logits - logit_hi.astype(F32)).astype(BF16)
    four = jnp.concatenate([logit_hi, logit_lo], axis=0)
    home = lax.dot_general(
        hit.astype(BF16), four, (((0,), (1,)), ((), ())), preferred_element_type=F32
    )
    home = jnp.pad(
        home.reshape(groups, 1, 4 * pair_count),
        ((0, 0), (out_rows, pad_rows - out_rows - 1), (0, 2 * cols - 4 * pair_count)),
    )
    leaving = (grad.reshape(groups, pad_rows, 2 * cols) + home).astype(BF16)
    arrived = lax.all_to_all(leaving, "dp", split_axis=0, concat_axis=0, tiled=True)
    summed = jnp.sum(arrived.astype(F32), axis=0)
    grad_part = jnp.transpose(summed[:out_rows].reshape(out_rows, 2, cols), (1, 0, 2))
    back = summed[out_rows, : 4 * pair_count].reshape(pair_count, 2, 2)
    pushed_logits = back[:, 0] + back[:, 1]
    slot = jnp.arange(n_slots, dtype=jnp.int32)[None, :]
    own_logits = []
    for j in range(2):
        here = (first[:, None] * CE + j == slot)[:, None, :]
        own_logits.append(jnp.sum(jnp.where(here, logits[None], 0.0), axis=-1))
    return (jnp.stack(own_logits + [pushed_logits]), grad_part)


def solution(mesh):
    return jax.shard_map(
        local,
        mesh=mesh,
        in_specs=(
            P("dp", None, None),
            P("dp", None, None),
            P("dp"),
            P("dp"),
            P(None, "mp"),
            P(None, None, "mp"),
            P("mp", None),
            P(),
            P(),
        ),
        out_specs=(P(None, "dp", None), P(None, "dp", "mp")),
        check_vma=False,
    )
```

```python
import functools

import jax
import jax.numpy as jnp
from jax import lax
from jax.experimental import pallas as pl
from jax.experimental.pallas import tpu as pltpu
from jax.sharding import PartitionSpec as P

HEADS = 12
EPS = 1e-06
CE = 4
NB = 8
LANES = 256
NZ, NX, NC = 8, 4, 2
BF16 = jnp.bfloat16
F32 = jnp.float32
I32 = jnp.int32


def dot(a, b):
    return jnp.dot(a, b, preferred_element_type=F32)


def dot_nt(a, b):
    return lax.dot_general(a, b, (((1,), (1,)), ((), ())), preferred_element_type=F32)


def dot_tn(a, b):
    return lax.dot_general(a, b, (((0,), (0,)), ((), ())), preferred_element_type=F32)


def iota(shape, axis):
    return lax.broadcasted_iota(I32, shape, axis)


def head_blocks(rows, heads, head):
    lane_head = iota(rows.shape, 1) // head
    zero = jnp.zeros_like(rows)
    return jnp.concatenate([jnp.where(lane_head == h, rows, zero) for h in range(heads)], axis=0)


def head_sum(values, head):
    width = values.shape[-1]
    same = iota((width, width), 0) // head == iota((width, width), 1) // head
    ones = jnp.where(same, 1.0, 0.0).astype(BF16)
    upper = values.astype(BF16)
    lower = (values - upper.astype(F32)).astype(BF16)
    return dot(upper, ones) + dot(lower, ones)


def plan_kernel(dp_ref, ids_ref, neg_ref, ints_out, sign_out, hit_out):
    total = ids_ref.shape[0]
    images = neg_ref.shape[0]
    slots = sign_out.shape[1]
    base = dp_ref[0] * images
    own = (ids_ref[...] - base) == iota((total, images), 1)
    ones = jnp.where(own, 1.0, 0.0)
    below = jnp.where(iota((128, 128), 0) >= iota((128, 128), 1), 1.0, 0.0).astype(BF16)
    count_row = jnp.zeros((1, images), F32)
    upto = []
    for j in range(total // 128):
        piece = ones[128 * j : 128 * (j + 1)]
        upto.append(dot(below, piece.astype(BF16)) + count_row)
        count_row = count_row + jnp.sum(piece, axis=0, keepdims=True)
    upto = jnp.concatenate(upto, axis=0)
    diagonal = iota((images, images), 0) == iota((images, images), 1)
    count_col = jnp.sum(jnp.where(diagonal, count_row, 0.0), axis=1, keepdims=True)

    def chunks_of(count):
        return lax.div(count.astype(I32) + (2 + CE - 1), jnp.full(count.shape, CE, I32))

    chunks_row, chunks_col = chunks_of(count_row), chunks_of(count_col)
    before = iota((images, images), 0) < iota((images, images), 1)
    after = iota((images, images), 0) > iota((images, images), 1)
    first_row = jnp.sum(jnp.where(before, chunks_col, 0), axis=0, keepdims=True)
    first_col = jnp.sum(jnp.where(after, chunks_row, 0), axis=1, keepdims=True)
    n_chunks = jnp.sum(chunks_row, axis=1, keepdims=True)
    slot_of = jnp.sum(
        jnp.where(own, (first_row * CE + 1).astype(F32) + upto, 0.0), axis=1, keepdims=True
    ).astype(I32)
    slot = iota((1, slots), 1)
    chunk = lax.div(slot, jnp.full(slot.shape, CE, I32))
    img = jnp.sum(jnp.where(chunk >= first_col, 1, 0), axis=0, keepdims=True) - 1
    at_img = img == iota((images, slots), 0)
    pos = slot - CE * jnp.sum(jnp.where(at_img, first_col, 0), axis=0, keepdims=True)
    negative = jnp.sum(jnp.where(at_img, neg_ref[...], 0), axis=0, keepdims=True)
    hit = (slot_of == slot) & (pos >= 2)
    number = jnp.where(hit, iota((total, slots), 0) + 1, 0)
    pushed = jnp.sum(number, axis=0, keepdims=True)
    used = (chunk < n_chunks) & ((pos < 2) | (pushed > 0))
    cap = jnp.where(pos == 0, base + img, jnp.where(pos == 1, negative, pushed - 1))
    cap = jnp.where(used, cap, -1)
    row = iota((8, slots), 0)
    ints = jnp.where(row == 0, cap, jnp.where(row == 1, img, jnp.where(row == 2, pos, n_chunks)))
    ints_out[...] = ints
    sign_out[...] = jnp.where(used, jnp.where(pos == 0, -1.0, 1.0), 0.0)
    hit_out[...] = jnp.where(hit, 1.0, 0.0).astype(BF16)


def blocks_of(ints):
    return lax.div(ints[3, 0] + (NB - 1), NB)


def patch_rows(ints, step, patches):
    return [
        pl.multiple_of(ints[1, (step * NB + c) * CE] * patches, patches) for c in range(NB)
    ]


def forward_kernel(
    ints, pool, k_ref, v_ref, wq_ref, wo_ref, const_ref, q_out, p_out, d_out, log_out, xbuf, sems,
    *, head, scale,
):
    step = pl.program_id(0)
    width = wo_ref.shape[1]
    shards = wq_ref.shape[0] // LANES
    heads = HEADS // shards
    slots = NB * CE
    blocks = blocks_of(ints)

    def each(blk, act):
        def one(j, carry):
            slot = blk * slots + j

            @pl.when(ints[0, slot] >= 0)
            def _():
                act(pltpu.make_async_copy(pool.at[ints[0, slot]], xbuf.at[slot], sems.at[blk]))

            return carry

        lax.fori_loop(0, slots, one, 0)

    @pl.when(step == 0)
    def _():
        xbuf[...] = jnp.zeros_like(xbuf)
        each(0, lambda copy: copy.start())

    @pl.when(step + 1 < blocks)
    def _():
        each(step + 1, lambda copy: copy.start())

    @pl.when(step < blocks)
    def _():
        each(step, lambda copy: copy.wait())
        x16 = xbuf[pl.ds(pl.multiple_of(step * slots, slots), slots)].astype(F32)
        rows = x16.shape[1] // 2
        xf = jnp.concatenate([x16[:, :rows], x16[:, rows:]], axis=-1)
        xf = xf.reshape(slots * rows, width)
        q = (dot_nt(xf.astype(BF16), wq_ref[...]) * scale).astype(BF16)
        q_out[...] = q
        crow = CE * rows
        parts = [slice(c * crow, (c + 1) * crow) for c in range(NB)]
        at = patch_rows(ints, step, head)
        mixed = []
        for s in range(shards):
            lanes = slice(s * LANES, (s + 1) * LANES)
            scores = jnp.concatenate(
                [
                    dot_nt(
                        q[parts[c], lanes],
                        head_blocks(k_ref[pl.ds(at[c], head), lanes], heads, head),
                    )
                    for c in range(NB)
                ],
                axis=0,
            )
            raised = jnp.exp(scores)
            prob = raised / head_sum(raised, head)
            p_out[:, s * LANES : s * LANES + heads * head] = prob
            half = prob.astype(BF16)
            mixed.append(
                jnp.concatenate(
                    [
                        dot(
                            half[parts[c]],
                            head_blocks(v_ref[pl.ds(at[c], head), lanes], heads, head),
                        )
                        for c in range(NB)
                    ],
                    axis=0,
                ).astype(BF16)
            )
        residual = xf + dot(jnp.concatenate(mixed, axis=-1), wo_ref[...])
        centred = residual - jnp.mean(residual, axis=-1, keepdims=True)
        variance = jnp.mean(centred * centred, axis=-1, keepdims=True)
        inverse = 1.0 / jnp.sqrt(variance + EPS)
        unit = centred * inverse
        scaled = const_ref[1:2]
        none = jnp.sum(unit * const_ref[0:1], axis=-1, keepdims=True)
        gap = jnp.sum(unit * scaled, axis=-1, keepdims=True)
        both = jnp.where(iota((slots * rows, 128), 1) == 0, none, none + gap)
        log_out[...] = jnp.sum(both.reshape(slots, rows, 128), axis=1)
        flat = scaled - jnp.mean(scaled, axis=-1, keepdims=True)
        d_out[...] = (inverse * (flat - unit * (gap / width))).astype(BF16)


def backward_kernel(ints, delta_ref, d_ref, q_ref, p_ref, v_ref, wo_ref, *rest, head, heads):
    *arrived, out_ref, acc = rest
    step = pl.program_id(0)
    cols = heads * head
    blocks = blocks_of(ints)

    @pl.when(step == 0)
    def _():
        acc[...] = sum((a[...].astype(F32) for a in arrived), jnp.zeros_like(acc))

    @pl.when(step < blocks)
    def _():
        q = q_ref[...]
        prob = p_ref[:, :cols]
        dm = dot_nt(d_ref[...], wo_ref[...]).astype(BF16)
        crow = q.shape[0] // NB
        parts = [slice(c * crow, (c + 1) * crow) for c in range(NB)]
        at = patch_rows(ints, step, head)
        d_att = jnp.concatenate(
            [
                dot_nt(dm[parts[c]], head_blocks(v_ref[pl.ds(at[c], head), :], heads, head))
                for c in range(NB)
            ],
            axis=0,
        )
        inner = head_sum(d_att * prob, head)
        weighted = prob * delta_ref[:, :1]
        ds = (weighted * (d_att - inner)).astype(BF16)
        pd = weighted.astype(BF16)
        lane_head = iota((head, LANES), 1) // head

        def diagonal(block):
            total = block[:head]
            for h in range(1, heads):
                total = jnp.where(lane_head == h, block[h * head : (h + 1) * head], total)
            return total[:, :cols]

        terms = []
        for c in range(NB):
            dk = diagonal(dot_tn(ds[parts[c]], q[parts[c]]))
            dv = diagonal(dot_tn(pd[parts[c]], dm[parts[c]]))
            terms.append(jnp.concatenate([dk, dv], axis=-1))
        for c in range(NB):
            acc[pl.ds(at[c], head), :] += terms[c]

    @pl.when(step == pl.num_programs(0) - 1)
    def _():
        out_ref[...] = acc[...].astype(out_ref.dtype)


def whole(a):
    return pl.BlockSpec(a.shape, lambda *_: (0,) * a.ndim)


def local(
    images, query_states, neg_caption, neg_image, cross_query, cross_kv, cross_out, norm_gain,
    itm_weight,
):
    pair_count, patches, vis = images.shape
    queries, width = query_states.shape[1:]
    cols = cross_query.shape[1]
    head = width // HEADS
    scale = 1.0 / head**0.5
    groups = lax.axis_size("dp")
    shards = lax.axis_size("mp")
    dp, mp = lax.axis_index("dp"), lax.axis_index("mp")
    core = dp % NC
    rows = queries // shards
    half = width // 2

    def around(x, by):
        return lax.ppermute(x, "mp", [(i, (i + by) % shards) for i in range(shards)])

    def shift(x, by_z, by_x, by_core):
        moves = []
        for i in range(groups):
            z, x_, c = i // (NX * NC), i // NC % NX, i % NC
            to = ((z + by_z) % NZ * NX + (x_ + by_x) % NX) * NC + (c + by_core) % NC
            moves.append((i, to))
        return lax.ppermute(x, "dp", moves)

    own_rows = lax.dynamic_slice_in_dim(query_states, mp * rows, rows, 1)
    packed = jnp.concatenate([own_rows[:, :, :half], own_rows[:, :, half:]], axis=1)
    pool = lax.all_gather(packed, "dp", axis=0, tiled=True)
    ids = jnp.zeros((8, 128), I32).at[0, :pair_count].set(neg_image)
    all_images = lax.all_gather(ids, "dp", axis=0, tiled=True)
    all_images = all_images.reshape(groups, 8, 128)[:, 0, :pair_count].reshape(-1, 1)

    halves = [
        jnp.concatenate([cross_kv[0].T, cross_query.T], axis=1),
        jnp.concatenate([cross_kv[1].T, cross_out], axis=1),
    ]
    brought = jnp.where(core == 0, halves[0], halves[1])
    got = [around(brought, shards - s) for s in range(1, shards)]
    swap = [shift(g, 0, 0, 1) for g in got]
    padded = []
    for c in range(NC):
        pieces = [halves[c]] + [jnp.where(core == c, g, w) for g, w in zip(got, swap)]
        stacked = jnp.stack([jnp.pad(p, ((0, LANES - cols), (0, 0))) for p in pieces])
        padded.append(stacked.reshape(shards * LANES, vis + width))
    flat = images.reshape(pair_count * patches, vis)
    keys = dot_nt(flat, padded[0][:, :vis]).astype(BF16)
    values = dot_nt(flat, padded[1][:, :vis]).astype(BF16)
    wq, wo = padded[0][:, vis:], padded[1][:, vis:]

    out_rows = vis // groups
    pad_rows = (out_rows + 1 + 7) // 8 * 8
    feature = iota((vis, groups * pad_rows), 0)
    place = iota((vis, groups * pad_rows), 1)
    target = jnp.where(
        place % pad_rows < out_rows, place // pad_rows * out_rows + place % pad_rows, -1
    )
    chosen = (feature == target).astype(BF16)
    spread = lax.dot_general(
        chosen, flat, (((0,), (1,)), ((), ())), preferred_element_type=F32
    ).astype(BF16)
    spread, keys = lax.optimization_barrier((spread, keys))

    steps = -(-(pair_count * (2 + CE - 1) + 2 * groups) // (CE * NB))
    n_slots = steps * NB * CE
    n_rows = n_slots * rows
    blk = NB * CE * rows
    params = pltpu.CompilerParams(vmem_limit_bytes=56 * 2**20)
    ints, sign, hit = pl.pallas_call(
        plan_kernel,
        in_specs=[
            pl.BlockSpec(memory_space=pltpu.SMEM),
            pl.BlockSpec(memory_space=pltpu.VMEM),
            pl.BlockSpec(memory_space=pltpu.VMEM),
        ],
        out_specs=[pl.BlockSpec(memory_space=pltpu.VMEM)] * 3,
        out_shape=[
            jax.ShapeDtypeStruct((8, n_slots), I32),
            jax.ShapeDtypeStruct((1, n_slots), F32),
            jax.ShapeDtypeStruct((groups * pair_count, n_slots), BF16),
        ],
        compiler_params=params,
        name="plan",
    )(dp.astype(I32).reshape(1), all_images, neg_caption.reshape(-1, 1))
    sign = sign[0]

    def last(i, n):
        return jnp.minimum(i, blocks_of(n) - 1)

    def rows_of(lanes, s=0):
        return pl.BlockSpec((blk, lanes), lambda i, n: (last(i, n), s))

    fold = norm_gain / queries
    const = jnp.stack([fold * itm_weight[:, 0], fold * (itm_weight[:, 1] - itm_weight[:, 0])])
    q_rows, prob, d_res, log_part = pl.pallas_call(
        functools.partial(forward_kernel, head=head, scale=scale),
        grid_spec=pltpu.PrefetchScalarGridSpec(
            num_scalar_prefetch=1,
            grid=(steps,),
            in_specs=[pl.BlockSpec(memory_space=pl.ANY)]
            + [whole(a) for a in (keys, values, wq, wo, const)],
            out_specs=[
                rows_of(shards * LANES), rows_of(shards * LANES), rows_of(width),
                pl.BlockSpec((NB * CE, 128), lambda i, n: (last(i, n), 0)),
            ],
            scratch_shapes=[
                pltpu.VMEM((n_slots, 2 * rows, half), BF16),
                pltpu.SemaphoreType.DMA((steps,)),
            ],
        ),
        out_shape=[
            jax.ShapeDtypeStruct((n_rows, shards * LANES), BF16),
            jax.ShapeDtypeStruct((n_rows, shards * LANES), F32),
            jax.ShapeDtypeStruct((n_rows, width), BF16),
            jax.ShapeDtypeStruct((n_slots, 128), F32),
        ],
        compiler_params=params,
        name="forward",
    )(ints, pool, keys, values, wq, wo, const)

    part = jnp.where((sign != 0.0)[None, :], log_part[:, :2].T, 0.0)
    terms = [part] + [around(part, shards - s) for s in range(1, shards)]
    logits = jnp.zeros_like(part)
    for m in range(shards):
        for s in range(shards):
            logits = logits + jnp.where((mp + s) % shards == m, terms[s], 0.0)
    delta = sign / (1.0 + jnp.exp(sign * (logits[0] - logits[1])))
    delta = jnp.broadcast_to(delta[:, None, None], (n_slots, rows, 128)).reshape(n_rows, 128)

    def backward(s, arrived=(), kind=BF16):
        shape = (pair_count * patches, 2 * cols)
        return pl.pallas_call(
            functools.partial(backward_kernel, head=head, heads=HEADS // shards),
            grid_spec=pltpu.PrefetchScalarGridSpec(
                num_scalar_prefetch=1,
                grid=(steps,),
                in_specs=[
                    rows_of(128), rows_of(width), rows_of(LANES, s), rows_of(LANES, s),
                    pl.BlockSpec((pair_count * patches, LANES), lambda *_: (0, s)),
                    pl.BlockSpec((LANES, width), lambda *_: (s, 0)),
                ]
                + [whole(a) for a in arrived],
                out_specs=pl.BlockSpec(shape, lambda *_: (0, 0)),
                scratch_shapes=[pltpu.VMEM(shape, F32)],
            ),
            out_shape=jax.ShapeDtypeStruct(shape, kind),
            compiler_params=params,
            cost_estimate=pl.CostEstimate(flops=10**6, bytes_accessed=10**4, transcendentals=0),
            name="backward",
        )(ints, delta, d_res, q_rows, prob, values, wo, *arrived)

    terms = [around(backward(s), s) for s in range(1, shards)]
    d_kv = backward(0, terms[:2], F32)
    d_kv = (d_kv + sum(term.astype(F32) for term in terms[2:])).astype(BF16)

    logit_hi = logits.astype(BF16)
    logit_lo = (logits - logit_hi.astype(F32)).astype(BF16)
    four = jnp.concatenate([logit_hi, logit_lo], axis=0)
    home = dot_nt(hit, four).astype(BF16)
    home = jnp.pad(
        home.reshape(groups, 1, 4 * pair_count),
        ((0, 0), (out_rows, pad_rows - out_rows - 1), (0, 2 * cols - 4 * pair_count)),
    )
    home, d_kv = lax.optimization_barrier((home, d_kv))
    grad = dot(spread, d_kv).astype(BF16)
    leaving = grad.reshape(groups, pad_rows, 2 * cols) + home
    arrived = lax.all_to_all(leaving, "dp", split_axis=0, concat_axis=0, tiled=True)
    summed = jnp.sum(arrived.astype(F32), axis=0)
    grad_part = jnp.transpose(summed[:out_rows].reshape(out_rows, 2, cols), (1, 0, 2))
    back = summed[out_rows, : 4 * pair_count].reshape(pair_count, 2, 2)
    pushed_logits = back[:, 0] + back[:, 1]
    image = jnp.arange(pair_count, dtype=I32)[:, None]
    own_logits = []
    for j in range(2):
        here = ((ints[1:2] == image) & (ints[2:3] == j))[:, None, :]
        own_logits.append(jnp.sum(jnp.where(here, logits[None], 0.0), axis=-1))
    return (jnp.stack(own_logits + [pushed_logits]), grad_part)


def solution(mesh):
    return jax.shard_map(
        local,
        mesh=mesh,
        in_specs=(
            P("dp", None, None),
            P("dp", None, None),
            P("dp"),
            P("dp"),
            P(None, "mp"),
            P(None, None, "mp"),
            P("mp", None),
            P(),
            P(),
        ),
        out_specs=(P(None, "dp", None), P(None, "dp", "mp")),
        check_vma=False,
    )
```

```python
import functools

import jax
import jax.numpy as jnp
from jax import lax
from jax.experimental import pallas as pl
from jax.experimental.pallas import tpu as pltpu
from jax.sharding import PartitionSpec as P

HEADS = 12
EPS = 1e-06
CE = 2
SB = 32
WIN = 16
LANES = 256
NZ, NX, NC = 8, 4, 2
BF16 = jnp.bfloat16
F32 = jnp.float32
I32 = jnp.int32


def dot(a, b):
    return jnp.dot(a, b, preferred_element_type=F32)


def dot_nt(a, b):
    return lax.dot_general(a, b, (((1,), (1,)), ((), ())), preferred_element_type=F32)


def dot_tn(a, b):
    return lax.dot_general(a, b, (((0,), (0,)), ((), ())), preferred_element_type=F32)


def iota(shape, axis):
    return lax.broadcasted_iota(I32, shape, axis)


def head_blocks(rows, heads, head):
    lane_head = iota(rows.shape, 1) // head
    zero = jnp.zeros_like(rows)
    return jnp.concatenate([jnp.where(lane_head == h, rows, zero) for h in range(heads)], axis=0)


def head_sum(values, head):
    width = values.shape[-1]
    same = iota((width, width), 0) // head == iota((width, width), 1) // head
    ones = jnp.where(same, 1.0, 0.0).astype(BF16)
    upper = values.astype(BF16)
    lower = (values - upper.astype(F32)).astype(BF16)
    return dot(upper, ones) + dot(lower, ones)


def plan_kernel(dp_ref, ids_ref, neg_ref, ints_out, sign_out, hit_out):
    total = ids_ref.shape[0]
    images = neg_ref.shape[0]
    slots = sign_out.shape[1]
    base = dp_ref[0] * images
    own = (ids_ref[...] - base) == iota((total, images), 1)
    ones = jnp.where(own, 1.0, 0.0)
    below = jnp.where(iota((128, 128), 0) >= iota((128, 128), 1), 1.0, 0.0).astype(BF16)
    count_row = jnp.zeros((1, images), F32)
    upto = []
    for j in range(total // 128):
        piece = ones[128 * j : 128 * (j + 1)]
        upto.append(dot(below, piece.astype(BF16)) + count_row)
        count_row = count_row + jnp.sum(piece, axis=0, keepdims=True)
    upto = jnp.concatenate(upto, axis=0)
    diagonal = iota((images, images), 0) == iota((images, images), 1)
    count_col = jnp.sum(jnp.where(diagonal, count_row, 0.0), axis=1, keepdims=True)

    def chunks_of(count):
        return lax.div(count.astype(I32) + (2 + CE - 1), jnp.full(count.shape, CE, I32))

    chunks_row, chunks_col = chunks_of(count_row), chunks_of(count_col)
    before = iota((images, images), 0) < iota((images, images), 1)
    after = iota((images, images), 0) > iota((images, images), 1)
    first_row = jnp.sum(jnp.where(before, chunks_col, 0), axis=0, keepdims=True)
    first_col = jnp.sum(jnp.where(after, chunks_row, 0), axis=1, keepdims=True)
    n_chunks = jnp.sum(chunks_row, axis=1, keepdims=True)
    slot_of = jnp.sum(
        jnp.where(own, (first_row * CE + 1).astype(F32) + upto, 0.0), axis=1, keepdims=True
    ).astype(I32)
    slot = iota((1, slots), 1)
    chunk = lax.div(slot, jnp.full(slot.shape, CE, I32))
    img = jnp.sum(jnp.where(chunk >= first_col, 1, 0), axis=0, keepdims=True) - 1
    at_img = img == iota((images, slots), 0)
    pos = slot - CE * jnp.sum(jnp.where(at_img, first_col, 0), axis=0, keepdims=True)
    negative = jnp.sum(jnp.where(at_img, neg_ref[...], 0), axis=0, keepdims=True)
    hit = (slot_of == slot) & (pos >= 2)
    number = jnp.where(hit, iota((total, slots), 0) + 1, 0)
    pushed = jnp.sum(number, axis=0, keepdims=True)
    used = (chunk < n_chunks) & ((pos < 2) | (pushed > 0))
    cap = jnp.where(pos == 0, base + img, jnp.where(pos == 1, negative, pushed - 1))
    cap = jnp.where(used, cap, -1)
    row = iota((8, slots), 0)
    lane = iota((images, slots), 0) == iota((images, slots), 1)
    start = jnp.sum(jnp.where(lane, first_col * CE, 0), axis=0, keepdims=True)
    count = jnp.sum(jnp.where(lane, count_col.astype(I32) + 2, 0), axis=0, keepdims=True)
    ints = n_chunks
    for at, values in enumerate((cap, img, pos, n_chunks, start, count)):
        ints = jnp.where(row == at, values, ints)
    ints_out[...] = ints
    sign_out[...] = jnp.where(used, jnp.where(pos == 0, -1.0, 1.0), 0.0)
    hit_out[...] = jnp.where(hit, 1.0, 0.0).astype(BF16)


def blocks_of(ints):
    return lax.div(ints[3, 0] * CE + (SB - 1), SB)


def windows(ints, images, rows, act, extra_first):
    def extra():
        def one(img, carry):
            count = ints[5, img]

            def more(w, carry):
                at = pl.multiple_of((ints[4, img] + w * WIN) * rows, CE * rows)
                act(img, at, (count - w * WIN) * rows, False)
                return carry

            return lax.fori_loop(1, lax.div(count + (WIN - 1), WIN), more, carry)

        lax.fori_loop(0, images, one, 0)

    if extra_first:
        extra()
    for img in range(images):
        at = pl.multiple_of(ints[4, img] * rows, CE * rows)
        act(img, at, ints[5, img] * rows, True)
    if not extra_first:
        extra()


def block_rows(blk, size):
    return pl.ds(pl.multiple_of(blk * size, size), size)


def forward_kernel(
    ints, pool, wq_in, k_in, v_in, wo_in, const_ref, q_out, p_out, d_out, log_out,
    xbuf, wq, k, v, wo, q, p, half, mixed, d_res, sem_x, sem_w, sem_o, *, head, scale,
):
    width = wo.shape[1]
    shards = wq.shape[0] // LANES
    heads = HEADS // shards
    cols = heads * head
    images = k.shape[0] // head
    rows = xbuf.shape[1] // 2
    size = SB * rows
    win = WIN * rows
    blocks = blocks_of(ints)
    weights = [
        pltpu.make_async_copy(src, dst, sem_w.at[j])
        for j, (src, dst) in enumerate(((wq_in, wq), (k_in, k), (v_in, v), (wo_in, wo)))
    ]
    for copy in weights:
        copy.start()

    def each(blk, act):
        def one(j, carry):
            slot = blk * SB + j

            @pl.when(ints[0, slot] >= 0)
            def _():
                act(pltpu.make_async_copy(pool.at[ints[0, slot]], xbuf.at[slot], sem_x.at[blk]))

            return carry

        lax.fori_loop(0, SB, one, 0)

    def results(blk, s):
        at = block_rows(blk, size)
        return [
            pltpu.make_async_copy(q.at[s, at], q_out.at[s, at], sem_o.at[0]),
            pltpu.make_async_copy(p.at[s, at], p_out.at[s, at], sem_o.at[1]),
        ]

    def gradient(blk):
        at = block_rows(blk, size)
        return pltpu.make_async_copy(d_res.at[at], d_out.at[at], sem_o.at[2])

    def loop(body):
        def one(blk, carry):
            body(blk)
            return carry

        lax.fori_loop(0, blocks, one, 0)

    xbuf[...] = jnp.zeros_like(xbuf)
    loop(lambda blk: each(blk, lambda copy: copy.start()))
    weights[0].wait()

    def take(blk):
        x16 = xbuf[block_rows(blk, SB)].astype(F32)
        return jnp.concatenate([x16[:, :rows], x16[:, rows:]], axis=-1).reshape(size, width)

    def queries(blk):
        each(blk, lambda copy: copy.wait())
        got = (dot_nt(take(blk).astype(BF16), wq[...]) * scale).astype(BF16)
        for s in range(shards):
            q[s, block_rows(blk, size), :] = got[:, s * LANES : (s + 1) * LANES]

    loop(queries)
    weights[1].wait()

    def score(img, at, count, first):
        for s in range(shards):
            keys = k[pl.ds(img * head, head), s * LANES : (s + 1) * LANES]
            p[s, pl.ds(at, win), :cols] = dot_nt(
                q[s, pl.ds(at, win), :], head_blocks(keys, heads, head)
            )

    windows(ints, images, rows, score, True)

    def soften(blk):
        at = block_rows(blk, size)
        for s in range(shards):
            raised = jnp.exp(p[s, at, :cols])
            prob = raised / head_sum(raised, head)
            p[s, at, :cols] = prob
            half[s, at, :cols] = prob.astype(BF16)
            for copy in results(blk, s):
                copy.start()

    loop(soften)
    weights[2].wait()

    def mix(img, at, count, first):
        for s in range(shards):
            lanes = slice(s * LANES, (s + 1) * LANES)
            vals = head_blocks(v[pl.ds(img * head, head), lanes], heads, head)
            mixed[pl.ds(at, win), lanes] = dot(half[s, pl.ds(at, win), :cols], vals).astype(BF16)

    windows(ints, images, rows, mix, True)
    weights[3].wait()
    scaled = const_ref[1:2]
    flat = scaled - jnp.mean(scaled, axis=-1, keepdims=True)

    def finish(blk):
        at = block_rows(blk, size)
        residual = take(blk) + dot(mixed[at, :], wo[...])
        centred = residual - jnp.mean(residual, axis=-1, keepdims=True)
        variance = jnp.mean(centred * centred, axis=-1, keepdims=True)
        inverse = 1.0 / jnp.sqrt(variance + EPS)
        unit = centred * inverse
        none = jnp.sum(unit * const_ref[0:1], axis=-1, keepdims=True)
        gap = jnp.sum(unit * scaled, axis=-1, keepdims=True)
        both = jnp.where(iota((size, 128), 1) == 0, none, none + gap)
        log_out[block_rows(blk, SB), :] = jnp.sum(both.reshape(SB, rows, 128), axis=1)
        d_res[at, :] = (inverse * (flat - unit * (gap / width))).astype(BF16)
        gradient(blk).start()

    loop(finish)

    def settle(blk):
        for s in range(shards):
            for copy in results(blk, s):
                copy.wait()
        gradient(blk).wait()

    loop(settle)


def backward_kernel(
    ints, delta_ref, d_in, wo_in, v_in, p_in, q_in, *rest, shard, head, heads, rows
):
    *arrived, out_ref, d_res, wo, v, p, q, dm, d_att, ds, pd, acc, sems = rest
    cols = heads * head
    images = v.shape[0] // head
    size = SB * rows
    win = WIN * rows
    blocks = blocks_of(ints)
    lanes = pl.ds(shard * LANES, LANES)
    used = pl.ds(0, q.shape[0] - win)
    copies = [
        pltpu.make_async_copy(src, dst, sems.at[j])
        for j, (src, dst) in enumerate(
            (
                (d_in, d_res),
                (wo_in.at[lanes, :], wo),
                (v_in.at[:, lanes], v),
                (p_in.at[shard], p),
                (q_in.at[shard], q.at[used]),
            )
        )
    ]
    for copy in copies:
        copy.start()

    def loop(body):
        def one(blk, carry):
            body(blk)
            return carry

        lax.fori_loop(0, blocks, one, 0)

    tail = pl.ds(pl.multiple_of(blocks * size, size), win)
    dm[tail, :] = jnp.zeros((win, LANES), BF16)
    copies[0].wait()
    copies[1].wait()

    def carry_back(blk):
        at = block_rows(blk, size)
        dm[at, :] = dot_nt(d_res[at, :], wo[...]).astype(BF16)

    loop(carry_back)
    copies[2].wait()

    def attend(img, at, count, first):
        vals = head_blocks(v[pl.ds(img * head, head), :], heads, head)
        d_att[pl.ds(at, win), :cols] = dot_nt(dm[pl.ds(at, win), :], vals)

    windows(ints, images, rows, attend, True)
    copies[3].wait()

    def soften(blk):
        at = block_rows(blk, size)
        prob = p[at, :cols]
        grad = d_att[at, :cols]
        weight = delta_ref[block_rows(blk, SB), :]
        weight = jnp.broadcast_to(weight[:, None, :], (SB, rows, 128)).reshape(size, 128)[:, :1]
        inner = head_sum(grad * prob, head)
        weighted = prob * weight
        ds[at, :cols] = (weighted * (grad - inner)).astype(BF16)
        pd[at, :cols] = weighted.astype(BF16)

    loop(soften)
    copies[4].wait()
    q[tail, :] = jnp.zeros((win, LANES), BF16)
    lane_head = iota((head, LANES), 1) // head
    place = iota((win, cols), 0)

    def diagonal(block):
        total = block[:head]
        for h in range(1, heads):
            total = jnp.where(lane_head == h, block[h * head : (h + 1) * head], total)
        return total[:, :cols]

    def outer(img, at, count, first):
        own = place < count
        here = pl.ds(at, win)
        zero = jnp.zeros((win, cols), BF16)
        dk = diagonal(dot_tn(jnp.where(own, ds[here, :cols], zero), q[here, :]))
        dv = diagonal(dot_tn(jnp.where(own, pd[here, :cols], zero), dm[here, :]))
        term = jnp.concatenate([dk, dv], axis=-1)
        if first:
            acc[img * head : (img + 1) * head, :] = term
        else:
            acc[pl.ds(pl.multiple_of(img * head, head), head), :] += term

    windows(ints, images, rows, outer, False)
    total = acc[...]
    for a in arrived:
        total = total + a[...].astype(F32)
    out_ref[...] = total.astype(out_ref.dtype)


def whole(a):
    return pl.BlockSpec(a.shape, lambda *_: (0,) * a.ndim)


def local(
    images, query_states, neg_caption, neg_image, cross_query, cross_kv, cross_out, norm_gain,
    itm_weight,
):
    pair_count, patches, vis = images.shape
    queries, width = query_states.shape[1:]
    cols = cross_query.shape[1]
    head = width // HEADS
    scale = 1.0 / head**0.5
    groups = lax.axis_size("dp")
    shards = lax.axis_size("mp")
    dp, mp = lax.axis_index("dp"), lax.axis_index("mp")
    core = dp % NC
    rows = queries // shards
    half = width // 2

    def around(x, by):
        return lax.ppermute(x, "mp", [(i, (i + by) % shards) for i in range(shards)])

    def shift(x, by_z, by_x, by_core):
        moves = []
        for i in range(groups):
            z, x_, c = i // (NX * NC), i // NC % NX, i % NC
            to = ((z + by_z) % NZ * NX + (x_ + by_x) % NX) * NC + (c + by_core) % NC
            moves.append((i, to))
        return lax.ppermute(x, "dp", moves)

    own_rows = lax.dynamic_slice_in_dim(query_states, mp * rows, rows, 1)
    packed = jnp.concatenate([own_rows[:, :, :half], own_rows[:, :, half:]], axis=1)
    pool = lax.all_gather(packed, "dp", axis=0, tiled=True)
    ids = jnp.zeros((8, 128), I32).at[0, :pair_count].set(neg_image)
    all_images = lax.all_gather(ids, "dp", axis=0, tiled=True)
    all_images = all_images.reshape(groups, 8, 128)[:, 0, :pair_count].reshape(-1, 1)

    halves = [
        jnp.concatenate([cross_kv[0].T, cross_query.T], axis=1),
        jnp.concatenate([cross_kv[1].T, cross_out], axis=1),
    ]
    brought = jnp.where(core == 0, halves[0], halves[1])
    got = [around(brought, shards - s) for s in range(1, shards)]
    swap = [shift(g, 0, 0, 1) for g in got]
    padded = []
    for c in range(NC):
        pieces = [halves[c]] + [jnp.where(core == c, g, w) for g, w in zip(got, swap)]
        stacked = jnp.stack([jnp.pad(p, ((0, LANES - cols), (0, 0))) for p in pieces])
        padded.append(stacked.reshape(shards * LANES, vis + width))
    flat = images.reshape(pair_count * patches, vis)
    keys = dot_nt(flat, padded[0][:, :vis]).astype(BF16)
    values = dot_nt(flat, padded[1][:, :vis]).astype(BF16)
    wq, wo = padded[0][:, vis:], padded[1][:, vis:]

    out_rows = vis // groups
    pad_rows = (out_rows + 1 + 7) // 8 * 8
    feature = iota((vis, groups * pad_rows), 0)
    place = iota((vis, groups * pad_rows), 1)
    target = jnp.where(
        place % pad_rows < out_rows, place // pad_rows * out_rows + place % pad_rows, -1
    )
    chosen = (feature == target).astype(BF16)
    spread = lax.dot_general(
        chosen, flat, (((0,), (1,)), ((), ())), preferred_element_type=F32
    ).astype(BF16)
    spread, keys = lax.optimization_barrier((spread, keys))

    most = pair_count * (2 + CE - 1) + 2 * groups
    n_slots = -(-(most + WIN - CE) // SB) * SB
    n_rows = n_slots * rows
    params = pltpu.CompilerParams(vmem_limit_bytes=56 * 2**20)
    ints, sign, hit = pl.pallas_call(
        plan_kernel,
        in_specs=[
            pl.BlockSpec(memory_space=pltpu.SMEM),
            pl.BlockSpec(memory_space=pltpu.VMEM),
            pl.BlockSpec(memory_space=pltpu.VMEM),
        ],
        out_specs=[pl.BlockSpec(memory_space=pltpu.VMEM)] * 3,
        out_shape=[
            jax.ShapeDtypeStruct((8, n_slots), I32),
            jax.ShapeDtypeStruct((1, n_slots), F32),
            jax.ShapeDtypeStruct((groups * pair_count, n_slots), BF16),
        ],
        compiler_params=params,
        name="plan",
    )(dp.astype(I32).reshape(1), all_images, neg_caption.reshape(-1, 1))
    sign = sign[0]

    fold = norm_gain / queries
    const = jnp.stack([fold * itm_weight[:, 0], fold * (itm_weight[:, 1] - itm_weight[:, 0])])
    smem = pl.BlockSpec(memory_space=pltpu.SMEM)
    anywhere = pl.BlockSpec(memory_space=pl.ANY)
    vmem = pl.BlockSpec(memory_space=pltpu.VMEM)
    q_rows, prob, d_res, log_part = pl.pallas_call(
        functools.partial(forward_kernel, head=head, scale=scale),
        in_specs=[smem] + [anywhere] * 5 + [vmem],
        out_specs=[anywhere] * 3 + [vmem],
        scratch_shapes=[
            pltpu.VMEM((n_slots, 2 * rows, half), BF16),
            pltpu.VMEM(wq.shape, BF16),
            pltpu.VMEM(keys.shape, BF16),
            pltpu.VMEM(values.shape, BF16),
            pltpu.VMEM(wo.shape, BF16),
            pltpu.VMEM((shards, n_rows, LANES), BF16),
            pltpu.VMEM((shards, n_rows, LANES), F32),
            pltpu.VMEM((shards, n_rows, LANES), BF16),
            pltpu.VMEM((n_rows, shards * LANES), BF16),
            pltpu.VMEM((n_rows, width), BF16),
            pltpu.SemaphoreType.DMA((n_slots // SB,)),
            pltpu.SemaphoreType.DMA((4,)),
            pltpu.SemaphoreType.DMA((3,)),
        ],
        out_shape=[
            jax.ShapeDtypeStruct((shards, n_rows, LANES), BF16),
            jax.ShapeDtypeStruct((shards, n_rows, LANES), F32),
            jax.ShapeDtypeStruct((n_rows, width), BF16),
            jax.ShapeDtypeStruct((n_slots, 128), F32),
        ],
        compiler_params=params,
        name="forward",
    )(ints, pool, wq, keys, values, wo, const)

    part = jnp.where((sign != 0.0)[None, :], log_part[:, :2].T, 0.0)
    terms = [part] + [around(part, shards - s) for s in range(1, shards)]
    logits = jnp.zeros_like(part)
    for m in range(shards):
        for s in range(shards):
            logits = logits + jnp.where((mp + s) % shards == m, terms[s], 0.0)
    delta = sign / (1.0 + jnp.exp(sign * (logits[0] - logits[1])))
    delta = jnp.broadcast_to(delta[:, None], (n_slots, 128))

    def backward(s, arrived=(), kind=BF16):
        shape = (pair_count * patches, 2 * cols)
        slack = n_rows + WIN * rows
        return pl.pallas_call(
            functools.partial(
                backward_kernel, shard=s, head=head, heads=HEADS // shards, rows=rows
            ),
            in_specs=[smem, vmem] + [anywhere] * 5 + [vmem] * len(arrived),
            out_specs=vmem,
            scratch_shapes=[
                pltpu.VMEM((n_rows, width), BF16),
                pltpu.VMEM((LANES, width), BF16),
                pltpu.VMEM((pair_count * patches, LANES), BF16),
                pltpu.VMEM((n_rows, LANES), F32),
                pltpu.VMEM((slack, LANES), BF16),
                pltpu.VMEM((slack, LANES), BF16),
                pltpu.VMEM((slack, LANES), F32),
                pltpu.VMEM((slack, LANES), BF16),
                pltpu.VMEM((slack, LANES), BF16),
                pltpu.VMEM(shape, F32),
                pltpu.SemaphoreType.DMA((5,)),
            ],
            out_shape=jax.ShapeDtypeStruct(shape, kind),
            compiler_params=params,
            cost_estimate=pl.CostEstimate(flops=10**6, bytes_accessed=10**4, transcendentals=0),
            name="backward",
        )(ints, delta, d_res, wo, values, prob, q_rows, *arrived)

    terms = [around(backward(s), s) for s in range(1, shards)]
    d_kv = backward(0, terms[:2], F32)
    d_kv = (d_kv + sum(term.astype(F32) for term in terms[2:])).astype(BF16)

    logit_hi = logits.astype(BF16)
    logit_lo = (logits - logit_hi.astype(F32)).astype(BF16)
    four = jnp.concatenate([logit_hi, logit_lo], axis=0)
    home = dot_nt(hit, four).astype(BF16)
    home = jnp.pad(
        home.reshape(groups, 1, 4 * pair_count),
        ((0, 0), (out_rows, pad_rows - out_rows - 1), (0, 2 * cols - 4 * pair_count)),
    )
    home, d_kv = lax.optimization_barrier((home, d_kv))
    grad = dot(spread, d_kv).astype(BF16)
    leaving = grad.reshape(groups, pad_rows, 2 * cols) + home
    arrived = lax.all_to_all(leaving, "dp", split_axis=0, concat_axis=0, tiled=True)
    summed = jnp.sum(arrived.astype(F32), axis=0)
    grad_part = jnp.transpose(summed[:out_rows].reshape(out_rows, 2, cols), (1, 0, 2))
    back = summed[out_rows, : 4 * pair_count].reshape(pair_count, 2, 2)
    pushed_logits = back[:, 0] + back[:, 1]
    image = jnp.arange(pair_count, dtype=I32)[:, None]
    own_logits = []
    for j in range(2):
        here = ((ints[1:2] == image) & (ints[2:3] == j))[:, None, :]
        own_logits.append(jnp.sum(jnp.where(here, logits[None], 0.0), axis=-1))
    return (jnp.stack(own_logits + [pushed_logits]), grad_part)


def solution(mesh):
    return jax.shard_map(
        local,
        mesh=mesh,
        in_specs=(
            P("dp", None, None),
            P("dp", None, None),
            P("dp"),
            P("dp"),
            P(None, "mp"),
            P(None, None, "mp"),
            P("mp", None),
            P(),
            P(),
        ),
        out_specs=(P(None, "dp", None), P(None, "dp", "mp")),
        check_vma=False,
    )
```

```python
import functools

import jax
import jax.numpy as jnp
from jax import lax
from jax.experimental import pallas as pl
from jax.experimental.pallas import tpu as pltpu
from jax.sharding import PartitionSpec as P

HEADS = 12
EPS = 1e-06
CE = 2
SB = 32
WIN = 16
LANES = 256
NZ, NX, NC = 8, 4, 2
BF16 = jnp.bfloat16
F32 = jnp.float32
I32 = jnp.int32


def dot(a, b):
    return jnp.dot(a, b, preferred_element_type=F32)


def dot_nt(a, b):
    return lax.dot_general(a, b, (((1,), (1,)), ((), ())), preferred_element_type=F32)


def dot_tn(a, b):
    return lax.dot_general(a, b, (((0,), (0,)), ((), ())), preferred_element_type=F32)


def iota(shape, axis):
    return lax.broadcasted_iota(I32, shape, axis)


def head_blocks(rows, heads, head):
    lane_head = iota(rows.shape, 1) // head
    zero = jnp.zeros_like(rows)
    return jnp.concatenate([jnp.where(lane_head == h, rows, zero) for h in range(heads)], axis=0)


def head_sum(values, head):
    width = values.shape[-1]
    same = iota((width, width), 0) // head == iota((width, width), 1) // head
    ones = jnp.where(same, 1.0, 0.0).astype(BF16)
    upper = values.astype(BF16)
    lower = (values - upper.astype(F32)).astype(BF16)
    return dot(upper, ones) + dot(lower, ones)


def plan_kernel(dp_ref, ids_ref, neg_ref, ints_out, sign_out, hit_out):
    total = ids_ref.shape[0]
    images = neg_ref.shape[0]
    slots = ints_out.shape[1]
    base = dp_ref[0] * images
    own = (ids_ref[...] - base) == iota((total, images), 1)
    ones = jnp.where(own, 1.0, 0.0)
    below = jnp.where(iota((128, 128), 0) >= iota((128, 128), 1), 1.0, 0.0).astype(BF16)
    count_row = jnp.zeros((1, images), F32)
    upto = []
    for j in range(total // 128):
        piece = ones[128 * j : 128 * (j + 1)]
        upto.append(dot(below, piece.astype(BF16)) + count_row)
        count_row = count_row + jnp.sum(piece, axis=0, keepdims=True)
    upto = jnp.concatenate(upto, axis=0)
    diagonal = iota((images, images), 0) == iota((images, images), 1)
    count_col = jnp.sum(jnp.where(diagonal, count_row, 0.0), axis=1, keepdims=True)

    def chunks_of(count):
        return lax.div(count.astype(I32) + (2 + CE - 1), jnp.full(count.shape, CE, I32))

    chunks_row, chunks_col = chunks_of(count_row), chunks_of(count_col)
    before = iota((images, images), 0) < iota((images, images), 1)
    after = iota((images, images), 0) > iota((images, images), 1)
    first_row = jnp.sum(jnp.where(before, chunks_col, 0), axis=0, keepdims=True)
    first_col = jnp.sum(jnp.where(after, chunks_row, 0), axis=1, keepdims=True)
    n_chunks = jnp.sum(chunks_row, axis=1, keepdims=True)
    slot_of = jnp.sum(
        jnp.where(own, (first_row * CE + 1).astype(F32) + upto, 0.0), axis=1, keepdims=True
    ).astype(I32)
    slot = iota((1, slots), 1)
    chunk = lax.div(slot, jnp.full(slot.shape, CE, I32))
    img = jnp.sum(jnp.where(chunk >= first_col, 1, 0), axis=0, keepdims=True) - 1
    at_img = img == iota((images, slots), 0)
    pos = slot - CE * jnp.sum(jnp.where(at_img, first_col, 0), axis=0, keepdims=True)
    negative = jnp.sum(jnp.where(at_img, neg_ref[...], 0), axis=0, keepdims=True)
    hit = (slot_of == slot) & (pos >= 2)
    number = jnp.where(hit, iota((total, slots), 0) + 1, 0)
    pushed = jnp.sum(number, axis=0, keepdims=True)
    used = (chunk < n_chunks) & ((pos < 2) | (pushed > 0))
    cap = jnp.where(pos == 0, base + img, jnp.where(pos == 1, negative, pushed - 1))
    cap = jnp.where(used, cap, -1)
    row = iota((8, slots), 0)
    lane = iota((images, slots), 0) == iota((images, slots), 1)
    start = jnp.sum(jnp.where(lane, first_col * CE, 0), axis=0, keepdims=True)
    count = jnp.sum(jnp.where(lane, count_col.astype(I32) + 2, 0), axis=0, keepdims=True)
    ints = n_chunks
    for at, values in enumerate((cap, img, pos, n_chunks, start, count)):
        ints = jnp.where(row == at, values, ints)
    ints_out[...] = ints
    sign_out[...] = jnp.zeros_like(sign_out)
    sign_out[:, :slots] = jnp.where(used, jnp.where(pos == 0, -1.0, 1.0), 0.0)
    place = iota((total, 1), 0)
    chip = lax.div(place, jnp.full_like(place, images))
    half = lax.div(chip, jnp.full_like(chip, total // images // NC))
    core = lax.rem(half + lax.rem(dp_ref[0], NC), jnp.full_like(half, NC))
    chip = lax.rem(chip, jnp.full_like(chip, total // images // NC))
    number = (chip * NC + core) * images + lax.rem(place, jnp.full_like(place, images))
    home = (number == cap) & used & (pos >= 2)
    hit_out[...] = jnp.where(home, 1.0, 0.0).astype(BF16)


def blocks_of(ints):
    return lax.div(ints[3, 0] * CE + (SB - 1), SB)


def windows(ints, images, rows, act, extra_first):
    def extra():
        def one(img, carry):
            count = ints[5, img]

            def more(w, carry):
                at = pl.multiple_of((ints[4, img] + w * WIN) * rows, CE * rows)
                act(img, at, (count - w * WIN) * rows, False)
                return carry

            return lax.fori_loop(1, lax.div(count + (WIN - 1), WIN), more, carry)

        lax.fori_loop(0, images, one, 0)

    if extra_first:
        extra()
    for img in range(images):
        at = pl.multiple_of(ints[4, img] * rows, CE * rows)
        act(img, at, ints[5, img] * rows, True)
    if not extra_first:
        extra()


def block_rows(blk, size):
    return pl.ds(pl.multiple_of(blk * size, size), size)


def forward_kernel(
    ints, pool, wq_in, k_in, v_in, wo_in, const_ref, q_out, p_out, d_out, log_out,
    xbuf, wq, k, v, wo, q, p, half, mixed, d_res, logs, sem_x, sem_w, sem_o, *, head, scale,
):
    width = wo.shape[1]
    shards = wq.shape[0] // LANES
    heads = HEADS // shards
    cols = heads * head
    images = k.shape[0] // head
    rows = xbuf.shape[1] // 2
    size = SB * rows
    win = WIN * rows
    blocks = blocks_of(ints)
    weights = [
        pltpu.make_async_copy(src, dst, sem_w.at[j])
        for j, (src, dst) in enumerate(((wq_in, wq), (k_in, k), (v_in, v), (wo_in, wo)))
    ]
    for copy in weights:
        copy.start()

    def each(blk, act):
        def one(j, carry):
            slot = blk * SB + j

            @pl.when(ints[0, slot] >= 0)
            def _():
                act(pltpu.make_async_copy(pool.at[ints[0, slot]], xbuf.at[slot], sem_x.at[blk]))

            return carry

        lax.fori_loop(0, SB, one, 0)

    def results(blk, s):
        at = block_rows(blk, size)
        return [
            pltpu.make_async_copy(q.at[s, at], q_out.at[s, at], sem_o.at[0]),
            pltpu.make_async_copy(p.at[s, at], p_out.at[s, at], sem_o.at[1]),
        ]

    def gradient(blk):
        at = block_rows(blk, size)
        return pltpu.make_async_copy(d_res.at[at], d_out.at[at], sem_o.at[2])

    def loop(body):
        def one(blk, carry):
            body(blk)
            return carry

        lax.fori_loop(0, blocks, one, 0)

    xbuf[...] = jnp.zeros_like(xbuf)
    loop(lambda blk: each(blk, lambda copy: copy.start()))
    weights[0].wait()

    def take(blk):
        x16 = xbuf[block_rows(blk, SB)].astype(F32)
        return jnp.concatenate([x16[:, :rows], x16[:, rows:]], axis=-1).reshape(size, width)

    def queries(blk):
        each(blk, lambda copy: copy.wait())
        got = (dot_nt(take(blk).astype(BF16), wq[...]) * scale).astype(BF16)
        for s in range(shards):
            q[s, block_rows(blk, size), :] = got[:, s * LANES : (s + 1) * LANES]

    loop(queries)
    weights[1].wait()

    def score(img, at, count, first):
        for s in range(shards):
            keys = k[pl.ds(img * head, head), s * LANES : (s + 1) * LANES]
            p[s, pl.ds(at, win), :cols] = dot_nt(
                q[s, pl.ds(at, win), :], head_blocks(keys, heads, head)
            )

    windows(ints, images, rows, score, True)

    def soften(blk):
        at = block_rows(blk, size)
        for s in range(shards):
            raised = jnp.exp(p[s, at, :cols])
            prob = raised / head_sum(raised, head)
            p[s, at, :cols] = prob
            half[s, at, :cols] = prob.astype(BF16)
            for copy in results(blk, s):
                copy.start()

    loop(soften)
    weights[2].wait()

    def mix(img, at, count, first):
        for s in range(shards):
            lanes = slice(s * LANES, (s + 1) * LANES)
            vals = head_blocks(v[pl.ds(img * head, head), lanes], heads, head)
            mixed[pl.ds(at, win), lanes] = dot(half[s, pl.ds(at, win), :cols], vals).astype(BF16)

    windows(ints, images, rows, mix, True)
    weights[3].wait()
    scaled = const_ref[1:2]
    flat = scaled - jnp.mean(scaled, axis=-1, keepdims=True)

    def finish(blk):
        at = block_rows(blk, size)
        residual = take(blk) + dot(mixed[at, :], wo[...])
        centred = residual - jnp.mean(residual, axis=-1, keepdims=True)
        variance = jnp.mean(centred * centred, axis=-1, keepdims=True)
        inverse = 1.0 / jnp.sqrt(variance + EPS)
        unit = centred * inverse
        none = jnp.sum(unit * const_ref[0:1], axis=-1, keepdims=True)
        gap = jnp.sum(unit * scaled, axis=-1, keepdims=True)
        both = jnp.where(iota((size, 128), 1) == 0, none, none + gap)
        logs[block_rows(blk, SB), :] = jnp.sum(both.reshape(SB, rows, 128), axis=1)
        d_res[at, :] = (inverse * (flat - unit * (gap / width))).astype(BF16)
        gradient(blk).start()

    loop(finish)
    log_out[...] = logs[...].T[: log_out.shape[0]]

    def settle(blk):
        for s in range(shards):
            for copy in results(blk, s):
                copy.wait()
        gradient(blk).wait()

    loop(settle)


def backward_kernel(
    ints, sign_ref, *rest, mine, arrivals, head, heads, rows, terms
):
    parts, rest = rest[:terms], rest[terms:]
    d_in, wo_in, v_in, p_in, q_in = rest[:5]
    arrived, rest = rest[5 : 5 + arrivals], rest[5 + arrivals :]
    outs, rest = rest[: len(mine)], rest[len(mine) :]
    d_res, wo, v, p, q, dm, d_att, ds, pd, acc, delta, sems = rest
    cols = heads * head
    images = v.shape[1] // head
    size = SB * rows
    win = WIN * rows
    blocks = blocks_of(ints)
    used = pl.ds(0, q.shape[1] - win)
    pltpu.make_async_copy(d_in, d_res, sems.at[0]).start()
    copies = []
    for j, shard in enumerate(mine):
        lanes = pl.ds(shard * LANES, LANES)
        copies.append(
            [
                pltpu.make_async_copy(src, dst, sems.at[1 + 4 * j + n])
                for n, (src, dst) in enumerate(
                    (
                        (wo_in.at[lanes, :], wo.at[j]),
                        (v_in.at[:, lanes], v.at[j]),
                        (p_in.at[shard], p.at[j]),
                        (q_in.at[shard], q.at[j, used]),
                    )
                )
            ]
        )
    for n in range(4):
        for group in copies:
            group[n].start()

    def loop(body):
        def one(blk, carry):
            body(blk)
            return carry

        lax.fori_loop(0, blocks, one, 0)

    def settle(n):
        for group in copies:
            group[n].wait()

    logits = sum(part[...] for part in parts[1:]) + parts[0][...]
    sign = sign_ref[...]
    factor = sign / (1.0 + jnp.exp(sign * (logits[0:1] - logits[1:2])))
    delta[...] = jnp.broadcast_to(factor, (128, factor.shape[1])).T
    tail = pl.ds(pl.multiple_of(blocks * size, size), win)
    for j in range(len(mine)):
        dm[j, tail, :] = jnp.zeros((win, LANES), BF16)
    pltpu.make_async_copy(d_in, d_res, sems.at[0]).wait()
    settle(0)

    def carry_back(blk):
        at = block_rows(blk, size)
        for j in range(len(mine)):
            dm[j, at, :] = dot_nt(d_res[at, :], wo[j]).astype(BF16)

    loop(carry_back)
    settle(1)

    def attend(img, at, count, first):
        for j in range(len(mine)):
            vals = head_blocks(v[j, pl.ds(img * head, head), :], heads, head)
            d_att[j, pl.ds(at, win), :cols] = dot_nt(dm[j, pl.ds(at, win), :], vals)

    windows(ints, images, rows, attend, True)
    settle(2)

    def soften(blk):
        at = block_rows(blk, size)
        weight = delta[block_rows(blk, SB), :]
        weight = jnp.broadcast_to(weight[:, None, :], (SB, rows, 128)).reshape(size, 128)[:, :1]
        for j in range(len(mine)):
            prob = p[j, at, :cols]
            grad = d_att[j, at, :cols]
            inner = head_sum(grad * prob, head)
            weighted = prob * weight
            ds[j, at, :cols] = (weighted * (grad - inner)).astype(BF16)
            pd[j, at, :cols] = weighted.astype(BF16)

    loop(soften)
    settle(3)
    for j in range(len(mine)):
        q[j, tail, :] = jnp.zeros((win, LANES), BF16)
    lane_head = iota((head, LANES), 1) // head
    place = iota((win, cols), 0)

    def diagonal(block):
        total = block[:head]
        for h in range(1, heads):
            total = jnp.where(lane_head == h, block[h * head : (h + 1) * head], total)
        return total[:, :cols]

    def outer(img, at, count, first):
        own = place < count
        here = pl.ds(at, win)
        zero = jnp.zeros((win, cols), BF16)
        for j in range(len(mine)):
            dk = diagonal(dot_tn(jnp.where(own, ds[j, here, :cols], zero), q[j, here, :]))
            dv = diagonal(dot_tn(jnp.where(own, pd[j, here, :cols], zero), dm[j, here, :]))
            term = jnp.concatenate([dk, dv], axis=-1)
            if first:
                acc[j, img * head : (img + 1) * head, :] = term
            else:
                acc[j, pl.ds(pl.multiple_of(img * head, head), head), :] += term

    windows(ints, images, rows, outer, False)
    for j, out_ref in enumerate(outs):
        total = acc[j]
        for a in arrived:
            total = total + a[...].astype(F32)
        out_ref[...] = total.astype(out_ref.dtype)


def whole(a):
    return pl.BlockSpec(a.shape, lambda *_: (0,) * a.ndim)


def local(
    images, query_states, neg_caption, neg_image, cross_query, cross_kv, cross_out, norm_gain,
    itm_weight,
):
    pair_count, patches, vis = images.shape
    queries, width = query_states.shape[1:]
    cols = cross_query.shape[1]
    head = width // HEADS
    scale = 1.0 / head**0.5
    groups = lax.axis_size("dp")
    shards = lax.axis_size("mp")
    dp, mp = lax.axis_index("dp"), lax.axis_index("mp")
    core = dp % NC
    rows = queries // shards
    half = width // 2

    def around(x, by):
        return lax.ppermute(x, "mp", [(i, (i + by) % shards) for i in range(shards)])

    def shift(x, by_z, by_x, by_core):
        moves = []
        for i in range(groups):
            z, x_, c = i // (NX * NC), i // NC % NX, i % NC
            to = ((z + by_z) % NZ * NX + (x_ + by_x) % NX) * NC + (c + by_core) % NC
            moves.append((i, to))
        return lax.ppermute(x, "dp", moves)

    own_rows = lax.dynamic_slice_in_dim(query_states, mp * rows, rows, 1)
    packed = jnp.concatenate([own_rows[:, :, :half], own_rows[:, :, half:]], axis=1)
    pool = lax.all_gather(packed, "dp", axis=0, tiled=True)
    ids = jnp.zeros((8, 128), I32).at[0, :pair_count].set(neg_image)
    all_images = lax.all_gather(ids, "dp", axis=0, tiled=True)
    all_images = all_images.reshape(groups, 8, 128)[:, 0, :pair_count].reshape(-1, 1)

    halves = [
        jnp.concatenate([cross_kv[0].T, cross_query.T], axis=1),
        jnp.concatenate([cross_kv[1].T, cross_out], axis=1),
    ]
    brought = jnp.where(core == 0, halves[0], halves[1])
    got = [around(brought, shards - s) for s in range(1, shards)]
    swap = [shift(g, 0, 0, 1) for g in got]
    padded = []
    for c in range(NC):
        pieces = [halves[c]] + [jnp.where(core == c, g, w) for g, w in zip(got, swap)]
        stacked = jnp.stack([jnp.pad(p, ((0, LANES - cols), (0, 0))) for p in pieces])
        padded.append(stacked.reshape(shards * LANES, vis + width))
    flat = images.reshape(pair_count * patches, vis)
    keys = dot_nt(flat, padded[0][:, :vis]).astype(BF16)
    values = dot_nt(flat, padded[1][:, :vis]).astype(BF16)
    wq, wo = padded[0][:, vis:], padded[1][:, vis:]

    out_rows = vis // groups
    pad_rows = (out_rows + 1 + 7) // 8 * 8
    feature = iota((vis, groups * pad_rows), 0)
    place = iota((vis, groups * pad_rows), 1)
    chips = groups // NC
    goal = place // pad_rows
    goal = goal % chips * NC + (goal // chips + core) % NC
    target = jnp.where(place % pad_rows < out_rows, goal * out_rows + place % pad_rows, -1)
    chosen = (feature == target).astype(BF16)
    spread = lax.dot_general(
        chosen, flat, (((0,), (1,)), ((), ())), preferred_element_type=F32
    ).astype(BF16)

    most = pair_count * (2 + CE - 1) + 2 * groups
    n_slots = -(-(most + WIN - CE) // SB) * SB
    n_rows = n_slots * rows
    n_lanes = -(-n_slots // 128) * 128
    params = pltpu.CompilerParams(vmem_limit_bytes=56 * 2**20)
    ints, sign, hit = pl.pallas_call(
        plan_kernel,
        in_specs=[
            pl.BlockSpec(memory_space=pltpu.SMEM),
            pl.BlockSpec(memory_space=pltpu.VMEM),
            pl.BlockSpec(memory_space=pltpu.VMEM),
        ],
        out_specs=[pl.BlockSpec(memory_space=pltpu.VMEM)] * 3,
        out_shape=[
            jax.ShapeDtypeStruct((8, n_slots), I32),
            jax.ShapeDtypeStruct((1, n_lanes), F32),
            jax.ShapeDtypeStruct((groups * pair_count, n_slots), BF16),
        ],
        compiler_params=params,
        name="plan",
    )(dp.astype(I32).reshape(1), all_images, neg_caption.reshape(-1, 1))

    fold = norm_gain / queries
    const = jnp.stack([fold * itm_weight[:, 0], fold * (itm_weight[:, 1] - itm_weight[:, 0])])
    smem = pl.BlockSpec(memory_space=pltpu.SMEM)
    anywhere = pl.BlockSpec(memory_space=pl.ANY)
    vmem = pl.BlockSpec(memory_space=pltpu.VMEM)
    q_rows, prob, d_res, log_part = pl.pallas_call(
        functools.partial(forward_kernel, head=head, scale=scale),
        in_specs=[smem] + [anywhere] * 5 + [vmem],
        out_specs=[anywhere] * 3 + [vmem],
        scratch_shapes=[
            pltpu.VMEM((n_slots, 2 * rows, half), BF16),
            pltpu.VMEM(wq.shape, BF16),
            pltpu.VMEM(keys.shape, BF16),
            pltpu.VMEM(values.shape, BF16),
            pltpu.VMEM(wo.shape, BF16),
            pltpu.VMEM((shards, n_rows, LANES), BF16),
            pltpu.VMEM((shards, n_rows, LANES), F32),
            pltpu.VMEM((shards, n_rows, LANES), BF16),
            pltpu.VMEM((n_rows, shards * LANES), BF16),
            pltpu.VMEM((n_rows, width), BF16),
            pltpu.VMEM((n_lanes, 128), F32),
            pltpu.SemaphoreType.DMA((n_slots // SB,)),
            pltpu.SemaphoreType.DMA((4,)),
            pltpu.SemaphoreType.DMA((3,)),
        ],
        out_shape=[
            jax.ShapeDtypeStruct((shards, n_rows, LANES), BF16),
            jax.ShapeDtypeStruct((shards, n_rows, LANES), F32),
            jax.ShapeDtypeStruct((n_rows, width), BF16),
            jax.ShapeDtypeStruct((8, n_lanes), F32),
        ],
        compiler_params=params,
        name="forward",
    )(ints, pool, wq, keys, values, wo, const)

    parts = [log_part] + [around(log_part, shards - s) for s in range(1, shards)]
    logits = jnp.zeros((2, n_slots), F32)
    for m in range(shards):
        for s in range(shards):
            logits = logits + jnp.where((mp + s) % shards == m, parts[s][:2, :n_slots], 0.0)
    logits = jnp.where(sign[:, :n_slots] != 0.0, logits, 0.0)

    def backward(mine, arrived=(), kind=BF16):
        shape = (pair_count * patches, 2 * cols)
        slack = n_rows + WIN * rows
        n = len(mine)
        return pl.pallas_call(
            functools.partial(
                backward_kernel, mine=mine, arrivals=len(arrived), head=head,
                heads=HEADS // shards, rows=rows, terms=shards,
            ),
            in_specs=[smem] + [vmem] * (1 + shards) + [anywhere] * 5 + [vmem] * len(arrived),
            out_specs=[vmem] * n,
            scratch_shapes=[
                pltpu.VMEM((n_rows, width), BF16),
                pltpu.VMEM((n, LANES, width), BF16),
                pltpu.VMEM((n, pair_count * patches, LANES), BF16),
                pltpu.VMEM((n, n_rows, LANES), F32),
                pltpu.VMEM((n, slack, LANES), BF16),
                pltpu.VMEM((n, slack, LANES), BF16),
                pltpu.VMEM((n, slack, LANES), F32),
                pltpu.VMEM((n, slack, LANES), BF16),
                pltpu.VMEM((n, slack, LANES), BF16),
                pltpu.VMEM((n,) + shape, F32),
                pltpu.VMEM((n_lanes, 128), F32),
                pltpu.SemaphoreType.DMA((1 + 4 * n,)),
            ],
            out_shape=[jax.ShapeDtypeStruct(shape, kind)] * n,
            compiler_params=params,
            cost_estimate=pl.CostEstimate(flops=10**6, bytes_accessed=10**4, transcendentals=0),
            name="backward",
        )(ints, sign, *parts, d_res, wo, values, prob, q_rows, *arrived)

    one, three = backward((1, 3))
    terms = [around(one, 1), around(three, 3), around(backward((2,))[0], 2)]
    own, spread = lax.optimization_barrier((backward((0,), terms[:2], F32)[0], spread))
    d_kv = (own + terms[2].astype(F32)).astype(BF16)

    logit_hi = logits.astype(BF16)
    logit_lo = (logits - logit_hi.astype(F32)).astype(BF16)
    four = jnp.concatenate([logit_hi, logit_lo], axis=0)
    home = dot_nt(hit, four).astype(BF16)
    home = jnp.pad(
        home.reshape(groups, 1, 4 * pair_count),
        ((0, 0), (out_rows, pad_rows - out_rows - 1), (0, 2 * cols - 4 * pair_count)),
    )
    home, d_kv = lax.optimization_barrier((home, d_kv))
    grad = dot(spread, d_kv).reshape(groups, pad_rows, 2 * cols)
    over = shift((grad[chips:] + home[chips:]).astype(BF16), 0, 0, 1)
    leaving = (grad[:chips] + home[:chips] + over).astype(BF16)
    alike = [[chip * NC + c for chip in range(chips)] for c in range(NC)]
    arrived = lax.all_to_all(
        leaving, "dp", split_axis=0, concat_axis=0, tiled=True, axis_index_groups=alike
    )
    summed = jnp.sum(arrived.astype(F32), axis=0)
    grad_part = jnp.transpose(summed[:out_rows].reshape(out_rows, 2, cols), (1, 0, 2))
    back = summed[out_rows, : 4 * pair_count].reshape(pair_count, 2, 2)
    pushed_logits = back[:, 0] + back[:, 1]
    image = jnp.arange(pair_count, dtype=I32)[:, None]
    own_logits = []
    for j in range(2):
        here = ((ints[1:2] == image) & (ints[2:3] == j))[:, None, :]
        own_logits.append(jnp.sum(jnp.where(here, logits[None], 0.0), axis=-1))
    return (jnp.stack(own_logits + [pushed_logits]), grad_part)


def solution(mesh):
    return jax.shard_map(
        local,
        mesh=mesh,
        in_specs=(
            P("dp", None, None),
            P("dp", None, None),
            P("dp"),
            P("dp"),
            P(None, "mp"),
            P(None, None, "mp"),
            P("mp", None),
            P(),
            P(),
        ),
        out_specs=(P(None, "dp", None), P(None, "dp", "mp")),
        check_vma=False,
    )
```

```python
import functools

import jax
import jax.numpy as jnp
from jax import lax
from jax.experimental import pallas as pl
from jax.experimental.pallas import tpu as pltpu
from jax.sharding import PartitionSpec as P

HEADS = 12
EPS = 1e-06
CE = 2
SB = 32
WIN = 16
LANES = 256
NZ, NX, NC = 8, 4, 2
GATHERED = 12
BF16 = jnp.bfloat16
F32 = jnp.float32
I32 = jnp.int32


def dot(a, b):
    return jnp.dot(a, b, preferred_element_type=F32)


def dot_nt(a, b):
    return lax.dot_general(a, b, (((1,), (1,)), ((), ())), preferred_element_type=F32)


def dot_tn(a, b):
    return lax.dot_general(a, b, (((0,), (0,)), ((), ())), preferred_element_type=F32)


def iota(shape, axis):
    return lax.broadcasted_iota(I32, shape, axis)


def head_blocks(rows, heads, head):
    lane_head = iota(rows.shape, 1) // head
    zero = jnp.zeros_like(rows)
    return jnp.concatenate([jnp.where(lane_head == h, rows, zero) for h in range(heads)], axis=0)


def head_sum(values, head):
    width = values.shape[-1]
    same = iota((width, width), 0) // head == iota((width, width), 1) // head
    ones = jnp.where(same, 1.0, 0.0).astype(BF16)
    upper = values.astype(BF16)
    lower = (values - upper.astype(F32)).astype(BF16)
    return dot(upper, ones) + dot(lower, ones)


def plan_kernel(dp_ref, ids_ref, neg_ref, ints_out, sign_out, hit_out):
    total = ids_ref.shape[0]
    images = neg_ref.shape[0]
    slots = ints_out.shape[1]
    dp = dp_ref[0]
    z, x, c = lax.div(dp, NX * NC), lax.rem(lax.div(dp, NC), NX), lax.rem(dp, NC)
    base = dp * images
    place = iota((total, 1), 0)

    def digit(value, by, size):
        return lax.rem(lax.div(value, jnp.full_like(value, by)), jnp.full_like(value, size))

    def ahead(start, steps, size):
        to = start + steps
        return jnp.where(to >= size, to - size, to)

    block = ahead(z, digit(place, images * NX, NZ), NZ) * NX
    block = (block + ahead(x, digit(place, images, NX), NX)) * NC
    block = block + ahead(c, digit(place, images * NX * NZ, NC), NC)
    number = block * images + digit(place, 1, images)
    ids = ids_ref[...].astype(I32)
    ids = ids[:, :1] * 32 + ids[:, 1:]
    own = (ids - base) == iota((total, images), 1)
    ones = jnp.where(own, 1.0, 0.0)
    below = jnp.where(iota((128, 128), 0) >= iota((128, 128), 1), 1.0, 0.0).astype(BF16)
    count_row = jnp.zeros((1, images), F32)
    upto = []
    for j in range(total // 128):
        piece = ones[128 * j : 128 * (j + 1)]
        upto.append(dot(below, piece.astype(BF16)) + count_row)
        count_row = count_row + jnp.sum(piece, axis=0, keepdims=True)
    upto = jnp.concatenate(upto, axis=0)
    diagonal = iota((images, images), 0) == iota((images, images), 1)
    count_col = jnp.sum(jnp.where(diagonal, count_row, 0.0), axis=1, keepdims=True)

    def chunks_of(count):
        return lax.div(count.astype(I32) + (2 + CE - 1), jnp.full(count.shape, CE, I32))

    chunks_row, chunks_col = chunks_of(count_row), chunks_of(count_col)
    before = iota((images, images), 0) < iota((images, images), 1)
    after = iota((images, images), 0) > iota((images, images), 1)
    first_row = jnp.sum(jnp.where(before, chunks_col, 0), axis=0, keepdims=True)
    first_col = jnp.sum(jnp.where(after, chunks_row, 0), axis=1, keepdims=True)
    n_chunks = jnp.sum(chunks_row, axis=1, keepdims=True)
    slot_of = jnp.sum(
        jnp.where(own, (first_row * CE + 1).astype(F32) + upto, 0.0), axis=1, keepdims=True
    ).astype(I32)
    slot = iota((1, slots), 1)
    chunk = lax.div(slot, jnp.full(slot.shape, CE, I32))
    img = jnp.sum(jnp.where(chunk >= first_col, 1, 0), axis=0, keepdims=True) - 1
    at_img = img == iota((images, slots), 0)
    pos = slot - CE * jnp.sum(jnp.where(at_img, first_col, 0), axis=0, keepdims=True)
    negative = jnp.sum(jnp.where(at_img, neg_ref[...], 0), axis=0, keepdims=True)
    hit = (slot_of == slot) & (pos >= 2)
    pushed = jnp.sum(jnp.where(hit, number + 1, 0), axis=0, keepdims=True)
    used = (chunk < n_chunks) & ((pos < 2) | (pushed > 0))
    cap = jnp.where(pos == 0, base + img, jnp.where(pos == 1, negative, pushed - 1))
    local = digit(cap, 1, images)
    block = digit(cap, images, total)
    by_z = digit(block, NX * NC, NZ) - z
    by_x = digit(block, NC, NX) - x
    by_z = jnp.where(by_z < 0, by_z + NZ, by_z)
    by_x = jnp.where(by_x < 0, by_x + NX, by_x)
    gathered = local < GATHERED
    carried = (by_z * NX + by_x) * (images - GATHERED + 1) + local - GATHERED
    unit = jnp.where(gathered, block * GATHERED + local, carried)
    kind = jnp.where(gathered, 0, jnp.where(digit(block, 1, NC) == c, 1, 2))
    unit = jnp.where(used, unit, 0)
    kind = jnp.where(used, kind, -1)
    row = iota((8, slots), 0)
    lane = iota((images, slots), 0) == iota((images, slots), 1)
    start = jnp.sum(jnp.where(lane, first_col * CE, 0), axis=0, keepdims=True)
    count = jnp.sum(jnp.where(lane, count_col.astype(I32) + 2, 0), axis=0, keepdims=True)
    ints = n_chunks
    for at, values in enumerate((unit, img, pos, n_chunks, start, count, kind)):
        ints = jnp.where(row == at, values, ints)
    ints_out[...] = ints
    sign_out[...] = jnp.zeros_like(sign_out)
    sign_out[:, :slots] = jnp.where(used, jnp.where(pos == 0, -1.0, 1.0), 0.0)
    chips = total // images // NC
    half = digit(place, images * chips, NC)
    number = digit(place, images, chips) * NC + ahead(c, half, NC)
    number = number * images + digit(place, 1, images)
    home = (number == cap) & used & (pos >= 2)
    hit_out[...] = jnp.where(home, 1.0, 0.0).astype(BF16)


def blocks_of(ints):
    return lax.div(ints[3, 0] * CE + (SB - 1), SB)


def windows(ints, images, rows, act, extra_first):
    def extra():
        def one(img, carry):
            count = ints[5, img]

            def more(w, carry):
                at = pl.multiple_of((ints[4, img] + w * WIN) * rows, CE * rows)
                act(img, at, (count - w * WIN) * rows, False)
                return carry

            return lax.fori_loop(1, lax.div(count + (WIN - 1), WIN), more, carry)

        lax.fori_loop(0, images, one, 0)

    if extra_first:
        extra()
    for img in range(images):
        at = pl.multiple_of(ints[4, img] * rows, CE * rows)
        act(img, at, ints[5, img] * rows, True)
    if not extra_first:
        extra()


def block_rows(blk, size):
    return pl.ds(pl.multiple_of(blk * size, size), size)


def forward_kernel(
    ints, pool, carried, carried_other, wq_in, k_in, v_in, wo_in, const_ref, q_out, p_out, d_out, log_out,
    xbuf, wq, k, v, wo, q, p, half, mixed, d_res, logs, sem_x, sem_w, sem_o, *, head, scale,
):
    width = wo.shape[1]
    shards = wq.shape[0] // LANES
    heads = HEADS // shards
    cols = heads * head
    images = k.shape[0] // head
    rows = xbuf.shape[1] // 2
    size = SB * rows
    win = WIN * rows
    blocks = blocks_of(ints)
    weights = [
        pltpu.make_async_copy(src, dst, sem_w.at[j])
        for j, (src, dst) in enumerate(((wq_in, wq), (k_in, k), (v_in, v), (wo_in, wo)))
    ]
    for copy in weights:
        copy.start()

    def fetch(blk):
        def one(j, carry):
            slot = blk * SB + j
            for at, source in enumerate((pool, carried, carried_other)):

                @pl.when(ints[6, slot] == at)
                def _():
                    pltpu.make_async_copy(
                        source.at[ints[0, slot]], xbuf.at[slot], sem_x.at[blk]
                    ).start()

            return carry

        lax.fori_loop(0, SB, one, 0)

    def fetched(blk):
        def one(j, carry):
            slot = blk * SB + j

            @pl.when(ints[6, slot] >= 0)
            def _():
                pltpu.make_async_copy(pool.at[0], xbuf.at[slot], sem_x.at[blk]).wait()

            return carry

        lax.fori_loop(0, SB, one, 0)

    def results(blk, s):
        at = block_rows(blk, size)
        return [
            pltpu.make_async_copy(q.at[s, at], q_out.at[s, at], sem_o.at[0]),
            pltpu.make_async_copy(p.at[s, at], p_out.at[s, at], sem_o.at[1]),
        ]

    def gradient(blk):
        at = block_rows(blk, size)
        return pltpu.make_async_copy(d_res.at[at], d_out.at[at], sem_o.at[2])

    def loop(body):
        def one(blk, carry):
            body(blk)
            return carry

        lax.fori_loop(0, blocks, one, 0)

    xbuf[...] = jnp.zeros_like(xbuf)
    loop(fetch)
    weights[0].wait()

    def take(blk):
        x16 = xbuf[block_rows(blk, SB)].astype(F32)
        return jnp.concatenate([x16[:, :rows], x16[:, rows:]], axis=-1).reshape(size, width)

    def queries(blk):
        fetched(blk)
        got = (dot_nt(take(blk).astype(BF16), wq[...]) * scale).astype(BF16)
        for s in range(shards):
            q[s, block_rows(blk, size), :] = got[:, s * LANES : (s + 1) * LANES]

    loop(queries)
    weights[1].wait()

    def score(img, at, count, first):
        for s in range(shards):
            keys = k[pl.ds(img * head, head), s * LANES : (s + 1) * LANES]
            p[s, pl.ds(at, win), :cols] = dot_nt(
                q[s, pl.ds(at, win), :], head_blocks(keys, heads, head)
            )

    windows(ints, images, rows, score, True)

    def soften(blk):
        at = block_rows(blk, size)
        for s in range(shards):
            raised = jnp.exp(p[s, at, :cols])
            prob = raised / head_sum(raised, head)
            p[s, at, :cols] = prob
            half[s, at, :cols] = prob.astype(BF16)
            for copy in results(blk, s):
                copy.start()

    loop(soften)
    weights[2].wait()

    def mix(img, at, count, first):
        for s in range(shards):
            lanes = slice(s * LANES, (s + 1) * LANES)
            vals = head_blocks(v[pl.ds(img * head, head), lanes], heads, head)
            mixed[pl.ds(at, win), lanes] = dot(half[s, pl.ds(at, win), :cols], vals).astype(BF16)

    windows(ints, images, rows, mix, True)
    weights[3].wait()
    scaled = const_ref[1:2]
    flat = scaled - jnp.mean(scaled, axis=-1, keepdims=True)

    def finish(blk):
        at = block_rows(blk, size)
        residual = take(blk) + dot(mixed[at, :], wo[...])
        centred = residual - jnp.mean(residual, axis=-1, keepdims=True)
        variance = jnp.mean(centred * centred, axis=-1, keepdims=True)
        inverse = 1.0 / jnp.sqrt(variance + EPS)
        unit = centred * inverse
        none = jnp.sum(unit * const_ref[0:1], axis=-1, keepdims=True)
        gap = jnp.sum(unit * scaled, axis=-1, keepdims=True)
        both = jnp.where(iota((size, 128), 1) == 0, none, none + gap)
        logs[block_rows(blk, SB), :] = jnp.sum(both.reshape(SB, rows, 128), axis=1)
        d_res[at, :] = (inverse * (flat - unit * (gap / width))).astype(BF16)
        gradient(blk).start()

    loop(finish)
    log_out[...] = logs[...].T[: log_out.shape[0]]

    def settle(blk):
        for s in range(shards):
            for copy in results(blk, s):
                copy.wait()
        gradient(blk).wait()

    loop(settle)


def backward_kernel(
    ints, sign_ref, *rest, mine, arrivals, head, heads, rows, terms
):
    parts, rest = rest[:terms], rest[terms:]
    d_in, wo_in, v_in, p_in, q_in = rest[:5]
    arrived, rest = rest[5 : 5 + arrivals], rest[5 + arrivals :]
    outs, rest = rest[: len(mine)], rest[len(mine) :]
    d_res, wo, v, p, q, dm, d_att, ds, pd, acc, delta, sems = rest
    cols = heads * head
    images = v.shape[1] // head
    size = SB * rows
    win = WIN * rows
    blocks = blocks_of(ints)
    used = pl.ds(0, q.shape[1] - win)
    pltpu.make_async_copy(d_in, d_res, sems.at[0]).start()
    copies = []
    for j, shard in enumerate(mine):
        lanes = pl.ds(shard * LANES, LANES)
        copies.append(
            [
                pltpu.make_async_copy(src, dst, sems.at[1 + 4 * j + n])
                for n, (src, dst) in enumerate(
                    (
                        (wo_in.at[lanes, :], wo.at[j]),
                        (v_in.at[:, lanes], v.at[j]),
                        (p_in.at[shard], p.at[j]),
                        (q_in.at[shard], q.at[j, used]),
                    )
                )
            ]
        )
    for n in range(4):
        for group in copies:
            group[n].start()

    def loop(body):
        def one(blk, carry):
            body(blk)
            return carry

        lax.fori_loop(0, blocks, one, 0)

    def settle(n):
        for group in copies:
            group[n].wait()

    logits = sum(part[...] for part in parts[1:]) + parts[0][...]
    sign = sign_ref[...]
    factor = sign / (1.0 + jnp.exp(sign * (logits[0:1] - logits[1:2])))
    delta[...] = jnp.broadcast_to(factor, (128, factor.shape[1])).T
    tail = pl.ds(pl.multiple_of(blocks * size, size), win)
    for j in range(len(mine)):
        dm[j, tail, :] = jnp.zeros((win, LANES), BF16)
    pltpu.make_async_copy(d_in, d_res, sems.at[0]).wait()
    settle(0)

    def carry_back(blk):
        at = block_rows(blk, size)
        for j in range(len(mine)):
            dm[j, at, :] = dot_nt(d_res[at, :], wo[j]).astype(BF16)

    loop(carry_back)
    settle(1)

    def attend(img, at, count, first):
        for j in range(len(mine)):
            vals = head_blocks(v[j, pl.ds(img * head, head), :], heads, head)
            d_att[j, pl.ds(at, win), :cols] = dot_nt(dm[j, pl.ds(at, win), :], vals)

    windows(ints, images, rows, attend, True)
    settle(2)

    def soften(blk):
        at = block_rows(blk, size)
        weight = delta[block_rows(blk, SB), :]
        weight = jnp.broadcast_to(weight[:, None, :], (SB, rows, 128)).reshape(size, 128)[:, :1]
        for j in range(len(mine)):
            prob = p[j, at, :cols]
            grad = d_att[j, at, :cols]
            inner = head_sum(grad * prob, head)
            weighted = prob * weight
            ds[j, at, :cols] = (weighted * (grad - inner)).astype(BF16)
            pd[j, at, :cols] = weighted.astype(BF16)

    loop(soften)
    settle(3)
    for j in range(len(mine)):
        q[j, tail, :] = jnp.zeros((win, LANES), BF16)
    lane_head = iota((head, LANES), 1) // head
    place = iota((win, cols), 0)

    def diagonal(block):
        total = block[:head]
        for h in range(1, heads):
            total = jnp.where(lane_head == h, block[h * head : (h + 1) * head], total)
        return total[:, :cols]

    def outer(img, at, count, first):
        own = place < count
        here = pl.ds(at, win)
        zero = jnp.zeros((win, cols), BF16)
        for j in range(len(mine)):
            dk = diagonal(dot_tn(jnp.where(own, ds[j, here, :cols], zero), q[j, here, :]))
            dv = diagonal(dot_tn(jnp.where(own, pd[j, here, :cols], zero), dm[j, here, :]))
            term = jnp.concatenate([dk, dv], axis=-1)
            if first:
                acc[j, img * head : (img + 1) * head, :] = term
            else:
                acc[j, pl.ds(pl.multiple_of(img * head, head), head), :] += term

    windows(ints, images, rows, outer, False)
    for j, out_ref in enumerate(outs):
        total = acc[j]
        for a in arrived:
            total = total + a[...].astype(F32)
        out_ref[...] = total.astype(out_ref.dtype)


def whole(a):
    return pl.BlockSpec(a.shape, lambda *_: (0,) * a.ndim)


def local(
    images, query_states, neg_caption, neg_image, cross_query, cross_kv, cross_out, norm_gain,
    itm_weight,
):
    pair_count, patches, vis = images.shape
    queries, width = query_states.shape[1:]
    cols = cross_query.shape[1]
    head = width // HEADS
    scale = 1.0 / head**0.5
    groups = lax.axis_size("dp")
    shards = lax.axis_size("mp")
    dp, mp = lax.axis_index("dp"), lax.axis_index("mp")
    core = dp % NC
    rows = queries // shards
    half = width // 2

    def around(x, by):
        return lax.ppermute(x, "mp", [(i, (i + by) % shards) for i in range(shards)])

    def shift(x, by_z, by_x, by_core):
        moves = []
        for i in range(groups):
            z, x_, c = i // (NX * NC), i // NC % NX, i % NC
            to = ((z + by_z) % NZ * NX + (x_ + by_x) % NX) * NC + (c + by_core) % NC
            moves.append((i, to))
        return lax.ppermute(x, "dp", moves)

    own_rows = lax.dynamic_slice_in_dim(query_states, mp * rows, rows, 1)
    packed = jnp.concatenate([own_rows[:, :, :half], own_rows[:, :, half:]], axis=1)
    pool = lax.all_gather(packed[:GATHERED], "dp", axis=0, tiled=True)
    number = jnp.stack([neg_image // 32, neg_image % 32], axis=-1).astype(BF16)
    number = jnp.pad(number, ((0, 2 * rows - pair_count), (0, half - 2)))
    part = jnp.concatenate([packed[GATHERED:], number[None]], axis=0)
    units = part.shape[0]
    line = jnp.concatenate([part] + [shift(part, 0, -d, 0) for d in range(1, NX)], axis=0)
    up, down = [line], [line]
    for _ in range(NZ // 2 - 1):
        up.append(shift(up[-1], -1, 0, 0))
        down.append(shift(down[-1], 1, 0, 0))
    cut = NX // 2 * units
    across = [shift(up[-1][:cut], -1, 0, 0), shift(down[-1][cut:], 1, 0, 0)]
    carried = jnp.concatenate(up + across + down[:0:-1], axis=0)
    carried_other = shift(carried, 0, 0, 1)
    all_images = jnp.concatenate(
        [
            x[:, :, :2].reshape(-1, units, 2 * rows, 2)[:, -1, :pair_count]
            for x in (carried, carried_other)
        ],
        axis=0,
    ).reshape(groups * pair_count, 2)

    halves = [
        jnp.concatenate([cross_kv[0].T, cross_query.T], axis=1),
        jnp.concatenate([cross_kv[1].T, cross_out], axis=1),
    ]
    brought = jnp.where(core == 0, halves[0], halves[1])
    got = [around(brought, shards - s) for s in range(1, shards)]
    swap = [shift(g, 0, 0, 1) for g in got]
    padded = []
    for c in range(NC):
        pieces = [halves[c]] + [jnp.where(core == c, g, w) for g, w in zip(got, swap)]
        stacked = jnp.stack([jnp.pad(p, ((0, LANES - cols), (0, 0))) for p in pieces])
        padded.append(stacked.reshape(shards * LANES, vis + width))
    flat = images.reshape(pair_count * patches, vis)
    keys = dot_nt(flat, padded[0][:, :vis]).astype(BF16)
    values = dot_nt(flat, padded[1][:, :vis]).astype(BF16)
    wq, wo = padded[0][:, vis:], padded[1][:, vis:]

    out_rows = vis // groups
    pad_rows = (out_rows + 1 + 7) // 8 * 8
    feature = iota((vis, groups * pad_rows), 0)
    place = iota((vis, groups * pad_rows), 1)
    chips = groups // NC
    goal = place // pad_rows
    goal = goal % chips * NC + (goal // chips + core) % NC
    target = jnp.where(place % pad_rows < out_rows, goal * out_rows + place % pad_rows, -1)
    chosen = (feature == target).astype(BF16)
    spread = lax.dot_general(
        chosen, flat, (((0,), (1,)), ((), ())), preferred_element_type=F32
    ).astype(BF16)
    spread, keys = lax.optimization_barrier((spread, keys))

    most = pair_count * (2 + CE - 1) + 2 * groups
    n_slots = -(-(most + WIN - CE) // SB) * SB
    n_rows = n_slots * rows
    n_lanes = -(-n_slots // 128) * 128
    params = pltpu.CompilerParams(vmem_limit_bytes=56 * 2**20)
    ints, sign, hit = pl.pallas_call(
        plan_kernel,
        in_specs=[
            pl.BlockSpec(memory_space=pltpu.SMEM),
            pl.BlockSpec(memory_space=pltpu.VMEM),
            pl.BlockSpec(memory_space=pltpu.VMEM),
        ],
        out_specs=[pl.BlockSpec(memory_space=pltpu.VMEM)] * 3,
        out_shape=[
            jax.ShapeDtypeStruct((8, n_slots), I32),
            jax.ShapeDtypeStruct((1, n_lanes), F32),
            jax.ShapeDtypeStruct((groups * pair_count, n_slots), BF16),
        ],
        compiler_params=params,
        name="plan",
    )(dp.astype(I32).reshape(1), all_images, neg_caption.reshape(-1, 1))

    fold = norm_gain / queries
    const = jnp.stack([fold * itm_weight[:, 0], fold * (itm_weight[:, 1] - itm_weight[:, 0])])
    smem = pl.BlockSpec(memory_space=pltpu.SMEM)
    anywhere = pl.BlockSpec(memory_space=pl.ANY)
    vmem = pl.BlockSpec(memory_space=pltpu.VMEM)
    q_rows, prob, d_res, log_part = pl.pallas_call(
        functools.partial(forward_kernel, head=head, scale=scale),
        in_specs=[smem] + [anywhere] * 7 + [vmem],
        out_specs=[anywhere] * 3 + [vmem],
        scratch_shapes=[
            pltpu.VMEM((n_slots, 2 * rows, half), BF16),
            pltpu.VMEM(wq.shape, BF16),
            pltpu.VMEM(keys.shape, BF16),
            pltpu.VMEM(values.shape, BF16),
            pltpu.VMEM(wo.shape, BF16),
            pltpu.VMEM((shards, n_rows, LANES), BF16),
            pltpu.VMEM((shards, n_rows, LANES), F32),
            pltpu.VMEM((shards, n_rows, LANES), BF16),
            pltpu.VMEM((n_rows, shards * LANES), BF16),
            pltpu.VMEM((n_rows, width), BF16),
            pltpu.VMEM((n_lanes, 128), F32),
            pltpu.SemaphoreType.DMA((n_slots // SB,)),
            pltpu.SemaphoreType.DMA((4,)),
            pltpu.SemaphoreType.DMA((3,)),
        ],
        out_shape=[
            jax.ShapeDtypeStruct((shards, n_rows, LANES), BF16),
            jax.ShapeDtypeStruct((shards, n_rows, LANES), F32),
            jax.ShapeDtypeStruct((n_rows, width), BF16),
            jax.ShapeDtypeStruct((8, n_lanes), F32),
        ],
        compiler_params=params,
        name="forward",
    )(ints, pool, carried, carried_other, wq, keys, values, wo, const)

    parts = [log_part] + [around(log_part, shards - s) for s in range(1, shards)]
    logits = jnp.zeros((2, n_slots), F32)
    for m in range(shards):
        for s in range(shards):
            logits = logits + jnp.where((mp + s) % shards == m, parts[s][:2, :n_slots], 0.0)
    logits = jnp.where(sign[:, :n_slots] != 0.0, logits, 0.0)

    def backward(mine, arrived=(), kind=BF16):
        shape = (pair_count * patches, 2 * cols)
        slack = n_rows + WIN * rows
        n = len(mine)
        return pl.pallas_call(
            functools.partial(
                backward_kernel, mine=mine, arrivals=len(arrived), head=head,
                heads=HEADS // shards, rows=rows, terms=shards,
            ),
            in_specs=[smem] + [vmem] * (1 + shards) + [anywhere] * 5 + [vmem] * len(arrived),
            out_specs=[vmem] * n,
            scratch_shapes=[
                pltpu.VMEM((n_rows, width), BF16),
                pltpu.VMEM((n, LANES, width), BF16),
                pltpu.VMEM((n, pair_count * patches, LANES), BF16),
                pltpu.VMEM((n, n_rows, LANES), F32),
                pltpu.VMEM((n, slack, LANES), BF16),
                pltpu.VMEM((n, slack, LANES), BF16),
                pltpu.VMEM((n, slack, LANES), F32),
                pltpu.VMEM((n, slack, LANES), BF16),
                pltpu.VMEM((n, slack, LANES), BF16),
                pltpu.VMEM((n,) + shape, F32),
                pltpu.VMEM((n_lanes, 128), F32),
                pltpu.SemaphoreType.DMA((1 + 4 * n,)),
            ],
            out_shape=[jax.ShapeDtypeStruct(shape, kind)] * n,
            compiler_params=params,
            cost_estimate=pl.CostEstimate(flops=10**6, bytes_accessed=10**4, transcendentals=0),
            name="backward",
        )(ints, sign, *parts, d_res, wo, values, prob, q_rows, *arrived)

    two = around(backward((2,))[0], 2)
    one, three = backward((1, 3))
    one, three = around(one, 1), around(three, 3)
    own = backward((0,), (two,), F32)[0]
    d_kv = (own + one.astype(F32) + three.astype(F32)).astype(BF16)

    logit_hi = logits.astype(BF16)
    logit_lo = (logits - logit_hi.astype(F32)).astype(BF16)
    four = jnp.concatenate([logit_hi, logit_lo], axis=0)
    home = dot_nt(hit, four).astype(BF16)
    home = jnp.pad(
        home.reshape(groups, 1, 4 * pair_count),
        ((0, 0), (out_rows, pad_rows - out_rows - 1), (0, 2 * cols - 4 * pair_count)),
    )
    home, d_kv = lax.optimization_barrier((home, d_kv))
    grad = dot(spread, d_kv).reshape(groups, pad_rows, 2 * cols)
    over = shift((grad[chips:] + home[chips:]).astype(BF16), 0, 0, 1)
    leaving = (grad[:chips] + home[:chips] + over).astype(BF16)
    alike = [[chip * NC + c for chip in range(chips)] for c in range(NC)]
    arrived = lax.all_to_all(
        leaving, "dp", split_axis=0, concat_axis=0, tiled=True, axis_index_groups=alike
    )
    summed = jnp.sum(arrived.astype(F32), axis=0)
    grad_part = jnp.transpose(summed[:out_rows].reshape(out_rows, 2, cols), (1, 0, 2))
    back = summed[out_rows, : 4 * pair_count].reshape(pair_count, 2, 2)
    pushed_logits = back[:, 0] + back[:, 1]
    image = jnp.arange(pair_count, dtype=I32)[:, None]
    own_logits = []
    for j in range(2):
        here = ((ints[1:2] == image) & (ints[2:3] == j))[:, None, :]
        own_logits.append(jnp.sum(jnp.where(here, logits[None], 0.0), axis=-1))
    return (jnp.stack(own_logits + [pushed_logits]), grad_part)


def solution(mesh):
    return jax.shard_map(
        local,
        mesh=mesh,
        in_specs=(
            P("dp", None, None),
            P("dp", None, None),
            P("dp"),
            P("dp"),
            P(None, "mp"),
            P(None, None, "mp"),
            P("mp", None),
            P(),
            P(),
        ),
        out_specs=(P(None, "dp", None), P(None, "dp", "mp")),
        check_vma=False,
    )
```

```python
import functools

import jax
import jax.numpy as jnp
from jax import lax
from jax.experimental import pallas as pl
from jax.experimental.pallas import tpu as pltpu
from jax.sharding import PartitionSpec as P

HEADS = 12
EPS = 1e-06
CE = 2
SB = 32
WIN = 16
LANES = 256
NZ, NX, NC = 8, 4, 2
GATHERED = 12
BF16 = jnp.bfloat16
F32 = jnp.float32
I32 = jnp.int32


def dot(a, b):
    return jnp.dot(a, b, preferred_element_type=F32)


def dot_nt(a, b):
    return lax.dot_general(a, b, (((1,), (1,)), ((), ())), preferred_element_type=F32)


def dot_tn(a, b):
    return lax.dot_general(a, b, (((0,), (0,)), ((), ())), preferred_element_type=F32)


def iota(shape, axis):
    return lax.broadcasted_iota(I32, shape, axis)


def head_blocks(rows, heads, head):
    lane_head = iota(rows.shape, 1) // head
    zero = jnp.zeros_like(rows)
    return jnp.concatenate([jnp.where(lane_head == h, rows, zero) for h in range(heads)], axis=0)


def head_sum(values, head):
    width = values.shape[-1]
    same = iota((width, width), 0) // head == iota((width, width), 1) // head
    ones = jnp.where(same, 1.0, 0.0).astype(BF16)
    upper = values.astype(BF16)
    lower = (values - upper.astype(F32)).astype(BF16)
    return dot(upper, ones) + dot(lower, ones)


def plan_kernel(dp_ref, ids_ref, neg_ref, ints_out, sign_out, hit_out):
    total = ids_ref.shape[0]
    images = neg_ref.shape[0]
    slots = ints_out.shape[1]
    dp = dp_ref[0]
    z, x, c = lax.div(dp, NX * NC), lax.rem(lax.div(dp, NC), NX), lax.rem(dp, NC)
    base = dp * images
    place = iota((total, 1), 0)

    def digit(value, by, size):
        return lax.rem(lax.div(value, jnp.full_like(value, by)), jnp.full_like(value, size))

    def ahead(start, steps, size):
        to = start + steps
        return jnp.where(to >= size, to - size, to)

    block = ahead(z, digit(place, images * NX, NZ), NZ) * NX
    block = (block + ahead(x, digit(place, images, NX), NX)) * NC
    block = block + ahead(c, digit(place, images * NX * NZ, NC), NC)
    number = block * images + digit(place, 1, images)
    ids = ids_ref[...].astype(I32)
    ids = ids[:, :1] * 32 + ids[:, 1:]
    own = (ids - base) == iota((total, images), 1)
    ones = jnp.where(own, 1.0, 0.0)
    below = jnp.where(iota((128, 128), 0) >= iota((128, 128), 1), 1.0, 0.0).astype(BF16)
    count_row = jnp.zeros((1, images), F32)
    upto = []
    for j in range(total // 128):
        piece = ones[128 * j : 128 * (j + 1)]
        upto.append(dot(below, piece.astype(BF16)) + count_row)
        count_row = count_row + jnp.sum(piece, axis=0, keepdims=True)
    upto = jnp.concatenate(upto, axis=0)
    diagonal = iota((images, images), 0) == iota((images, images), 1)
    count_col = jnp.sum(jnp.where(diagonal, count_row, 0.0), axis=1, keepdims=True)

    def chunks_of(count):
        return lax.div(count.astype(I32) + (2 + CE - 1), jnp.full(count.shape, CE, I32))

    chunks_row, chunks_col = chunks_of(count_row), chunks_of(count_col)
    before = iota((images, images), 0) < iota((images, images), 1)
    after = iota((images, images), 0) > iota((images, images), 1)
    first_row = jnp.sum(jnp.where(before, chunks_col, 0), axis=0, keepdims=True)
    first_col = jnp.sum(jnp.where(after, chunks_row, 0), axis=1, keepdims=True)
    n_chunks = jnp.sum(chunks_row, axis=1, keepdims=True)
    slot_of = jnp.sum(
        jnp.where(own, (first_row * CE + 1).astype(F32) + upto, 0.0), axis=1, keepdims=True
    ).astype(I32)
    slot = iota((1, slots), 1)
    chunk = lax.div(slot, jnp.full(slot.shape, CE, I32))
    img = jnp.sum(jnp.where(chunk >= first_col, 1, 0), axis=0, keepdims=True) - 1
    at_img = img == iota((images, slots), 0)
    pos = slot - CE * jnp.sum(jnp.where(at_img, first_col, 0), axis=0, keepdims=True)
    negative = jnp.sum(jnp.where(at_img, neg_ref[...], 0), axis=0, keepdims=True)
    hit = (slot_of == slot) & (pos >= 2)
    pushed = jnp.sum(jnp.where(hit, number + 1, 0), axis=0, keepdims=True)
    used = (chunk < n_chunks) & ((pos < 2) | (pushed > 0))
    cap = jnp.where(pos == 0, base + img, jnp.where(pos == 1, negative, pushed - 1))
    local = digit(cap, 1, images)
    block = digit(cap, images, total)
    by_z = digit(block, NX * NC, NZ) - z
    by_x = digit(block, NC, NX) - x
    by_z = jnp.where(by_z < 0, by_z + NZ, by_z)
    by_x = jnp.where(by_x < 0, by_x + NX, by_x)
    gathered = local < GATHERED
    carried = (by_z * NX + by_x) * (images - GATHERED + 1) + local - GATHERED
    unit = jnp.where(gathered, block * GATHERED + local, carried)
    kind = jnp.where(gathered, 0, jnp.where(digit(block, 1, NC) == c, 1, 2))
    unit = jnp.where(used, unit, 0)
    kind = jnp.where(used, kind, 0)
    most = jnp.max(count_row, axis=1, keepdims=True).astype(I32) + 2
    row = iota((8, slots), 0)
    lane = iota((images, slots), 0) == iota((images, slots), 1)
    start = jnp.sum(jnp.where(lane, first_col * CE, 0), axis=0, keepdims=True)
    count = jnp.sum(jnp.where(lane, count_col.astype(I32) + 2, 0), axis=0, keepdims=True)
    ints = n_chunks
    for at, values in enumerate((unit, img, pos, n_chunks, start, count, kind, most)):
        ints = jnp.where(row == at, values, ints)
    ints_out[...] = ints
    sign_out[...] = jnp.zeros_like(sign_out)
    sign_out[:, :slots] = jnp.where(used, jnp.where(pos == 0, -1.0, 1.0), 0.0)
    chips = total // images // NC
    half = digit(place, images * chips, NC)
    number = digit(place, images, chips) * NC + ahead(c, half, NC)
    number = number * images + digit(place, 1, images)
    home = (number == cap) & used & (pos >= 2)
    hit_out[...] = jnp.where(home, 1.0, 0.0).astype(BF16)


def blocks_of(ints):
    return lax.div(ints[3, 0] * CE + (SB - 1), SB)


def windows(ints, images, rows, act, extra_first):
    def extra():
        def one(img, carry):
            count = ints[5, img]

            def more(w, carry):
                at = pl.multiple_of((ints[4, img] + w * WIN) * rows, CE * rows)
                act(img, at, (count - w * WIN) * rows, False)
                return carry

            return lax.fori_loop(1, lax.div(count + (WIN - 1), WIN), more, carry)

        @pl.when(ints[7, 0] > WIN)
        def _():
            lax.fori_loop(0, images, one, 0)

    if extra_first:
        extra()
    for img in range(images):
        at = pl.multiple_of(ints[4, img] * rows, CE * rows)
        act(img, at, ints[5, img] * rows, True)
    if not extra_first:
        extra()


def block_rows(blk, size):
    return pl.ds(pl.multiple_of(blk * size, size), size)


def project_kernel(
    core, flat_in, first_in, second_in, *rest, shards, cols, vis
):
    got, swap = rest[: shards - 1], rest[shards - 1 : 2 * shards - 2]
    k_out, v_out, wq_out, wo_out, flat, first, second, sems = rest[2 * shards - 2 :]
    count = flat.shape[0]
    side = core[0]
    pltpu.make_async_copy(flat_in, flat, sems.at[0]).start()
    own = pl.ds(0, cols)

    def landing(j, s):
        return (first, second)[j].at[s, own], sems.at[1 + 2 * s + j]

    for j, source in enumerate((first_in, second_in)):
        pltpu.make_async_copy(source, *landing(j, 0)).start()
    for s in range(1, shards):
        for j in range(NC):

            @pl.when(side == j)
            def _():
                pltpu.make_async_copy(got[s - 1], *landing(j, s)).start()

            @pl.when(side != j)
            def _():
                pltpu.make_async_copy(swap[s - 1], *landing(j, s)).start()

    pad = jnp.zeros((LANES - cols, first.shape[2]), BF16)
    for s in range(shards):
        first[s, cols:, :] = pad
        second[s, cols:, :] = pad
    pltpu.make_async_copy(flat_in, flat, sems.at[0]).wait()
    for s in range(shards):
        lanes = slice(s * LANES, (s + 1) * LANES)
        for j, (held, out, other) in enumerate(((first, k_out, wq_out), (second, v_out, wo_out))):
            pltpu.make_async_copy(first_in, *landing(j, s)).wait()
            other[lanes, :] = held[s, :, vis:]

            def part(n, carry):
                at = block_rows(n, 256)
                out[at, lanes] = dot_nt(flat[at, :], held[s, :, :vis]).astype(BF16)
                return carry

            lax.fori_loop(0, count // 256, part, 0)


def forward_kernel(
    ints, pool, carried, carried_other, wq_in, k_in, v_in, wo_in, const_ref, q_out, p_out, d_out, log_out,
    xbuf, wq, k, v, wo, q, p, half, mixed, d_res, logs, sem_x, sem_w, sem_o, *, head, scale,
):
    width = wo.shape[1]
    shards = wq.shape[0] // LANES
    heads = HEADS // shards
    cols = heads * head
    images = k.shape[0] // head
    rows = xbuf.shape[1] // 2
    size = SB * rows
    win = WIN * rows
    blocks = blocks_of(ints)
    weights = [
        pltpu.make_async_copy(src, dst, sem_w.at[j])
        for j, (src, dst) in enumerate(((wq_in, wq), (k_in, k), (v_in, v), (wo_in, wo)))
    ]
    for copy in weights:
        copy.start()

    def fetch(blk):
        def one(j, carry):
            slot = blk * SB + j
            for at, source in enumerate((pool, carried, carried_other)):

                @pl.when(ints[6, slot] == at)
                def _():
                    pltpu.make_async_copy(
                        source.at[ints[0, slot]], xbuf.at[slot], sem_x.at[blk]
                    ).start()

            return carry

        lax.fori_loop(0, SB, one, 0, unroll=4)

    def fetched(blk):
        here = xbuf.at[block_rows(blk, SB)]
        pltpu.make_async_copy(pool.at[pl.ds(0, SB)], here, sem_x.at[blk]).wait()

    def results(blk, s):
        at = block_rows(blk, size)
        return [
            pltpu.make_async_copy(q.at[s, at], q_out.at[s, at], sem_o.at[0]),
            pltpu.make_async_copy(p.at[s, at], p_out.at[s, at], sem_o.at[1]),
        ]

    def gradient(blk):
        at = block_rows(blk, size)
        return pltpu.make_async_copy(d_res.at[at], d_out.at[at], sem_o.at[2])

    def loop(body):
        def one(blk, carry):
            body(blk)
            return carry

        lax.fori_loop(0, blocks, one, 0)

    loop(fetch)
    weights[0].wait()

    def take(blk):
        x16 = xbuf[block_rows(blk, SB)].astype(F32)
        return jnp.concatenate([x16[:, :rows], x16[:, rows:]], axis=-1).reshape(size, width)

    def queries(blk):
        fetched(blk)
        got = (dot_nt(take(blk).astype(BF16), wq[...]) * scale).astype(BF16)
        for s in range(shards):
            q[s, block_rows(blk, size), :] = got[:, s * LANES : (s + 1) * LANES]

    loop(queries)
    weights[1].wait()

    def score(img, at, count, first):
        for s in range(shards):
            keys = k[pl.ds(img * head, head), s * LANES : (s + 1) * LANES]
            p[s, pl.ds(at, win), :cols] = dot_nt(
                q[s, pl.ds(at, win), :], head_blocks(keys, heads, head)
            )

    windows(ints, images, rows, score, True)

    def soften(blk):
        at = block_rows(blk, size)
        for s in range(shards):
            raised = jnp.exp(p[s, at, :cols])
            prob = raised / head_sum(raised, head)
            p[s, at, :cols] = prob
            half[s, at, :cols] = prob.astype(BF16)
            for copy in results(blk, s):
                copy.start()

    loop(soften)
    weights[2].wait()

    def mix(img, at, count, first):
        for s in range(shards):
            lanes = slice(s * LANES, (s + 1) * LANES)
            vals = head_blocks(v[pl.ds(img * head, head), lanes], heads, head)
            mixed[pl.ds(at, win), lanes] = dot(half[s, pl.ds(at, win), :cols], vals).astype(BF16)

    windows(ints, images, rows, mix, True)
    weights[3].wait()
    scaled = const_ref[1:2]
    flat = scaled - jnp.mean(scaled, axis=-1, keepdims=True)

    def finish(blk):
        at = block_rows(blk, size)
        residual = take(blk) + dot(mixed[at, :], wo[...])
        centred = residual - jnp.mean(residual, axis=-1, keepdims=True)
        variance = jnp.mean(centred * centred, axis=-1, keepdims=True)
        inverse = 1.0 / jnp.sqrt(variance + EPS)
        unit = centred * inverse
        none = jnp.sum(unit * const_ref[0:1], axis=-1, keepdims=True)
        gap = jnp.sum(unit * scaled, axis=-1, keepdims=True)
        both = jnp.where(iota((size, 128), 1) == 0, none, none + gap)
        logs[block_rows(blk, SB), :] = jnp.sum(both.reshape(SB, rows, 128), axis=1)
        d_res[at, :] = (inverse * (flat - unit * (gap / width))).astype(BF16)
        gradient(blk).start()

    loop(finish)
    log_out[...] = logs[...].T[: log_out.shape[0]]

    def settle(blk):
        for s in range(shards):
            for copy in results(blk, s):
                copy.wait()
        gradient(blk).wait()

    loop(settle)


def backward_kernel(
    ints, sign_ref, *rest, mine, arrivals, head, heads, rows, terms
):
    parts, rest = rest[:terms], rest[terms:]
    d_in, wo_in, v_in, p_in, q_in = rest[:5]
    arrived, rest = rest[5 : 5 + arrivals], rest[5 + arrivals :]
    outs, rest = rest[: len(mine)], rest[len(mine) :]
    d_res, wo, v, p, q, dm, d_att, ds, pd, acc, delta, sems = rest
    cols = heads * head
    images = v.shape[1] // head
    size = SB * rows
    win = WIN * rows
    blocks = blocks_of(ints)
    used = pl.ds(0, q.shape[1] - win)
    pltpu.make_async_copy(d_in, d_res, sems.at[0]).start()
    copies = []
    for j, shard in enumerate(mine):
        lanes = pl.ds(shard * LANES, LANES)
        copies.append(
            [
                pltpu.make_async_copy(src, dst, sems.at[1 + 4 * j + n])
                for n, (src, dst) in enumerate(
                    (
                        (wo_in.at[lanes, :], wo.at[j]),
                        (v_in.at[:, lanes], v.at[j]),
                        (p_in.at[shard], p.at[j]),
                        (q_in.at[shard], q.at[j, used]),
                    )
                )
            ]
        )
    for n in range(4):
        for group in copies:
            group[n].start()

    def loop(body):
        def one(blk, carry):
            body(blk)
            return carry

        lax.fori_loop(0, blocks, one, 0)

    def settle(n):
        for group in copies:
            group[n].wait()

    logits = sum(part[...] for part in parts[1:]) + parts[0][...]
    sign = sign_ref[...]
    factor = sign / (1.0 + jnp.exp(sign * (logits[0:1] - logits[1:2])))
    delta[...] = jnp.broadcast_to(factor, (128, factor.shape[1])).T
    tail = pl.ds(pl.multiple_of(blocks * size, size), win)
    for j in range(len(mine)):
        dm[j, tail, :] = jnp.zeros((win, LANES), BF16)
    pltpu.make_async_copy(d_in, d_res, sems.at[0]).wait()
    settle(0)

    def carry_back(blk):
        at = block_rows(blk, size)
        for j in range(len(mine)):
            dm[j, at, :] = dot_nt(d_res[at, :], wo[j]).astype(BF16)

    loop(carry_back)
    settle(1)

    def attend(img, at, count, first):
        for j in range(len(mine)):
            vals = head_blocks(v[j, pl.ds(img * head, head), :], heads, head)
            d_att[j, pl.ds(at, win), :cols] = dot_nt(dm[j, pl.ds(at, win), :], vals)

    windows(ints, images, rows, attend, True)
    settle(2)

    def soften(blk):
        at = block_rows(blk, size)
        weight = delta[block_rows(blk, SB), :]
        weight = jnp.broadcast_to(weight[:, None, :], (SB, rows, 128)).reshape(size, 128)[:, :1]
        for j in range(len(mine)):
            prob = p[j, at, :cols]
            grad = d_att[j, at, :cols]
            inner = head_sum(grad * prob, head)
            weighted = prob * weight
            ds[j, at, :cols] = (weighted * (grad - inner)).astype(BF16)
            pd[j, at, :cols] = weighted.astype(BF16)

    loop(soften)
    settle(3)
    for j in range(len(mine)):
        q[j, tail, :] = jnp.zeros((win, LANES), BF16)
    lane_head = iota((head, LANES), 1) // head
    place = iota((win, cols), 0)

    def diagonal(block):
        total = block[:head]
        for h in range(1, heads):
            total = jnp.where(lane_head == h, block[h * head : (h + 1) * head], total)
        return total[:, :cols]

    def outer(img, at, count, first):
        own = place < count
        here = pl.ds(at, win)
        zero = jnp.zeros((win, cols), BF16)
        for j in range(len(mine)):
            dk = diagonal(dot_tn(jnp.where(own, ds[j, here, :cols], zero), q[j, here, :]))
            dv = diagonal(dot_tn(jnp.where(own, pd[j, here, :cols], zero), dm[j, here, :]))
            term = jnp.concatenate([dk, dv], axis=-1)
            if first:
                acc[j, img * head : (img + 1) * head, :] = term
            else:
                acc[j, pl.ds(pl.multiple_of(img * head, head), head), :] += term

    windows(ints, images, rows, outer, False)
    for j, out_ref in enumerate(outs):
        total = acc[j]
        for a in arrived:
            total = total + a[...].astype(F32)
        out_ref[...] = total.astype(out_ref.dtype)


def whole(a):
    return pl.BlockSpec(a.shape, lambda *_: (0,) * a.ndim)


def local(
    images, query_states, neg_caption, neg_image, cross_query, cross_kv, cross_out, norm_gain,
    itm_weight,
):
    pair_count, patches, vis = images.shape
    queries, width = query_states.shape[1:]
    cols = cross_query.shape[1]
    head = width // HEADS
    scale = 1.0 / head**0.5
    groups = lax.axis_size("dp")
    shards = lax.axis_size("mp")
    dp, mp = lax.axis_index("dp"), lax.axis_index("mp")
    core = dp % NC
    rows = queries // shards
    half = width // 2

    def around(x, by):
        return lax.ppermute(x, "mp", [(i, (i + by) % shards) for i in range(shards)])

    def shift(x, by_z, by_x, by_core):
        moves = []
        for i in range(groups):
            z, x_, c = i // (NX * NC), i // NC % NX, i % NC
            to = ((z + by_z) % NZ * NX + (x_ + by_x) % NX) * NC + (c + by_core) % NC
            moves.append((i, to))
        return lax.ppermute(x, "dp", moves)

    own_rows = lax.dynamic_slice_in_dim(query_states, mp * rows, rows, 1)
    packed = jnp.concatenate([own_rows[:, :, :half], own_rows[:, :, half:]], axis=1)
    pool = lax.all_gather(packed[:GATHERED], "dp", axis=0, tiled=True)
    number = jnp.stack([neg_image // 32, neg_image % 32], axis=-1).astype(BF16)
    number = jnp.pad(number, ((0, 2 * rows - pair_count), (0, half - 2)))
    part = jnp.concatenate([packed[GATHERED:], number[None]], axis=0)
    units = part.shape[0]
    line = jnp.concatenate([part] + [shift(part, 0, -d, 0) for d in range(1, NX)], axis=0)
    up, down = [line], [line]
    for _ in range(NZ // 2 - 1):
        up.append(shift(up[-1], -1, 0, 0))
        down.append(shift(down[-1], 1, 0, 0))
    cut = NX // 2 * units
    across = [shift(up[-1][:cut], -1, 0, 0), shift(down[-1][cut:], 1, 0, 0)]
    carried = jnp.concatenate(up + across + down[:0:-1], axis=0)
    carried_other = shift(carried, 0, 0, 1)
    all_images = jnp.concatenate(
        [
            x[:, :, :2].reshape(-1, units, 2 * rows, 2)[:, -1, :pair_count]
            for x in (carried, carried_other)
        ],
        axis=0,
    ).reshape(groups * pair_count, 2)

    halves = [
        jnp.concatenate([cross_kv[0].T, cross_query.T], axis=1),
        jnp.concatenate([cross_kv[1].T, cross_out], axis=1),
    ]
    brought = jnp.where(core == 0, halves[0], halves[1])
    got = [around(brought, shards - s) for s in range(1, shards)]
    swap = [shift(g, 0, 0, 1) for g in got]
    flat = images.reshape(pair_count * patches, vis)
    params = pltpu.CompilerParams(vmem_limit_bytes=56 * 2**20)
    smem = pl.BlockSpec(memory_space=pltpu.SMEM)
    anywhere = pl.BlockSpec(memory_space=pl.ANY)
    vmem = pl.BlockSpec(memory_space=pltpu.VMEM)
    tall = shards * LANES
    keys, values, wq, wo = pl.pallas_call(
        functools.partial(project_kernel, shards=shards, cols=cols, vis=vis),
        in_specs=[smem] + [anywhere] * (1 + 2 * shards),
        out_specs=[vmem] * 4,
        scratch_shapes=[
            pltpu.VMEM(flat.shape, BF16),
            pltpu.VMEM((shards, LANES, vis + width), BF16),
            pltpu.VMEM((shards, LANES, vis + width), BF16),
            pltpu.SemaphoreType.DMA((1 + 2 * shards,)),
        ],
        out_shape=[
            jax.ShapeDtypeStruct((pair_count * patches, tall), BF16),
            jax.ShapeDtypeStruct((pair_count * patches, tall), BF16),
            jax.ShapeDtypeStruct((tall, width), BF16),
            jax.ShapeDtypeStruct((tall, width), BF16),
        ],
        compiler_params=params,
        name="project",
    )(core.astype(I32).reshape(1), flat, *halves, *got, *swap)

    most = pair_count * (2 + CE - 1) + 2 * groups
    n_slots = -(-(most + WIN - CE) // SB) * SB
    n_rows = n_slots * rows
    n_lanes = -(-n_slots // 128) * 128
    ints, sign, hit = pl.pallas_call(
        plan_kernel,
        in_specs=[
            pl.BlockSpec(memory_space=pltpu.SMEM),
            pl.BlockSpec(memory_space=pltpu.VMEM),
            pl.BlockSpec(memory_space=pltpu.VMEM),
        ],
        out_specs=[pl.BlockSpec(memory_space=pltpu.VMEM)] * 3,
        out_shape=[
            jax.ShapeDtypeStruct((8, n_slots), I32),
            jax.ShapeDtypeStruct((1, n_lanes), F32),
            jax.ShapeDtypeStruct((groups * pair_count, n_slots), BF16),
        ],
        compiler_params=params,
        name="plan",
    )(dp.astype(I32).reshape(1), all_images, neg_caption.reshape(-1, 1))

    fold = norm_gain / queries
    const = jnp.stack([fold * itm_weight[:, 0], fold * (itm_weight[:, 1] - itm_weight[:, 0])])
    q_rows, prob, d_res, log_part = pl.pallas_call(
        functools.partial(forward_kernel, head=head, scale=scale),
        in_specs=[smem] + [anywhere] * 7 + [vmem],
        out_specs=[anywhere] * 3 + [vmem],
        scratch_shapes=[
            pltpu.VMEM((n_slots, 2 * rows, half), BF16),
            pltpu.VMEM(wq.shape, BF16),
            pltpu.VMEM(keys.shape, BF16),
            pltpu.VMEM(values.shape, BF16),
            pltpu.VMEM(wo.shape, BF16),
            pltpu.VMEM((shards, n_rows, LANES), BF16),
            pltpu.VMEM((shards, n_rows, LANES), F32),
            pltpu.VMEM((shards, n_rows, LANES), BF16),
            pltpu.VMEM((n_rows, shards * LANES), BF16),
            pltpu.VMEM((n_rows, width), BF16),
            pltpu.VMEM((n_lanes, 128), F32),
            pltpu.SemaphoreType.DMA((n_slots // SB,)),
            pltpu.SemaphoreType.DMA((4,)),
            pltpu.SemaphoreType.DMA((3,)),
        ],
        out_shape=[
            jax.ShapeDtypeStruct((shards, n_rows, LANES), BF16),
            jax.ShapeDtypeStruct((shards, n_rows, LANES), F32),
            jax.ShapeDtypeStruct((n_rows, width), BF16),
            jax.ShapeDtypeStruct((8, n_lanes), F32),
        ],
        compiler_params=params,
        name="forward",
    )(ints, pool, carried, carried_other, wq, keys, values, wo, const)

    late, log_part = lax.optimization_barrier((flat, log_part))
    out_rows = vis // groups
    pad_rows = (out_rows + 1 + 7) // 8 * 8
    feature = iota((vis, groups * pad_rows), 0)
    place = iota((vis, groups * pad_rows), 1)
    chips = groups // NC
    goal = place // pad_rows
    goal = goal % chips * NC + (goal // chips + core) % NC
    target = jnp.where(place % pad_rows < out_rows, goal * out_rows + place % pad_rows, -1)
    chosen = (feature == target).astype(BF16)
    spread = lax.dot_general(
        chosen, late, (((0,), (1,)), ((), ())), preferred_element_type=F32
    ).astype(BF16)

    parts = [log_part] + [around(log_part, shards - s) for s in range(1, shards)]
    spread, parts[-1] = lax.optimization_barrier((spread, parts[-1]))
    logits = jnp.zeros((2, n_slots), F32)
    for m in range(shards):
        for s in range(shards):
            logits = logits + jnp.where((mp + s) % shards == m, parts[s][:2, :n_slots], 0.0)
    logits = jnp.where(sign[:, :n_slots] != 0.0, logits, 0.0)

    def backward(mine, arrived=(), kind=BF16):
        shape = (pair_count * patches, 2 * cols)
        slack = n_rows + WIN * rows
        n = len(mine)
        return pl.pallas_call(
            functools.partial(
                backward_kernel, mine=mine, arrivals=len(arrived), head=head,
                heads=HEADS // shards, rows=rows, terms=shards,
            ),
            in_specs=[smem] + [vmem] * (1 + shards) + [anywhere] * 5 + [vmem] * len(arrived),
            out_specs=[vmem] * n,
            scratch_shapes=[
                pltpu.VMEM((n_rows, width), BF16),
                pltpu.VMEM((n, LANES, width), BF16),
                pltpu.VMEM((n, pair_count * patches, LANES), BF16),
                pltpu.VMEM((n, n_rows, LANES), F32),
                pltpu.VMEM((n, slack, LANES), BF16),
                pltpu.VMEM((n, slack, LANES), BF16),
                pltpu.VMEM((n, slack, LANES), F32),
                pltpu.VMEM((n, slack, LANES), BF16),
                pltpu.VMEM((n, slack, LANES), BF16),
                pltpu.VMEM((n,) + shape, F32),
                pltpu.VMEM((n_lanes, 128), F32),
                pltpu.SemaphoreType.DMA((1 + 4 * n,)),
            ],
            out_shape=[jax.ShapeDtypeStruct(shape, kind)] * n,
            compiler_params=params,
            cost_estimate=pl.CostEstimate(flops=10**6, bytes_accessed=10**4, transcendentals=0),
            name="backward",
        )(ints, sign, *parts, d_res, wo, values, prob, q_rows, *arrived)

    two = around(backward((2,))[0], 2)
    one, three = backward((1, 3))
    one, three = around(one, 1), around(three, 3)
    own = backward((0,), (two,), F32)[0]
    d_kv = (own + one.astype(F32) + three.astype(F32)).astype(BF16)

    logit_hi = logits.astype(BF16)
    logit_lo = (logits - logit_hi.astype(F32)).astype(BF16)
    four = jnp.concatenate([logit_hi, logit_lo], axis=0)
    home = dot_nt(hit, four).astype(BF16)
    home = jnp.pad(
        home.reshape(groups, 1, 4 * pair_count),
        ((0, 0), (out_rows, pad_rows - out_rows - 1), (0, 2 * cols - 4 * pair_count)),
    )
    home, d_kv = lax.optimization_barrier((home, d_kv))
    grad = dot(spread, d_kv).reshape(groups, pad_rows, 2 * cols)
    over = shift((grad[chips:] + home[chips:]).astype(BF16), 0, 0, 1)
    leaving = (grad[:chips] + home[:chips] + over).astype(BF16)
    alike = [[chip * NC + c for chip in range(chips)] for c in range(NC)]
    arrived = lax.all_to_all(
        leaving, "dp", split_axis=0, concat_axis=0, tiled=True, axis_index_groups=alike
    )
    summed = jnp.sum(arrived.astype(F32), axis=0)
    grad_part = jnp.transpose(summed[:out_rows].reshape(out_rows, 2, cols), (1, 0, 2))
    back = summed[out_rows, : 4 * pair_count].reshape(pair_count, 2, 2)
    pushed_logits = back[:, 0] + back[:, 1]
    image = jnp.arange(pair_count, dtype=I32)[:, None]
    own_logits = []
    for j in range(2):
        here = ((ints[1:2] == image) & (ints[2:3] == j))[:, None, :]
        own_logits.append(jnp.sum(jnp.where(here, logits[None], 0.0), axis=-1))
    return (jnp.stack(own_logits + [pushed_logits]), grad_part)


def solution(mesh):
    return jax.shard_map(
        local,
        mesh=mesh,
        in_specs=(
            P("dp", None, None),
            P("dp", None, None),
            P("dp"),
            P("dp"),
            P(None, "mp"),
            P(None, None, "mp"),
            P("mp", None),
            P(),
            P(),
        ),
        out_specs=(P(None, "dp", None), P(None, "dp", "mp")),
        check_vma=False,
    )
```

```python
import functools

import jax
import jax.numpy as jnp
from jax import lax
from jax.experimental import pallas as pl
from jax.experimental.pallas import tpu as pltpu
from jax.sharding import PartitionSpec as P

HEADS = 12
EPS = 1e-06
CE = 2
SB = 32
WIN = 16
LANES = 256
NZ, NX, NC = 8, 4, 2
GATHERED = 11
BF16 = jnp.bfloat16
F32 = jnp.float32
I32 = jnp.int32


def dot(a, b):
    return jnp.dot(a, b, preferred_element_type=F32)


def dot_nt(a, b):
    return lax.dot_general(a, b, (((1,), (1,)), ((), ())), preferred_element_type=F32)


def dot_tn(a, b):
    return lax.dot_general(a, b, (((0,), (0,)), ((), ())), preferred_element_type=F32)


def iota(shape, axis):
    return lax.broadcasted_iota(I32, shape, axis)


def head_blocks(rows, heads, head):
    lane_head = iota(rows.shape, 1) // head
    zero = jnp.zeros_like(rows)
    return jnp.concatenate([jnp.where(lane_head == h, rows, zero) for h in range(heads)], axis=0)


def head_sum(values, head):
    width = values.shape[-1]
    same = iota((width, width), 0) // head == iota((width, width), 1) // head
    ones = jnp.where(same, 1.0, 0.0).astype(BF16)
    upper = values.astype(BF16)
    lower = (values - upper.astype(F32)).astype(BF16)
    return dot(upper, ones) + dot(lower, ones)


def plan_kernel(dp_ref, ids_ref, neg_ref, ints_out, sign_out, hit_out):
    total = ids_ref.shape[0]
    images = neg_ref.shape[0]
    slots = ints_out.shape[1]
    dp = dp_ref[0]
    z, x, c = lax.div(dp, NX * NC), lax.rem(lax.div(dp, NC), NX), lax.rem(dp, NC)
    base = dp * images
    place = iota((total, 1), 0)

    def digit(value, by, size):
        return lax.rem(lax.div(value, jnp.full_like(value, by)), jnp.full_like(value, size))

    def ahead(start, steps, size):
        to = start + steps
        return jnp.where(to >= size, to - size, to)

    block = ahead(z, digit(place, images * NX, NZ), NZ) * NX
    block = (block + ahead(x, digit(place, images, NX), NX)) * NC
    block = block + ahead(c, digit(place, images * NX * NZ, NC), NC)
    number = block * images + digit(place, 1, images)
    ids = ids_ref[...].astype(I32)
    ids = ids[:, :1] * 32 + ids[:, 1:]
    own = (ids - base) == iota((total, images), 1)
    ones = jnp.where(own, 1.0, 0.0)
    below = jnp.where(iota((128, 128), 0) >= iota((128, 128), 1), 1.0, 0.0).astype(BF16)
    count_row = jnp.zeros((1, images), F32)
    upto = []
    for j in range(total // 128):
        piece = ones[128 * j : 128 * (j + 1)]
        upto.append(dot(below, piece.astype(BF16)) + count_row)
        count_row = count_row + jnp.sum(piece, axis=0, keepdims=True)
    upto = jnp.concatenate(upto, axis=0)
    diagonal = iota((images, images), 0) == iota((images, images), 1)
    count_col = jnp.sum(jnp.where(diagonal, count_row, 0.0), axis=1, keepdims=True)

    def chunks_of(count):
        return lax.div(count.astype(I32) + (2 + CE - 1), jnp.full(count.shape, CE, I32))

    chunks_row, chunks_col = chunks_of(count_row), chunks_of(count_col)
    before = iota((images, images), 0) < iota((images, images), 1)
    after = iota((images, images), 0) > iota((images, images), 1)
    first_row = jnp.sum(jnp.where(before, chunks_col, 0), axis=0, keepdims=True)
    first_col = jnp.sum(jnp.where(after, chunks_row, 0), axis=1, keepdims=True)
    n_chunks = jnp.sum(chunks_row, axis=1, keepdims=True)
    slot_of = jnp.sum(
        jnp.where(own, (first_row * CE + 1).astype(F32) + upto, 0.0), axis=1, keepdims=True
    ).astype(I32)
    slot = iota((1, slots), 1)
    chunk = lax.div(slot, jnp.full(slot.shape, CE, I32))
    img = jnp.sum(jnp.where(chunk >= first_col, 1, 0), axis=0, keepdims=True) - 1
    at_img = img == iota((images, slots), 0)
    pos = slot - CE * jnp.sum(jnp.where(at_img, first_col, 0), axis=0, keepdims=True)
    negative = jnp.sum(jnp.where(at_img, neg_ref[...], 0), axis=0, keepdims=True)
    hit = (slot_of == slot) & (pos >= 2)
    pushed = jnp.sum(jnp.where(hit, number + 1, 0), axis=0, keepdims=True)
    used = (chunk < n_chunks) & ((pos < 2) | (pushed > 0))
    cap = jnp.where(pos == 0, base + img, jnp.where(pos == 1, negative, pushed - 1))
    local = digit(cap, 1, images)
    block = digit(cap, images, total)
    by_z = digit(block, NX * NC, NZ) - z
    by_x = digit(block, NC, NX) - x
    by_z = jnp.where(by_z < 0, by_z + NZ, by_z)
    by_x = jnp.where(by_x < 0, by_x + NX, by_x)
    gathered = local < GATHERED
    carried = (by_z * NX + by_x) * (images - GATHERED + 1) + local - GATHERED
    unit = jnp.where(gathered, block * GATHERED + local, carried)
    kind = jnp.where(gathered, 0, jnp.where(digit(block, 1, NC) == c, 1, 2))
    unit = jnp.where(used, unit, 0)
    kind = jnp.where(used, kind, 0)
    most = jnp.max(count_row, axis=1, keepdims=True).astype(I32) + 2
    row = iota((8, slots), 0)
    lane = iota((images, slots), 0) == iota((images, slots), 1)
    start = jnp.sum(jnp.where(lane, first_col * CE, 0), axis=0, keepdims=True)
    count = jnp.sum(jnp.where(lane, count_col.astype(I32) + 2, 0), axis=0, keepdims=True)
    ints = n_chunks
    for at, values in enumerate((unit, img, pos, n_chunks, start, count, kind, most)):
        ints = jnp.where(row == at, values, ints)
    ints_out[...] = ints
    sign_out[...] = jnp.zeros_like(sign_out)
    sign_out[:, :slots] = jnp.where(used, jnp.where(pos == 0, -1.0, 1.0), 0.0)
    chips = total // images // NC
    half = digit(place, images * chips, NC)
    number = digit(place, images, chips) * NC + ahead(c, half, NC)
    number = number * images + digit(place, 1, images)
    home = (number == cap) & used & (pos >= 2)
    hit_out[...] = jnp.where(home, 1.0, 0.0).astype(BF16)


def blocks_of(ints):
    return lax.div(ints[3, 0] * CE + (SB - 1), SB)


def windows(ints, images, rows, act, extra_first):
    def extra():
        def one(img, carry):
            count = ints[5, img]

            def more(w, carry):
                at = pl.multiple_of((ints[4, img] + w * WIN) * rows, CE * rows)
                act(img, at, (count - w * WIN) * rows, False)
                return carry

            return lax.fori_loop(1, lax.div(count + (WIN - 1), WIN), more, carry)

        @pl.when(ints[7, 0] > WIN)
        def _():
            lax.fori_loop(0, images, one, 0)

    if extra_first:
        extra()
    for img in range(images):
        at = pl.multiple_of(ints[4, img] * rows, CE * rows)
        act(img, at, ints[5, img] * rows, True)
    if not extra_first:
        extra()


def block_rows(blk, size):
    return pl.ds(pl.multiple_of(blk * size, size), size)


def project_kernel(
    core, flat_in, first_in, second_in, *rest, shards, cols, vis
):
    got, swap = rest[: shards - 1], rest[shards - 1 : 2 * shards - 2]
    k_out, v_out, wq_out, wo_out, flat, first, second, sems = rest[2 * shards - 2 :]
    count = flat.shape[0]
    side = core[0]
    pltpu.make_async_copy(flat_in, flat, sems.at[0]).start()
    own = pl.ds(0, cols)

    def landing(j, s):
        return (first, second)[j].at[s, own], sems.at[1 + 2 * s + j]

    for j, source in enumerate((first_in, second_in)):
        pltpu.make_async_copy(source, *landing(j, 0)).start()
    for s in range(1, shards):
        for j in range(NC):

            @pl.when(side == j)
            def _():
                pltpu.make_async_copy(got[s - 1], *landing(j, s)).start()

            @pl.when(side != j)
            def _():
                pltpu.make_async_copy(swap[s - 1], *landing(j, s)).start()

    pad = jnp.zeros((LANES - cols, first.shape[2]), BF16)
    for s in range(shards):
        first[s, cols:, :] = pad
        second[s, cols:, :] = pad
    pltpu.make_async_copy(flat_in, flat, sems.at[0]).wait()
    for s in range(shards):
        lanes = slice(s * LANES, (s + 1) * LANES)
        for j, (held, out, other) in enumerate(((first, k_out, wq_out), (second, v_out, wo_out))):
            pltpu.make_async_copy(first_in, *landing(j, s)).wait()
            other[lanes, :] = held[s, :, vis:]

            for n in range(0, count, 512):
                out[n : n + 512, lanes] = dot_nt(flat[n : n + 512], held[s, :, :vis]).astype(BF16)


def forward_kernel(
    ints, pool, carried, carried_other, wq_in, k_in, v_in, wo_in, const_ref, q_out, p_out, d_out, log_out,
    xbuf, wq, k, v, wo, q, p, half, mixed, d_res, logs, sem_x, sem_w, sem_o, *, head, scale,
):
    width = wo.shape[1]
    shards = wq.shape[0] // LANES
    heads = HEADS // shards
    cols = heads * head
    images = k.shape[0] // head
    rows = xbuf.shape[1] // 2
    size = SB * rows
    win = WIN * rows
    blocks = blocks_of(ints)
    weights = [
        pltpu.make_async_copy(src, dst, sem_w.at[j])
        for j, (src, dst) in enumerate(((wq_in, wq), (k_in, k), (v_in, v), (wo_in, wo)))
    ]
    for copy in weights:
        copy.start()

    def fetch(blk):
        def one(j, carry):
            slot = blk * SB + j
            for at, source in enumerate((pool, carried, carried_other)):

                @pl.when(ints[6, slot] == at)
                def _():
                    pltpu.make_async_copy(
                        source.at[ints[0, slot]], xbuf.at[slot], sem_x.at[blk]
                    ).start()

            return carry

        lax.fori_loop(0, SB, one, 0, unroll=4)

    def fetched(blk):
        here = xbuf.at[block_rows(blk, SB)]
        pltpu.make_async_copy(pool.at[pl.ds(0, SB)], here, sem_x.at[blk]).wait()

    def results(blk, s):
        at = block_rows(blk, size)
        return [
            pltpu.make_async_copy(q.at[s, at], q_out.at[s, at], sem_o.at[0]),
            pltpu.make_async_copy(p.at[s, at], p_out.at[s, at], sem_o.at[1]),
        ]

    def gradient(blk):
        at = block_rows(blk, size)
        return pltpu.make_async_copy(d_res.at[at], d_out.at[at], sem_o.at[2])

    def loop(body):
        def one(blk, carry):
            body(blk)
            return carry

        lax.fori_loop(0, blocks, one, 0)

    loop(fetch)
    weights[0].wait()

    def take(blk):
        x16 = xbuf[block_rows(blk, SB)].astype(F32)
        return jnp.concatenate([x16[:, :rows], x16[:, rows:]], axis=-1).reshape(size, width)

    def queries(blk):
        fetched(blk)
        got = (dot_nt(take(blk).astype(BF16), wq[...]) * scale).astype(BF16)
        for s in range(shards):
            q[s, block_rows(blk, size), :] = got[:, s * LANES : (s + 1) * LANES]

    loop(queries)
    weights[1].wait()

    def score(img, at, count, first):
        for s in range(shards):
            keys = k[pl.ds(img * head, head), s * LANES : (s + 1) * LANES]
            p[s, pl.ds(at, win), :cols] = dot_nt(
                q[s, pl.ds(at, win), :], head_blocks(keys, heads, head)
            )

    windows(ints, images, rows, score, True)

    def soften(blk):
        at = block_rows(blk, size)
        for s in range(shards):
            raised = jnp.exp(p[s, at, :cols])
            prob = raised / head_sum(raised, head)
            p[s, at, :cols] = prob
            half[s, at, :cols] = prob.astype(BF16)
            for copy in results(blk, s):
                copy.start()

    loop(soften)
    weights[2].wait()

    def mix(img, at, count, first):
        for s in range(shards):
            lanes = slice(s * LANES, (s + 1) * LANES)
            vals = head_blocks(v[pl.ds(img * head, head), lanes], heads, head)
            mixed[pl.ds(at, win), lanes] = dot(half[s, pl.ds(at, win), :cols], vals).astype(BF16)

    windows(ints, images, rows, mix, True)
    weights[3].wait()
    scaled = const_ref[1:2]
    flat = scaled - jnp.mean(scaled, axis=-1, keepdims=True)

    def finish(blk):
        at = block_rows(blk, size)
        residual = take(blk) + dot(mixed[at, :], wo[...])
        centred = residual - jnp.mean(residual, axis=-1, keepdims=True)
        variance = jnp.mean(centred * centred, axis=-1, keepdims=True)
        inverse = 1.0 / jnp.sqrt(variance + EPS)
        unit = centred * inverse
        none = jnp.sum(unit * const_ref[0:1], axis=-1, keepdims=True)
        gap = jnp.sum(unit * scaled, axis=-1, keepdims=True)
        both = jnp.where(iota((size, 128), 1) == 0, none, none + gap)
        logs[block_rows(blk, SB), :] = jnp.sum(both.reshape(SB, rows, 128), axis=1)
        d_res[at, :] = (inverse * (flat - unit * (gap / width))).astype(BF16)
        gradient(blk).start()

    loop(finish)
    log_out[...] = logs[...].T[: log_out.shape[0]]

    def settle(blk):
        for s in range(shards):
            for copy in results(blk, s):
                copy.wait()
        gradient(blk).wait()

    loop(settle)


def backward_kernel(
    ints, sign_ref, *rest, mine, arrivals, head, heads, rows, terms
):
    parts, rest = rest[:terms], rest[terms:]
    d_in, wo_in, v_in, p_in, q_in = rest[:5]
    arrived, rest = rest[5 : 5 + arrivals], rest[5 + arrivals :]
    outs, rest = rest[: len(mine)], rest[len(mine) :]
    d_res, wo, v, p, q, dm, d_att, ds, pd, acc, delta, sems = rest
    cols = heads * head
    images = v.shape[1] // head
    size = SB * rows
    win = WIN * rows
    blocks = blocks_of(ints)
    used = pl.ds(0, q.shape[1] - win)
    pltpu.make_async_copy(d_in, d_res, sems.at[0]).start()
    copies = []
    for j, shard in enumerate(mine):
        lanes = pl.ds(shard * LANES, LANES)
        copies.append(
            [
                pltpu.make_async_copy(src, dst, sems.at[1 + 4 * j + n])
                for n, (src, dst) in enumerate(
                    (
                        (wo_in.at[lanes, :], wo.at[j]),
                        (v_in.at[:, lanes], v.at[j]),
                        (p_in.at[shard], p.at[j]),
                        (q_in.at[shard], q.at[j, used]),
                    )
                )
            ]
        )
    for n in range(4):
        for group in copies:
            group[n].start()

    def loop(body):
        def one(blk, carry):
            body(blk)
            return carry

        lax.fori_loop(0, blocks, one, 0)

    def settle(n):
        for group in copies:
            group[n].wait()

    logits = sum(part[...] for part in parts[1:]) + parts[0][...]
    sign = sign_ref[...]
    factor = sign / (1.0 + jnp.exp(sign * (logits[0:1] - logits[1:2])))
    delta[...] = jnp.broadcast_to(factor, (128, factor.shape[1])).T
    tail = pl.ds(pl.multiple_of(blocks * size, size), win)
    for j in range(len(mine)):
        dm[j, tail, :] = jnp.zeros((win, LANES), BF16)
    pltpu.make_async_copy(d_in, d_res, sems.at[0]).wait()
    settle(0)

    def carry_back(blk):
        at = block_rows(blk, size)
        for j in range(len(mine)):
            dm[j, at, :] = dot_nt(d_res[at, :], wo[j]).astype(BF16)

    loop(carry_back)
    settle(1)

    def attend(img, at, count, first):
        for j in range(len(mine)):
            vals = head_blocks(v[j, pl.ds(img * head, head), :], heads, head)
            d_att[j, pl.ds(at, win), :cols] = dot_nt(dm[j, pl.ds(at, win), :], vals)

    windows(ints, images, rows, attend, True)
    settle(2)

    def soften(blk):
        at = block_rows(blk, size)
        weight = delta[block_rows(blk, SB), :]
        weight = jnp.broadcast_to(weight[:, None, :], (SB, rows, 128)).reshape(size, 128)[:, :1]
        for j in range(len(mine)):
            prob = p[j, at, :cols]
            grad = d_att[j, at, :cols]
            inner = head_sum(grad * prob, head)
            weighted = prob * weight
            ds[j, at, :cols] = (weighted * (grad - inner)).astype(BF16)
            pd[j, at, :cols] = weighted.astype(BF16)

    loop(soften)
    settle(3)
    for j in range(len(mine)):
        q[j, tail, :] = jnp.zeros((win, LANES), BF16)
    lane_head = iota((head, LANES), 1) // head
    place = iota((win, cols), 0)

    def diagonal(block):
        total = block[:head]
        for h in range(1, heads):
            total = jnp.where(lane_head == h, block[h * head : (h + 1) * head], total)
        return total[:, :cols]

    def outer(img, at, count, first):
        own = place < count
        here = pl.ds(at, win)
        zero = jnp.zeros((win, cols), BF16)
        for j in range(len(mine)):
            dk = diagonal(dot_tn(jnp.where(own, ds[j, here, :cols], zero), q[j, here, :]))
            dv = diagonal(dot_tn(jnp.where(own, pd[j, here, :cols], zero), dm[j, here, :]))
            term = jnp.concatenate([dk, dv], axis=-1)
            if first:
                acc[j, img * head : (img + 1) * head, :] = term
            else:
                acc[j, pl.ds(pl.multiple_of(img * head, head), head), :] += term

    windows(ints, images, rows, outer, False)
    for j, out_ref in enumerate(outs):
        total = acc[j]
        for a in arrived:
            total = total + a[...].astype(F32)
        out_ref[...] = total.astype(out_ref.dtype)


def whole(a):
    return pl.BlockSpec(a.shape, lambda *_: (0,) * a.ndim)


def local(
    images, query_states, neg_caption, neg_image, cross_query, cross_kv, cross_out, norm_gain,
    itm_weight,
):
    pair_count, patches, vis = images.shape
    queries, width = query_states.shape[1:]
    cols = cross_query.shape[1]
    head = width // HEADS
    scale = 1.0 / head**0.5
    groups = lax.axis_size("dp")
    shards = lax.axis_size("mp")
    dp, mp = lax.axis_index("dp"), lax.axis_index("mp")
    core = dp % NC
    rows = queries // shards
    half = width // 2

    def around(x, by):
        return lax.ppermute(x, "mp", [(i, (i + by) % shards) for i in range(shards)])

    def shift(x, by_z, by_x, by_core):
        moves = []
        for i in range(groups):
            z, x_, c = i // (NX * NC), i // NC % NX, i % NC
            to = ((z + by_z) % NZ * NX + (x_ + by_x) % NX) * NC + (c + by_core) % NC
            moves.append((i, to))
        return lax.ppermute(x, "dp", moves)

    own_rows = lax.dynamic_slice_in_dim(query_states, mp * rows, rows, 1)
    packed = jnp.concatenate([own_rows[:, :, :half], own_rows[:, :, half:]], axis=1)
    pool = lax.all_gather(packed[:GATHERED], "dp", axis=0, tiled=True)
    number = jnp.stack([neg_image // 32, neg_image % 32], axis=-1).astype(BF16)
    number = jnp.pad(number, ((0, 2 * rows - pair_count), (0, half - 2)))
    part = jnp.concatenate([packed[GATHERED:], number[None]], axis=0)
    units = part.shape[0]
    line = jnp.concatenate([part] + [shift(part, 0, -d, 0) for d in range(1, NX)], axis=0)
    up, down = [line], [line]
    for _ in range(NZ // 2 - 1):
        up.append(shift(up[-1], -1, 0, 0))
        down.append(shift(down[-1], 1, 0, 0))
    cut = NX // 2 * units
    across = [shift(up[-1][:cut], -1, 0, 0), shift(down[-1][cut:], 1, 0, 0)]
    carried = jnp.concatenate(up + across + down[:0:-1], axis=0)
    carried_other = shift(carried, 0, 0, 1)
    all_images = jnp.concatenate(
        [
            x[:, :, :2].reshape(-1, units, 2 * rows, 2)[:, -1, :pair_count]
            for x in (carried, carried_other)
        ],
        axis=0,
    ).reshape(groups * pair_count, 2)

    halves = [
        jnp.concatenate([cross_kv[0].T, cross_query.T], axis=1),
        jnp.concatenate([cross_kv[1].T, cross_out], axis=1),
    ]
    brought = jnp.where(core == 0, halves[0], halves[1])
    got = [around(brought, shards - s) for s in range(1, shards)]
    swap = [shift(g, 0, 0, 1) for g in got]
    flat = images.reshape(pair_count * patches, vis)
    params = pltpu.CompilerParams(vmem_limit_bytes=56 * 2**20)
    smem = pl.BlockSpec(memory_space=pltpu.SMEM)
    anywhere = pl.BlockSpec(memory_space=pl.ANY)
    vmem = pl.BlockSpec(memory_space=pltpu.VMEM)
    tall = shards * LANES
    keys, values, wq, wo = pl.pallas_call(
        functools.partial(project_kernel, shards=shards, cols=cols, vis=vis),
        in_specs=[smem] + [anywhere] * (1 + 2 * shards),
        out_specs=[vmem] * 4,
        scratch_shapes=[
            pltpu.VMEM(flat.shape, BF16),
            pltpu.VMEM((shards, LANES, vis + width), BF16),
            pltpu.VMEM((shards, LANES, vis + width), BF16),
            pltpu.SemaphoreType.DMA((1 + 2 * shards,)),
        ],
        out_shape=[
            jax.ShapeDtypeStruct((pair_count * patches, tall), BF16),
            jax.ShapeDtypeStruct((pair_count * patches, tall), BF16),
            jax.ShapeDtypeStruct((tall, width), BF16),
            jax.ShapeDtypeStruct((tall, width), BF16),
        ],
        compiler_params=params,
        cost_estimate=pl.CostEstimate(
            flops=4 * 10**10, bytes_accessed=20 * 10**6, transcendentals=0
        ),
        name="project",
    )(core.astype(I32).reshape(1), flat, *halves, *got, *swap)

    out_rows = vis // groups
    pad_rows = (out_rows + 1 + 7) // 8 * 8
    feature = iota((vis, groups * pad_rows), 0)
    place = iota((vis, groups * pad_rows), 1)
    chips = groups // NC
    goal = place // pad_rows
    goal = goal % chips * NC + (goal // chips + core) % NC
    target = jnp.where(place % pad_rows < out_rows, goal * out_rows + place % pad_rows, -1)
    chosen = (feature == target).astype(BF16)
    spread = lax.dot_general(
        chosen, flat, (((0,), (1,)), ((), ())), preferred_element_type=F32
    ).astype(BF16)
    spread, keys = lax.optimization_barrier((spread, keys))

    most = pair_count * (2 + CE - 1) + 2 * groups
    n_slots = -(-(most + WIN - CE) // SB) * SB
    n_rows = n_slots * rows
    n_lanes = -(-n_slots // 128) * 128
    ints, sign, hit = pl.pallas_call(
        plan_kernel,
        in_specs=[
            pl.BlockSpec(memory_space=pltpu.SMEM),
            pl.BlockSpec(memory_space=pltpu.VMEM),
            pl.BlockSpec(memory_space=pltpu.VMEM),
        ],
        out_specs=[pl.BlockSpec(memory_space=pltpu.VMEM)] * 3,
        out_shape=[
            jax.ShapeDtypeStruct((8, n_slots), I32),
            jax.ShapeDtypeStruct((1, n_lanes), F32),
            jax.ShapeDtypeStruct((groups * pair_count, n_slots), BF16),
        ],
        compiler_params=params,
        name="plan",
    )(dp.astype(I32).reshape(1), all_images, neg_caption.reshape(-1, 1))

    fold = norm_gain / queries
    const = jnp.stack([fold * itm_weight[:, 0], fold * (itm_weight[:, 1] - itm_weight[:, 0])])
    q_rows, prob, d_res, log_part = pl.pallas_call(
        functools.partial(forward_kernel, head=head, scale=scale),
        in_specs=[smem] + [anywhere] * 7 + [vmem],
        out_specs=[anywhere] * 3 + [vmem],
        scratch_shapes=[
            pltpu.VMEM((n_slots, 2 * rows, half), BF16),
            pltpu.VMEM(wq.shape, BF16),
            pltpu.VMEM(keys.shape, BF16),
            pltpu.VMEM(values.shape, BF16),
            pltpu.VMEM(wo.shape, BF16),
            pltpu.VMEM((shards, n_rows, LANES), BF16),
            pltpu.VMEM((shards, n_rows, LANES), F32),
            pltpu.VMEM((shards, n_rows, LANES), BF16),
            pltpu.VMEM((n_rows, shards * LANES), BF16),
            pltpu.VMEM((n_rows, width), BF16),
            pltpu.VMEM((n_lanes, 128), F32),
            pltpu.SemaphoreType.DMA((n_slots // SB,)),
            pltpu.SemaphoreType.DMA((4,)),
            pltpu.SemaphoreType.DMA((3,)),
        ],
        out_shape=[
            jax.ShapeDtypeStruct((shards, n_rows, LANES), BF16),
            jax.ShapeDtypeStruct((shards, n_rows, LANES), F32),
            jax.ShapeDtypeStruct((n_rows, width), BF16),
            jax.ShapeDtypeStruct((8, n_lanes), F32),
        ],
        compiler_params=params,
        name="forward",
    )(ints, pool, carried, carried_other, wq, keys, values, wo, const)

    parts = [log_part] + [around(log_part, shards - s) for s in range(1, shards)]
    logits = jnp.zeros((2, n_slots), F32)
    for m in range(shards):
        for s in range(shards):
            logits = logits + jnp.where((mp + s) % shards == m, parts[s][:2, :n_slots], 0.0)
    logits = jnp.where(sign[:, :n_slots] != 0.0, logits, 0.0)

    def backward(mine, arrived=(), kind=BF16):
        shape = (pair_count * patches, 2 * cols)
        slack = n_rows + WIN * rows
        n = len(mine)
        return pl.pallas_call(
            functools.partial(
                backward_kernel, mine=mine, arrivals=len(arrived), head=head,
                heads=HEADS // shards, rows=rows, terms=shards,
            ),
            in_specs=[smem] + [vmem] * (1 + shards) + [anywhere] * 5 + [vmem] * len(arrived),
            out_specs=[vmem] * n,
            scratch_shapes=[
                pltpu.VMEM((n_rows, width), BF16),
                pltpu.VMEM((n, LANES, width), BF16),
                pltpu.VMEM((n, pair_count * patches, LANES), BF16),
                pltpu.VMEM((n, n_rows, LANES), F32),
                pltpu.VMEM((n, slack, LANES), BF16),
                pltpu.VMEM((n, slack, LANES), BF16),
                pltpu.VMEM((n, slack, LANES), F32),
                pltpu.VMEM((n, slack, LANES), BF16),
                pltpu.VMEM((n, slack, LANES), BF16),
                pltpu.VMEM((n,) + shape, F32),
                pltpu.VMEM((n_lanes, 128), F32),
                pltpu.SemaphoreType.DMA((1 + 4 * n,)),
            ],
            out_shape=[jax.ShapeDtypeStruct(shape, kind)] * n,
            compiler_params=params,
            cost_estimate=pl.CostEstimate(flops=10**6, bytes_accessed=10**4, transcendentals=0),
            name="backward",
        )(ints, sign, *parts, d_res, wo, values, prob, q_rows, *arrived)

    two = around(backward((2,))[0], 2)
    one, three = backward((1, 3))
    one, three = around(one, 1), around(three, 3)
    own = backward((0,), (two,), F32)[0]
    d_kv = (own + one.astype(F32) + three.astype(F32)).astype(BF16)

    logit_hi = logits.astype(BF16)
    logit_lo = (logits - logit_hi.astype(F32)).astype(BF16)
    four = jnp.concatenate([logit_hi, logit_lo], axis=0)
    home = dot_nt(hit, four).astype(BF16)
    home = jnp.pad(
        home.reshape(groups, 1, 4 * pair_count),
        ((0, 0), (out_rows, pad_rows - out_rows - 1), (0, 2 * cols - 4 * pair_count)),
    )
    home, d_kv = lax.optimization_barrier((home, d_kv))
    grad = dot(spread, d_kv).reshape(groups, pad_rows, 2 * cols)
    over = shift((grad[chips:] + home[chips:]).astype(BF16), 0, 0, 1)
    leaving = (grad[:chips] + home[:chips] + over).astype(BF16)
    alike = [[chip * NC + c for chip in range(chips)] for c in range(NC)]
    arrived = lax.all_to_all(
        leaving, "dp", split_axis=0, concat_axis=0, tiled=True, axis_index_groups=alike
    )
    summed = jnp.sum(arrived.astype(F32), axis=0)
    grad_part = jnp.transpose(summed[:out_rows].reshape(out_rows, 2, cols), (1, 0, 2))
    back = summed[out_rows, : 4 * pair_count].reshape(pair_count, 2, 2)
    pushed_logits = back[:, 0] + back[:, 1]
    image = jnp.arange(pair_count, dtype=I32)[:, None]
    own_logits = []
    for j in range(2):
        here = ((ints[1:2] == image) & (ints[2:3] == j))[:, None, :]
        own_logits.append(jnp.sum(jnp.where(here, logits[None], 0.0), axis=-1))
    return (jnp.stack(own_logits + [pushed_logits]), grad_part)


def solution(mesh):
    return jax.shard_map(
        local,
        mesh=mesh,
        in_specs=(
            P("dp", None, None),
            P("dp", None, None),
            P("dp"),
            P("dp"),
            P(None, "mp"),
            P(None, None, "mp"),
            P("mp", None),
            P(),
            P(),
        ),
        out_specs=(P(None, "dp", None), P(None, "dp", "mp")),
        check_vma=False,
    )
```

```python
import functools

import jax
import jax.numpy as jnp
from jax import lax
from jax.experimental import pallas as pl
from jax.experimental.pallas import tpu as pltpu
from jax.sharding import PartitionSpec as P

HEADS = 12
EPS = 1e-06
CE = 2
SB = 32
WIN = 16
LANES = 256
NZ, NX, NC = 8, 4, 2
GATHERED = 10
BF16 = jnp.bfloat16
F32 = jnp.float32
I32 = jnp.int32


def dot(a, b):
    return jnp.dot(a, b, preferred_element_type=F32)


def dot_nt(a, b):
    return lax.dot_general(a, b, (((1,), (1,)), ((), ())), preferred_element_type=F32)


def dot_tn(a, b):
    return lax.dot_general(a, b, (((0,), (0,)), ((), ())), preferred_element_type=F32)


def iota(shape, axis):
    return lax.broadcasted_iota(I32, shape, axis)


def head_blocks(rows, heads, head):
    lane_head = iota(rows.shape, 1) // head
    zero = jnp.zeros_like(rows)
    return jnp.concatenate([jnp.where(lane_head == h, rows, zero) for h in range(heads)], axis=0)


def head_sum(values, head):
    width = values.shape[-1]
    same = iota((width, width), 0) // head == iota((width, width), 1) // head
    ones = jnp.where(same, 1.0, 0.0).astype(BF16)
    upper = values.astype(BF16)
    lower = (values - upper.astype(F32)).astype(BF16)
    return dot(upper, ones) + dot(lower, ones)


def plan_kernel(dp_ref, mine_in, other_in, neg_ref, ints_out, sign_out, hit_out, held, sems):
    images = neg_ref.shape[0]
    copies = [
        pltpu.make_async_copy(
            source.at[:, source.shape[1] - 1, :, pl.ds(0, 128)], held.at[j], sems.at[j]
        )
        for j, source in enumerate((mine_in, other_in))
    ]
    for copy in copies:
        copy.start()
    total = hit_out.shape[0]
    slots = ints_out.shape[1]
    dp = dp_ref[0]
    z, x, c = lax.div(dp, NX * NC), lax.rem(lax.div(dp, NC), NX), lax.rem(dp, NC)
    base = dp * images
    place = iota((total, 1), 0)

    def digit(value, by, size):
        return lax.rem(lax.div(value, jnp.full_like(value, by)), jnp.full_like(value, size))

    def ahead(start, steps, size):
        to = start + steps
        return jnp.where(to >= size, to - size, to)

    block = ahead(z, digit(place, images * NX, NZ), NZ) * NX
    block = (block + ahead(x, digit(place, images, NX), NX)) * NC
    block = block + ahead(c, digit(place, images * NX * NZ, NC), NC)
    number = block * images + digit(place, 1, images)
    for copy in copies:
        copy.wait()
    ids = held[...].astype(F32).reshape(total, 128)
    ids = (ids[:, :1] * 32 + ids[:, 1:2]).astype(I32)
    own = (ids - base) == iota((total, images), 1)
    ones = jnp.where(own, 1.0, 0.0)
    below = jnp.where(iota((128, 128), 0) >= iota((128, 128), 1), 1.0, 0.0).astype(BF16)
    count_row = jnp.zeros((1, images), F32)
    upto = []
    for j in range(total // 128):
        piece = ones[128 * j : 128 * (j + 1)]
        upto.append(dot(below, piece.astype(BF16)) + count_row)
        count_row = count_row + jnp.sum(piece, axis=0, keepdims=True)
    upto = jnp.concatenate(upto, axis=0)
    diagonal = iota((images, images), 0) == iota((images, images), 1)
    count_col = jnp.sum(jnp.where(diagonal, count_row, 0.0), axis=1, keepdims=True)

    def chunks_of(count):
        return lax.div(count.astype(I32) + (2 + CE - 1), jnp.full(count.shape, CE, I32))

    chunks_row, chunks_col = chunks_of(count_row), chunks_of(count_col)
    before = iota((images, images), 0) < iota((images, images), 1)
    after = iota((images, images), 0) > iota((images, images), 1)
    first_row = jnp.sum(jnp.where(before, chunks_col, 0), axis=0, keepdims=True)
    first_col = jnp.sum(jnp.where(after, chunks_row, 0), axis=1, keepdims=True)
    n_chunks = jnp.sum(chunks_row, axis=1, keepdims=True)
    slot_of = jnp.sum(
        jnp.where(own, (first_row * CE + 1).astype(F32) + upto, 0.0), axis=1, keepdims=True
    ).astype(I32)
    slot = iota((1, slots), 1)
    chunk = lax.div(slot, jnp.full(slot.shape, CE, I32))
    img = jnp.sum(jnp.where(chunk >= first_col, 1, 0), axis=0, keepdims=True) - 1
    at_img = img == iota((images, slots), 0)
    pos = slot - CE * jnp.sum(jnp.where(at_img, first_col, 0), axis=0, keepdims=True)
    negative = jnp.sum(jnp.where(at_img, neg_ref[...], 0), axis=0, keepdims=True)
    hit = (slot_of == slot) & (pos >= 2)
    pushed = jnp.sum(jnp.where(hit, number + 1, 0), axis=0, keepdims=True)
    used = (chunk < n_chunks) & ((pos < 2) | (pushed > 0))
    cap = jnp.where(pos == 0, base + img, jnp.where(pos == 1, negative, pushed - 1))
    local = digit(cap, 1, images)
    block = digit(cap, images, total)
    by_z = digit(block, NX * NC, NZ) - z
    by_x = digit(block, NC, NX) - x
    by_z = jnp.where(by_z < 0, by_z + NZ, by_z)
    by_x = jnp.where(by_x < 0, by_x + NX, by_x)
    gathered = local < GATHERED
    carried = (by_z * NX + by_x) * (images - GATHERED + 1) + local - GATHERED
    unit = jnp.where(gathered, block * GATHERED + local, carried)
    kind = jnp.where(gathered, 0, jnp.where(digit(block, 1, NC) == c, 1, 2))
    unit = jnp.where(used, unit, 0)
    kind = jnp.where(used, kind, 0)
    most = jnp.max(count_row, axis=1, keepdims=True).astype(I32) + 2
    row = iota((8, slots), 0)
    lane = iota((images, slots), 0) == iota((images, slots), 1)
    start = jnp.sum(jnp.where(lane, first_col * CE, 0), axis=0, keepdims=True)
    count = jnp.sum(jnp.where(lane, count_col.astype(I32) + 2, 0), axis=0, keepdims=True)
    ints = n_chunks
    for at, values in enumerate((unit, img, pos, n_chunks, start, count, kind, most)):
        ints = jnp.where(row == at, values, ints)
    ints_out[...] = ints
    sign_out[...] = jnp.zeros_like(sign_out)
    sign_out[:, :slots] = jnp.where(used, jnp.where(pos == 0, -1.0, 1.0), 0.0)
    chips = total // images // NC
    half = digit(place, images * chips, NC)
    number = digit(place, images, chips) * NC + ahead(c, half, NC)
    number = number * images + digit(place, 1, images)
    home = (number == cap) & used & (pos >= 2)
    hit_out[...] = jnp.where(home, 1.0, 0.0).astype(BF16)


def blocks_of(ints):
    return lax.div(ints[3, 0] * CE + (SB - 1), SB)


def windows(ints, images, rows, act, extra_first):
    def extra():
        def one(img, carry):
            count = ints[5, img]

            def more(w, carry):
                at = pl.multiple_of((ints[4, img] + w * WIN) * rows, CE * rows)
                act(img, at, (count - w * WIN) * rows, False)
                return carry

            return lax.fori_loop(1, lax.div(count + (WIN - 1), WIN), more, carry)

        @pl.when(ints[7, 0] > WIN)
        def _():
            lax.fori_loop(0, images, one, 0)

    if extra_first:
        extra()
    for img in range(images):
        at = pl.multiple_of(ints[4, img] * rows, CE * rows)
        act(img, at, ints[5, img] * rows, True)
    if not extra_first:
        extra()


def block_rows(blk, size):
    return pl.ds(pl.multiple_of(blk * size, size), size)


def project_kernel(core, flat_in, first_in, second_in, *rest, shards, cols, vis, out_rows):
    got, swap = rest[: shards - 1], rest[shards - 1 : 2 * shards - 2]
    k_out, v_out, wq_out, wo_out, spread_out = rest[2 * shards - 2 : 2 * shards + 3]
    flat, first, second, k, v, spread, sems, sem_o = rest[2 * shards + 3 :]
    count = flat.shape[0]
    side = core[0]
    pltpu.make_async_copy(flat_in, flat, sems.at[0]).start()
    own = pl.ds(0, cols)

    def landing(j, s):
        return (first, second)[j].at[s, own], sems.at[1 + 2 * s + j]

    for j, source in enumerate((first_in, second_in)):
        pltpu.make_async_copy(source, *landing(j, 0)).start()
    for s in range(1, shards):
        for j in range(NC):

            @pl.when(side == j)
            def _():
                pltpu.make_async_copy(got[s - 1], *landing(j, s)).start()

            @pl.when(side != j)
            def _():
                pltpu.make_async_copy(swap[s - 1], *landing(j, s)).start()

    pad = jnp.zeros((LANES - cols, first.shape[2]), BF16)
    for s in range(shards):
        first[s, cols:, :] = pad
        second[s, cols:, :] = pad
    pltpu.make_async_copy(flat_in, flat, sems.at[0]).wait()
    leaving = []

    def leave(source, target):
        copy = pltpu.make_async_copy(source, target, sem_o.at[len(leaving)])
        copy.start()
        leaving.append(copy)

    step = vis // NZ
    slot = spread.shape[0] // (NZ * NX * NC)
    half = spread.shape[0] // NC
    for z in range(NZ):
        low = step * z // 128 * 128
        window = -(-(step * z + step - low) // 128) * 128
        row, lane = iota((NX * NC * slot, window), 0), iota((NX * NC * slot, window), 1)
        inner = row % slot
        kind = (row // (NX * slot) + side) % NC
        goal = (row // slot % NX * NC + kind) * out_rows + inner + (step * z - low)
        chosen = jnp.where((lane == goal) & (inner < out_rows), 1.0, 0.0).astype(BF16)
        moved = dot_nt(chosen, flat[:, low : low + window]).astype(BF16)
        for c in range(NC):
            part = slice(c * half + z * NX * slot, c * half + (z + 1) * NX * slot)
            spread[part, :] = moved[c * NX * slot : (c + 1) * NX * slot]
    leave(spread, spread_out)
    for s in range(shards):
        lanes = slice(s * LANES, (s + 1) * LANES)
        for j, (held, kept, out, other) in enumerate(
            ((first, k, k_out, wq_out), (second, v, v_out, wo_out))
        ):
            pltpu.make_async_copy(first_in, *landing(j, s)).wait()
            leave(held.at[s, :, pl.ds(vis, held.shape[2] - vis)], other.at[pl.ds(s * LANES, LANES)])
            for n in range(0, count, 512):
                kept[n : n + 512, lanes] = dot_nt(flat[n : n + 512], held[s, :, :vis]).astype(BF16)
            leave(kept.at[:, pl.ds(s * LANES, LANES)], out.at[:, pl.ds(s * LANES, LANES)])
    for copy in leaving:
        copy.wait()


def forward_kernel(
    ints, pool, carried, carried_other, wq_in, k_in, v_in, wo_in, const_ref, q_out, p_out, d_out, log_out,
    xbuf, wq, k, v, wo, q, p, half, mixed, d_res, logs, sem_x, sem_w, sem_o, *, head, scale,
):
    width = wo.shape[1]
    shards = wq.shape[0] // LANES
    heads = HEADS // shards
    cols = heads * head
    images = k.shape[0] // head
    rows = xbuf.shape[1] // 2
    size = SB * rows
    win = WIN * rows
    blocks = blocks_of(ints)
    weights = [
        pltpu.make_async_copy(src, dst, sem_w.at[j])
        for j, (src, dst) in enumerate(((wq_in, wq), (k_in, k), (v_in, v), (wo_in, wo)))
    ]
    for copy in weights:
        copy.start()

    def fetch(blk):
        def one(j, carry):
            slot = blk * SB + j
            for at, source in enumerate((pool, carried, carried_other)):

                @pl.when(ints[6, slot] == at)
                def _():
                    pltpu.make_async_copy(
                        source.at[ints[0, slot]], xbuf.at[slot], sem_x.at[blk]
                    ).start()

            return carry

        lax.fori_loop(0, SB, one, 0, unroll=4)

    def fetched(blk):
        here = xbuf.at[block_rows(blk, SB)]
        pltpu.make_async_copy(pool.at[pl.ds(0, SB)], here, sem_x.at[blk]).wait()

    def results(blk, s):
        at = block_rows(blk, size)
        return [
            pltpu.make_async_copy(q.at[s, at], q_out.at[s, at], sem_o.at[0]),
            pltpu.make_async_copy(p.at[s, at], p_out.at[s, at], sem_o.at[1]),
        ]

    def gradient(blk):
        at = block_rows(blk, size)
        return pltpu.make_async_copy(d_res.at[at], d_out.at[at], sem_o.at[2])

    def loop(body):
        def one(blk, carry):
            body(blk)
            return carry

        lax.fori_loop(0, blocks, one, 0)

    loop(fetch)
    weights[0].wait()

    def take(blk):
        x16 = xbuf[block_rows(blk, SB)].astype(F32)
        return jnp.concatenate([x16[:, :rows], x16[:, rows:]], axis=-1).reshape(size, width)

    def queries(blk):
        fetched(blk)
        got = (dot_nt(take(blk).astype(BF16), wq[...]) * scale).astype(BF16)
        for s in range(shards):
            q[s, block_rows(blk, size), :] = got[:, s * LANES : (s + 1) * LANES]

    loop(queries)
    weights[1].wait()

    def score(img, at, count, first):
        for s in range(shards):
            keys = k[pl.ds(img * head, head), s * LANES : (s + 1) * LANES]
            p[s, pl.ds(at, win), :cols] = dot_nt(
                q[s, pl.ds(at, win), :], head_blocks(keys, heads, head)
            )

    windows(ints, images, rows, score, True)

    def soften(blk):
        at = block_rows(blk, size)
        for s in range(shards):
            raised = jnp.exp(p[s, at, :cols])
            prob = raised / head_sum(raised, head)
            p[s, at, :cols] = prob
            half[s, at, :cols] = prob.astype(BF16)
            for copy in results(blk, s):
                copy.start()

    loop(soften)
    weights[2].wait()

    def mix(img, at, count, first):
        for s in range(shards):
            lanes = slice(s * LANES, (s + 1) * LANES)
            vals = head_blocks(v[pl.ds(img * head, head), lanes], heads, head)
            mixed[pl.ds(at, win), lanes] = dot(half[s, pl.ds(at, win), :cols], vals).astype(BF16)

    windows(ints, images, rows, mix, True)
    weights[3].wait()
    scaled = const_ref[1:2]
    flat = scaled - jnp.mean(scaled, axis=-1, keepdims=True)

    def finish(blk):
        at = block_rows(blk, size)
        residual = take(blk) + dot(mixed[at, :], wo[...])
        centred = residual - jnp.mean(residual, axis=-1, keepdims=True)
        variance = jnp.mean(centred * centred, axis=-1, keepdims=True)
        inverse = 1.0 / jnp.sqrt(variance + EPS)
        unit = centred * inverse
        none = jnp.sum(unit * const_ref[0:1], axis=-1, keepdims=True)
        gap = jnp.sum(unit * scaled, axis=-1, keepdims=True)
        both = jnp.where(iota((size, 128), 1) == 0, none, none + gap)
        logs[block_rows(blk, SB), :] = jnp.sum(both.reshape(SB, rows, 128), axis=1)
        d_res[at, :] = (inverse * (flat - unit * (gap / width))).astype(BF16)
        gradient(blk).start()

    loop(finish)
    log_out[...] = logs[...].T[: log_out.shape[0]]

    def settle(blk):
        for s in range(shards):
            for copy in results(blk, s):
                copy.wait()
        gradient(blk).wait()

    loop(settle)


def backward_kernel(
    ints, sign_ref, *rest, mine, arrivals, head, heads, rows, terms
):
    parts, rest = rest[:terms], rest[terms:]
    d_in, wo_in, v_in, p_in, q_in = rest[:5]
    arrived, rest = rest[5 : 5 + arrivals], rest[5 + arrivals :]
    outs, rest = rest[: len(mine)], rest[len(mine) :]
    d_res, wo, v, p, q, dm, d_att, ds, pd, acc, delta, sems, sem_d = rest
    cols = heads * head
    images = v.shape[1] // head
    size = SB * rows
    win = WIN * rows
    blocks = blocks_of(ints)
    used = pl.ds(0, q.shape[1] - win)

    def loop(body):
        def one(blk, carry):
            body(blk)
            return carry

        lax.fori_loop(0, blocks, one, 0)

    def arrival(blk):
        at = block_rows(blk, size)
        return pltpu.make_async_copy(d_in.at[at], d_res.at[at], sem_d.at[blk])

    loop(lambda blk: arrival(blk).start())
    copies = []
    for j, shard in enumerate(mine):
        lanes = pl.ds(shard * LANES, LANES)
        copies.append(
            [
                pltpu.make_async_copy(src, dst, sems.at[4 * j + n])
                for n, (src, dst) in enumerate(
                    (
                        (wo_in.at[lanes, :], wo.at[j]),
                        (v_in.at[:, lanes], v.at[j]),
                        (p_in.at[shard], p.at[j]),
                        (q_in.at[shard], q.at[j, used]),
                    )
                )
            ]
        )
    for n in range(4):
        for group in copies:
            group[n].start()

    def settle(n):
        for group in copies:
            group[n].wait()

    logits = sum(part[...] for part in parts[1:]) + parts[0][...]
    sign = sign_ref[...]
    factor = sign / (1.0 + jnp.exp(sign * (logits[0:1] - logits[1:2])))
    delta[...] = jnp.broadcast_to(factor, (128, factor.shape[1])).T
    tail = pl.ds(pl.multiple_of(blocks * size, size), win)
    for j in range(len(mine)):
        dm[j, tail, :] = jnp.zeros((win, LANES), BF16)
    settle(0)

    def carry_back(blk):
        at = block_rows(blk, size)
        arrival(blk).wait()
        for j in range(len(mine)):
            dm[j, at, :] = dot_nt(d_res[at, :], wo[j]).astype(BF16)

    loop(carry_back)
    settle(1)

    def attend(img, at, count, first):
        for j in range(len(mine)):
            vals = head_blocks(v[j, pl.ds(img * head, head), :], heads, head)
            d_att[j, pl.ds(at, win), :cols] = dot_nt(dm[j, pl.ds(at, win), :], vals)

    windows(ints, images, rows, attend, True)
    settle(2)

    def soften(blk):
        at = block_rows(blk, size)
        weight = delta[block_rows(blk, SB), :]
        weight = jnp.broadcast_to(weight[:, None, :], (SB, rows, 128)).reshape(size, 128)[:, :1]
        for j in range(len(mine)):
            prob = p[j, at, :cols]
            grad = d_att[j, at, :cols]
            inner = head_sum(grad * prob, head)
            weighted = prob * weight
            ds[j, at, :cols] = (weighted * (grad - inner)).astype(BF16)
            pd[j, at, :cols] = weighted.astype(BF16)

    loop(soften)
    settle(3)
    for j in range(len(mine)):
        q[j, tail, :] = jnp.zeros((win, LANES), BF16)
    lane_head = iota((head, LANES), 1) // head
    place = iota((win, cols), 0)

    def diagonal(block):
        total = block[:head]
        for h in range(1, heads):
            total = jnp.where(lane_head == h, block[h * head : (h + 1) * head], total)
        return total[:, :cols]

    def outer(img, at, count, first):
        own = place < count
        here = pl.ds(at, win)
        zero = jnp.zeros((win, cols), BF16)
        for j in range(len(mine)):
            dk = diagonal(dot_tn(jnp.where(own, ds[j, here, :cols], zero), q[j, here, :]))
            dv = diagonal(dot_tn(jnp.where(own, pd[j, here, :cols], zero), dm[j, here, :]))
            term = jnp.concatenate([dk, dv], axis=-1)
            if first:
                acc[j, img * head : (img + 1) * head, :] = term
            else:
                acc[j, pl.ds(pl.multiple_of(img * head, head), head), :] += term

    windows(ints, images, rows, outer, False)
    for j, out_ref in enumerate(outs):
        total = acc[j]
        for a in arrived:
            total = total + a[...].astype(F32)
        out_ref[...] = total.astype(out_ref.dtype)


def whole(a):
    return pl.BlockSpec(a.shape, lambda *_: (0,) * a.ndim)


def local(
    images, query_states, neg_caption, neg_image, cross_query, cross_kv, cross_out, norm_gain,
    itm_weight,
):
    pair_count, patches, vis = images.shape
    queries, width = query_states.shape[1:]
    cols = cross_query.shape[1]
    head = width // HEADS
    scale = 1.0 / head**0.5
    groups = lax.axis_size("dp")
    shards = lax.axis_size("mp")
    dp, mp = lax.axis_index("dp"), lax.axis_index("mp")
    core = dp % NC
    rows = queries // shards
    half = width // 2

    def around(x, by):
        return lax.ppermute(x, "mp", [(i, (i + by) % shards) for i in range(shards)])

    def shift(x, by_z, by_x, by_core):
        moves = []
        for i in range(groups):
            z, x_, c = i // (NX * NC), i // NC % NX, i % NC
            to = ((z + by_z) % NZ * NX + (x_ + by_x) % NX) * NC + (c + by_core) % NC
            moves.append((i, to))
        return lax.ppermute(x, "dp", moves)

    own_rows = lax.dynamic_slice_in_dim(query_states, mp * rows, rows, 1)
    packed = jnp.concatenate([own_rows[:, :, :half], own_rows[:, :, half:]], axis=1)
    pool = lax.all_gather(packed[:GATHERED], "dp", axis=0, tiled=True)
    number = jnp.stack([neg_image // 32, neg_image % 32], axis=-1).astype(BF16)
    number = jnp.pad(number, ((0, 2 * rows - pair_count), (0, half - 2)))
    part = jnp.concatenate([packed[GATHERED:], number[None]], axis=0)
    units = part.shape[0]
    line = jnp.concatenate([part] + [shift(part, 0, -d, 0) for d in range(1, NX)], axis=0)
    up, down = [line], [line]
    for _ in range(NZ // 2 - 1):
        up.append(shift(up[-1], -1, 0, 0))
        down.append(shift(down[-1], 1, 0, 0))
    cut = NX // 2 * units
    across = [shift(up[-1][:cut], -1, 0, 0), shift(down[-1][cut:], 1, 0, 0)]
    carried = jnp.concatenate(up + across + down[:0:-1], axis=0)
    carried_other = shift(carried, 0, 0, 1)
    numbers = [x.reshape(-1, units, 2 * rows, half) for x in (carried, carried_other)]

    halves = [
        jnp.concatenate([cross_kv[0].T, cross_query.T], axis=1),
        jnp.concatenate([cross_kv[1].T, cross_out], axis=1),
    ]
    brought = jnp.where(core == 0, halves[0], halves[1])
    got = [around(brought, shards - s) for s in range(1, shards)]
    swap = [shift(g, 0, 0, 1) for g in got]
    flat = images.reshape(pair_count * patches, vis)
    params = pltpu.CompilerParams(vmem_limit_bytes=56 * 2**20)
    smem = pl.BlockSpec(memory_space=pltpu.SMEM)
    anywhere = pl.BlockSpec(memory_space=pl.ANY)
    vmem = pl.BlockSpec(memory_space=pltpu.VMEM)
    tall = shards * LANES
    out_rows = vis // groups
    pad_rows = (out_rows + 1 + 7) // 8 * 8
    chips = groups // NC
    shapes = [
        (pair_count * patches, tall), (pair_count * patches, tall), (tall, width), (tall, width),
        (groups * pad_rows, pair_count * patches),
    ]
    keys, values, wq, wo, spread = pl.pallas_call(
        functools.partial(project_kernel, shards=shards, cols=cols, vis=vis, out_rows=out_rows),
        in_specs=[smem] + [anywhere] * (1 + 2 * shards),
        out_specs=[anywhere] * 5,
        scratch_shapes=[
            pltpu.VMEM(flat.shape, BF16),
            pltpu.VMEM((shards, LANES, vis + width), BF16),
            pltpu.VMEM((shards, LANES, vis + width), BF16),
            pltpu.VMEM(shapes[0], BF16),
            pltpu.VMEM(shapes[1], BF16),
            pltpu.VMEM(shapes[4], BF16),
            pltpu.SemaphoreType.DMA((1 + 2 * shards,)),
            pltpu.SemaphoreType.DMA((1 + 4 * shards,)),
        ],
        out_shape=[jax.ShapeDtypeStruct(shape, BF16) for shape in shapes],
        compiler_params=params,
        cost_estimate=pl.CostEstimate(
            flops=4 * 10**10, bytes_accessed=20 * 10**6, transcendentals=0
        ),
        name="project",
    )(core.astype(I32).reshape(1), flat, *halves, *got, *swap)

    most = pair_count * (2 + CE - 1) + 2 * groups
    n_slots = -(-(most + WIN - CE) // SB) * SB
    n_rows = n_slots * rows
    n_lanes = -(-n_slots // 128) * 128
    ints, sign, hit = pl.pallas_call(
        plan_kernel,
        in_specs=[
            smem, anywhere, anywhere, vmem,
        ],
        out_specs=[vmem] * 3,
        scratch_shapes=[
            pltpu.VMEM((NC, groups // NC, 2 * rows, 128), BF16),
            pltpu.SemaphoreType.DMA((NC,)),
        ],
        out_shape=[
            jax.ShapeDtypeStruct((8, n_slots), I32),
            jax.ShapeDtypeStruct((1, n_lanes), F32),
            jax.ShapeDtypeStruct((groups * pair_count, n_slots), BF16),
        ],
        compiler_params=params,
        name="plan",
    )(dp.astype(I32).reshape(1), *numbers, neg_caption.reshape(-1, 1))

    fold = norm_gain / queries
    const = jnp.stack([fold * itm_weight[:, 0], fold * (itm_weight[:, 1] - itm_weight[:, 0])])
    q_rows, prob, d_res, log_part = pl.pallas_call(
        functools.partial(forward_kernel, head=head, scale=scale),
        in_specs=[smem] + [anywhere] * 7 + [vmem],
        out_specs=[anywhere] * 3 + [vmem],
        scratch_shapes=[
            pltpu.VMEM((n_slots, 2 * rows, half), BF16),
            pltpu.VMEM(wq.shape, BF16),
            pltpu.VMEM(keys.shape, BF16),
            pltpu.VMEM(values.shape, BF16),
            pltpu.VMEM(wo.shape, BF16),
            pltpu.VMEM((shards, n_rows, LANES), BF16),
            pltpu.VMEM((shards, n_rows, LANES), F32),
            pltpu.VMEM((shards, n_rows, LANES), BF16),
            pltpu.VMEM((n_rows, shards * LANES), BF16),
            pltpu.VMEM((n_rows, width), BF16),
            pltpu.VMEM((n_lanes, 128), F32),
            pltpu.SemaphoreType.DMA((n_slots // SB,)),
            pltpu.SemaphoreType.DMA((4,)),
            pltpu.SemaphoreType.DMA((3,)),
        ],
        out_shape=[
            jax.ShapeDtypeStruct((shards, n_rows, LANES), BF16),
            jax.ShapeDtypeStruct((shards, n_rows, LANES), F32),
            jax.ShapeDtypeStruct((n_rows, width), BF16),
            jax.ShapeDtypeStruct((8, n_lanes), F32),
        ],
        compiler_params=params,
        name="forward",
    )(ints, pool, carried, carried_other, wq, keys, values, wo, const)

    parts = [log_part] + [around(log_part, shards - s) for s in range(1, shards)]
    logits = jnp.zeros((2, n_slots), F32)
    for m in range(shards):
        for s in range(shards):
            logits = logits + jnp.where((mp + s) % shards == m, parts[s][:2, :n_slots], 0.0)
    logits = jnp.where(sign[:, :n_slots] != 0.0, logits, 0.0)

    def backward(mine, arrived=(), kind=BF16):
        shape = (pair_count * patches, 2 * cols)
        slack = n_rows + WIN * rows
        n = len(mine)
        return pl.pallas_call(
            functools.partial(
                backward_kernel, mine=mine, arrivals=len(arrived), head=head,
                heads=HEADS // shards, rows=rows, terms=shards,
            ),
            in_specs=[smem] + [vmem] * (1 + shards) + [anywhere] * 5 + [vmem] * len(arrived),
            out_specs=[vmem] * n,
            scratch_shapes=[
                pltpu.VMEM((n_rows, width), BF16),
                pltpu.VMEM((n, LANES, width), BF16),
                pltpu.VMEM((n, pair_count * patches, LANES), BF16),
                pltpu.VMEM((n, n_rows, LANES), F32),
                pltpu.VMEM((n, slack, LANES), BF16),
                pltpu.VMEM((n, slack, LANES), BF16),
                pltpu.VMEM((n, slack, LANES), F32),
                pltpu.VMEM((n, slack, LANES), BF16),
                pltpu.VMEM((n, slack, LANES), BF16),
                pltpu.VMEM((n,) + shape, F32),
                pltpu.VMEM((n_lanes, 128), F32),
                pltpu.SemaphoreType.DMA((4 * n,)),
                pltpu.SemaphoreType.DMA((n_slots // SB,)),
            ],
            out_shape=[jax.ShapeDtypeStruct(shape, kind)] * n,
            compiler_params=params,
            cost_estimate=pl.CostEstimate(flops=10**6, bytes_accessed=10**4, transcendentals=0),
            name="backward",
        )(ints, sign, *parts, d_res, wo, values, prob, q_rows, *arrived)

    two = around(backward((2,))[0], 2)
    one, three = backward((1, 3))
    one, three = around(one, 1), around(three, 3)
    own = backward((0,), (two,), F32)[0]
    d_kv = (own + one.astype(F32) + three.astype(F32)).astype(BF16)

    logit_hi = logits.astype(BF16)
    logit_lo = (logits - logit_hi.astype(F32)).astype(BF16)
    four = jnp.concatenate([logit_hi, logit_lo], axis=0)
    home = dot_nt(hit, four).astype(BF16)
    home = jnp.pad(
        home.reshape(groups, 1, 4 * pair_count),
        ((0, 0), (out_rows, pad_rows - out_rows - 1), (0, 2 * cols - 4 * pair_count)),
    )
    home, d_kv = lax.optimization_barrier((home, d_kv))
    grad = dot(spread, d_kv).reshape(groups, pad_rows, 2 * cols)
    over = shift((grad[chips:] + home[chips:]).astype(BF16), 0, 0, 1)
    leaving = (grad[:chips] + home[:chips] + over).astype(BF16)
    alike = [[chip * NC + c for chip in range(chips)] for c in range(NC)]
    arrived = lax.all_to_all(
        leaving, "dp", split_axis=0, concat_axis=0, tiled=True, axis_index_groups=alike
    )
    summed = jnp.sum(arrived.astype(F32), axis=0)
    grad_part = jnp.transpose(summed[:out_rows].reshape(out_rows, 2, cols), (1, 0, 2))
    back = summed[out_rows, : 4 * pair_count].reshape(pair_count, 2, 2)
    pushed_logits = back[:, 0] + back[:, 1]
    image = jnp.arange(pair_count, dtype=I32)[:, None]
    own_logits = []
    for j in range(2):
        here = ((ints[1:2] == image) & (ints[2:3] == j))[:, None, :]
        own_logits.append(jnp.sum(jnp.where(here, logits[None], 0.0), axis=-1))
    return (jnp.stack(own_logits + [pushed_logits]), grad_part)


def solution(mesh):
    return jax.shard_map(
        local,
        mesh=mesh,
        in_specs=(
            P("dp", None, None),
            P("dp", None, None),
            P("dp"),
            P("dp"),
            P(None, "mp"),
            P(None, None, "mp"),
            P("mp", None),
            P(),
            P(),
        ),
        out_specs=(P(None, "dp", None), P(None, "dp", "mp")),
        check_vma=False,
    )
```

```python
import functools

import jax
import jax.numpy as jnp
from jax import lax
from jax.experimental import pallas as pl
from jax.experimental.pallas import tpu as pltpu
from jax.sharding import PartitionSpec as P

HEADS = 12
EPS = 1e-06
CE = 2
SB = 32
WIN = 16
LANES = 256
NZ, NX, NC = 8, 4, 2
GATHERED = 12
BF16 = jnp.bfloat16
F32 = jnp.float32
I32 = jnp.int32


def dot(a, b):
    return jnp.dot(a, b, preferred_element_type=F32)


def dot_nt(a, b):
    return lax.dot_general(a, b, (((1,), (1,)), ((), ())), preferred_element_type=F32)


def dot_tn(a, b):
    return lax.dot_general(a, b, (((0,), (0,)), ((), ())), preferred_element_type=F32)


def iota(shape, axis):
    return lax.broadcasted_iota(I32, shape, axis)


def head_blocks(rows, heads, head):
    lane_head = iota(rows.shape, 1) // head
    zero = jnp.zeros_like(rows)
    return jnp.concatenate([jnp.where(lane_head == h, rows, zero) for h in range(heads)], axis=0)


def head_sum(values, head):
    width = values.shape[-1]
    same = iota((width, width), 0) // head == iota((width, width), 1) // head
    ones = jnp.where(same, 1.0, 0.0).astype(BF16)
    upper = values.astype(BF16)
    lower = (values - upper.astype(F32)).astype(BF16)
    return dot(upper, ones) + dot(lower, ones)


def plan_kernel(dp_ref, mine_in, other_in, neg_ref, ints_out, sign_out, hit_out, held, sems):
    images = neg_ref.shape[0]
    copies = [
        pltpu.make_async_copy(
            source.at[:, source.shape[1] - 1, :, pl.ds(0, 128)], held.at[j], sems.at[j]
        )
        for j, source in enumerate((mine_in, other_in))
    ]
    for copy in copies:
        copy.start()
    total = hit_out.shape[0]
    slots = ints_out.shape[1]
    dp = dp_ref[0]
    z, x, c = lax.div(dp, NX * NC), lax.rem(lax.div(dp, NC), NX), lax.rem(dp, NC)
    base = dp * images
    place = iota((total, 1), 0)

    def digit(value, by, size):
        return lax.rem(lax.div(value, jnp.full_like(value, by)), jnp.full_like(value, size))

    def ahead(start, steps, size):
        to = start + steps
        return jnp.where(to >= size, to - size, to)

    block = ahead(z, digit(place, images * NX, NZ), NZ) * NX
    block = (block + ahead(x, digit(place, images, NX), NX)) * NC
    block = block + ahead(c, digit(place, images * NX * NZ, NC), NC)
    number = block * images + digit(place, 1, images)
    for copy in copies:
        copy.wait()
    ids = held[...].astype(F32).reshape(total, 128)
    ids = (ids[:, :1] * 32 + ids[:, 1:2]).astype(I32)
    own = (ids - base) == iota((total, images), 1)
    ones = jnp.where(own, 1.0, 0.0)
    below = jnp.where(iota((128, 128), 0) >= iota((128, 128), 1), 1.0, 0.0).astype(BF16)
    count_row = jnp.zeros((1, images), F32)
    upto = []
    for j in range(total // 128):
        piece = ones[128 * j : 128 * (j + 1)]
        upto.append(dot(below, piece.astype(BF16)) + count_row)
        count_row = count_row + jnp.sum(piece, axis=0, keepdims=True)
    upto = jnp.concatenate(upto, axis=0)
    diagonal = iota((images, images), 0) == iota((images, images), 1)
    count_col = jnp.sum(jnp.where(diagonal, count_row, 0.0), axis=1, keepdims=True)

    def chunks_of(count):
        return lax.div(count.astype(I32) + (2 + CE - 1), jnp.full(count.shape, CE, I32))

    chunks_row, chunks_col = chunks_of(count_row), chunks_of(count_col)
    before = iota((images, images), 0) < iota((images, images), 1)
    after = iota((images, images), 0) > iota((images, images), 1)
    first_row = jnp.sum(jnp.where(before, chunks_col, 0), axis=0, keepdims=True)
    first_col = jnp.sum(jnp.where(after, chunks_row, 0), axis=1, keepdims=True)
    n_chunks = jnp.sum(chunks_row, axis=1, keepdims=True)
    slot_of = jnp.sum(
        jnp.where(own, (first_row * CE + 1).astype(F32) + upto, 0.0), axis=1, keepdims=True
    ).astype(I32)
    slot = iota((1, slots), 1)
    chunk = lax.div(slot, jnp.full(slot.shape, CE, I32))
    img = jnp.sum(jnp.where(chunk >= first_col, 1, 0), axis=0, keepdims=True) - 1
    at_img = img == iota((images, slots), 0)
    pos = slot - CE * jnp.sum(jnp.where(at_img, first_col, 0), axis=0, keepdims=True)
    negative = jnp.sum(jnp.where(at_img, neg_ref[...], 0), axis=0, keepdims=True)
    hit = (slot_of == slot) & (pos >= 2)
    pushed = jnp.sum(jnp.where(hit, number + 1, 0), axis=0, keepdims=True)
    used = (chunk < n_chunks) & ((pos < 2) | (pushed > 0))
    cap = jnp.where(pos == 0, base + img, jnp.where(pos == 1, negative, pushed - 1))
    local = digit(cap, 1, images)
    block = digit(cap, images, total)
    by_z = digit(block, NX * NC, NZ) - z
    by_x = digit(block, NC, NX) - x
    by_z = jnp.where(by_z < 0, by_z + NZ, by_z)
    by_x = jnp.where(by_x < 0, by_x + NX, by_x)
    gathered = local < GATHERED
    carried = (by_z * NX + by_x) * (images - GATHERED + 1) + local - GATHERED
    unit = jnp.where(gathered, block * GATHERED + local, carried)
    kind = jnp.where(gathered, 0, jnp.where(digit(block, 1, NC) == c, 1, 2))
    unit = jnp.where(used, unit, 0)
    kind = jnp.where(used, kind, 0)
    most = jnp.max(count_row, axis=1, keepdims=True).astype(I32) + 2
    row = iota((8, slots), 0)
    lane = iota((images, slots), 0) == iota((images, slots), 1)
    start = jnp.sum(jnp.where(lane, first_col * CE, 0), axis=0, keepdims=True)
    count = jnp.sum(jnp.where(lane, count_col.astype(I32) + 2, 0), axis=0, keepdims=True)
    ints = n_chunks
    for at, values in enumerate((unit, img, pos, n_chunks, start, count, kind, most)):
        ints = jnp.where(row == at, values, ints)
    ints_out[...] = ints
    sign_out[...] = jnp.zeros_like(sign_out)
    sign_out[:, :slots] = jnp.where(used, jnp.where(pos == 0, -1.0, 1.0), 0.0)
    chips = total // images // NC
    half = digit(place, images * chips, NC)
    number = digit(place, images, chips) * NC + ahead(c, half, NC)
    number = number * images + digit(place, 1, images)
    home = (number == cap) & used & (pos >= 2)
    hit_out[...] = jnp.where(home, 1.0, 0.0).astype(BF16)


def blocks_of(ints):
    return lax.div(ints[3, 0] * CE + (SB - 1), SB)


def windows(ints, images, rows, act, extra_first):
    def extra():
        def one(img, carry):
            count = ints[5, img]

            def more(w, carry):
                at = pl.multiple_of((ints[4, img] + w * WIN) * rows, CE * rows)
                act(img, at, (count - w * WIN) * rows, False)
                return carry

            return lax.fori_loop(1, lax.div(count + (WIN - 1), WIN), more, carry)

        @pl.when(ints[7, 0] > WIN)
        def _():
            lax.fori_loop(0, images, one, 0)

    if extra_first:
        extra()
    for img in range(images):
        at = pl.multiple_of(ints[4, img] * rows, CE * rows)
        act(img, at, ints[5, img] * rows, True)
    if not extra_first:
        extra()


def block_rows(blk, size):
    return pl.ds(pl.multiple_of(blk * size, size), size)


def project_kernel(core, flat_in, first_in, second_in, *rest, shards, cols, vis, out_rows):
    got, swap = rest[: shards - 1], rest[shards - 1 : 2 * shards - 2]
    k_out, v_out, wq_out, wo_out, spread_out = rest[2 * shards - 2 : 2 * shards + 3]
    flat, first, second, k, v, spread, sems, sem_o = rest[2 * shards + 3 :]
    count = flat.shape[0]
    side = core[0]
    pltpu.make_async_copy(flat_in, flat, sems.at[0]).start()
    own = pl.ds(0, cols)

    def landing(j, s):
        return (first, second)[j].at[s, own], sems.at[1 + 2 * s + j]

    for j, source in enumerate((first_in, second_in)):
        pltpu.make_async_copy(source, *landing(j, 0)).start()
    for s in range(1, shards):
        for j in range(NC):

            @pl.when(side == j)
            def _():
                pltpu.make_async_copy(got[s - 1], *landing(j, s)).start()

            @pl.when(side != j)
            def _():
                pltpu.make_async_copy(swap[s - 1], *landing(j, s)).start()

    pad = jnp.zeros((LANES - cols, first.shape[2]), BF16)
    for s in range(shards):
        first[s, cols:, :] = pad
        second[s, cols:, :] = pad
    pltpu.make_async_copy(flat_in, flat, sems.at[0]).wait()
    leaving = []

    def leave(source, target):
        copy = pltpu.make_async_copy(source, target, sem_o.at[len(leaving)])
        copy.start()
        leaving.append(copy)

    step = vis // NZ
    slot = spread.shape[0] // (NZ * NX * NC)
    half = spread.shape[0] // NC
    for z in range(NZ):
        low = step * z // 128 * 128
        window = -(-(step * z + step - low) // 128) * 128
        row, lane = iota((NX * NC * slot, window), 0), iota((NX * NC * slot, window), 1)
        inner = row % slot
        kind = (row // (NX * slot) + side) % NC
        goal = (row // slot % NX * NC + kind) * out_rows + inner + (step * z - low)
        chosen = jnp.where((lane == goal) & (inner < out_rows), 1.0, 0.0).astype(BF16)
        moved = dot_nt(chosen, flat[:, low : low + window]).astype(BF16)
        for c in range(NC):
            part = slice(c * half + z * NX * slot, c * half + (z + 1) * NX * slot)
            spread[part, :] = moved[c * NX * slot : (c + 1) * NX * slot]
    leave(spread, spread_out)
    for s in range(shards):
        lanes = slice(s * LANES, (s + 1) * LANES)
        for j, (held, kept, out, other) in enumerate(
            ((first, k, k_out, wq_out), (second, v, v_out, wo_out))
        ):
            pltpu.make_async_copy(first_in, *landing(j, s)).wait()
            leave(held.at[s, :, pl.ds(vis, held.shape[2] - vis)], other.at[pl.ds(s * LANES, LANES)])
            for n in range(0, count, 512):
                kept[n : n + 512, lanes] = dot_nt(flat[n : n + 512], held[s, :, :vis]).astype(BF16)
            leave(kept.at[:, pl.ds(s * LANES, LANES)], out.at[:, pl.ds(s * LANES, LANES)])
    for copy in leaving:
        copy.wait()


def forward_kernel(
    ints, pool, carried, carried_other, wq_in, k_in, v_in, wo_in, const_ref, q_out, p_out, d_out, log_out,
    xbuf, wq, k, v, wo, q, p, half, mixed, d_res, logs, sem_x, sem_w, sem_o, *, head, scale,
):
    width = wo.shape[1]
    shards = wq.shape[0] // LANES
    heads = HEADS // shards
    cols = heads * head
    images = k.shape[0] // head
    rows = xbuf.shape[1] // 2
    size = SB * rows
    win = WIN * rows
    blocks = blocks_of(ints)
    weights = [
        pltpu.make_async_copy(src, dst, sem_w.at[j])
        for j, (src, dst) in enumerate(((wq_in, wq), (k_in, k), (v_in, v), (wo_in, wo)))
    ]
    for copy in weights:
        copy.start()

    def fetch(blk):
        def one(j, carry):
            slot = blk * SB + j
            for at, source in enumerate((pool, carried, carried_other)):

                @pl.when(ints[6, slot] == at)
                def _():
                    pltpu.make_async_copy(
                        source.at[ints[0, slot]], xbuf.at[slot], sem_x.at[blk]
                    ).start()

            return carry

        lax.fori_loop(0, SB, one, 0, unroll=4)

    def fetched(blk):
        here = xbuf.at[block_rows(blk, SB)]
        pltpu.make_async_copy(pool.at[pl.ds(0, SB)], here, sem_x.at[blk]).wait()

    def results(blk, s):
        at = block_rows(blk, size)
        return [
            pltpu.make_async_copy(q.at[s, at], q_out.at[s, at], sem_o.at[0]),
            pltpu.make_async_copy(p.at[s, at], p_out.at[s, at], sem_o.at[1]),
        ]

    def gradient(blk):
        at = block_rows(blk, size)
        return pltpu.make_async_copy(d_res.at[at], d_out.at[at], sem_o.at[2])

    def loop(body):
        def one(blk, carry):
            body(blk)
            return carry

        lax.fori_loop(0, blocks, one, 0)

    loop(fetch)
    weights[0].wait()

    def take(blk):
        x16 = xbuf[block_rows(blk, SB)].astype(F32)
        return jnp.concatenate([x16[:, :rows], x16[:, rows:]], axis=-1).reshape(size, width)

    def queries(blk):
        fetched(blk)
        got = (dot_nt(take(blk).astype(BF16), wq[...]) * scale).astype(BF16)
        for s in range(shards):
            q[s, block_rows(blk, size), :] = got[:, s * LANES : (s + 1) * LANES]

    loop(queries)
    weights[1].wait()

    def score(img, at, count, first):
        for s in range(shards):
            keys = k[pl.ds(img * head, head), s * LANES : (s + 1) * LANES]
            p[s, pl.ds(at, win), :cols] = dot_nt(
                q[s, pl.ds(at, win), :], head_blocks(keys, heads, head)
            )

    windows(ints, images, rows, score, True)

    def soften(blk):
        at = block_rows(blk, size)
        for s in range(shards):
            raised = jnp.exp(p[s, at, :cols])
            prob = raised / head_sum(raised, head)
            p[s, at, :cols] = prob
            half[s, at, :cols] = prob.astype(BF16)
            for copy in results(blk, s):
                copy.start()

    loop(soften)
    weights[2].wait()

    def mix(img, at, count, first):
        for s in range(shards):
            lanes = slice(s * LANES, (s + 1) * LANES)
            vals = head_blocks(v[pl.ds(img * head, head), lanes], heads, head)
            mixed[pl.ds(at, win), lanes] = dot(half[s, pl.ds(at, win), :cols], vals).astype(BF16)

    windows(ints, images, rows, mix, True)
    weights[3].wait()
    scaled = const_ref[1:2]
    flat = scaled - jnp.mean(scaled, axis=-1, keepdims=True)

    def finish(blk):
        at = block_rows(blk, size)
        residual = take(blk) + dot(mixed[at, :], wo[...])
        centred = residual - jnp.mean(residual, axis=-1, keepdims=True)
        variance = jnp.mean(centred * centred, axis=-1, keepdims=True)
        inverse = 1.0 / jnp.sqrt(variance + EPS)
        unit = centred * inverse
        none = jnp.sum(unit * const_ref[0:1], axis=-1, keepdims=True)
        gap = jnp.sum(unit * scaled, axis=-1, keepdims=True)
        both = jnp.where(iota((size, 128), 1) == 0, none, none + gap)
        logs[block_rows(blk, SB), :] = jnp.sum(both.reshape(SB, rows, 128), axis=1)
        d_res[at, :] = (inverse * (flat - unit * (gap / width))).astype(BF16)
        gradient(blk).start()

    loop(finish)
    log_out[...] = logs[...].T[: log_out.shape[0]]

    def settle(blk):
        for s in range(shards):
            for copy in results(blk, s):
                copy.wait()
        gradient(blk).wait()

    loop(settle)


def backward_kernel(
    ints, sign_ref, *rest, mine, arrivals, head, heads, rows, terms
):
    parts, rest = rest[:terms], rest[terms:]
    d_in, wo_in, v_in, p_in, q_in = rest[:5]
    arrived, rest = rest[5 : 5 + arrivals], rest[5 + arrivals :]
    outs, rest = rest[: len(mine)], rest[len(mine) :]
    d_res, wo, v, p, q, dm, d_att, ds, pd, acc, delta, sems, sem_d = rest
    cols = heads * head
    images = v.shape[1] // head
    size = SB * rows
    win = WIN * rows
    blocks = blocks_of(ints)
    used = pl.ds(0, q.shape[1] - win)

    def loop(body):
        def one(blk, carry):
            body(blk)
            return carry

        lax.fori_loop(0, blocks, one, 0)

    def arrival(blk):
        at = block_rows(blk, size)
        return pltpu.make_async_copy(d_in.at[at], d_res.at[at], sem_d.at[blk])

    loop(lambda blk: arrival(blk).start())
    copies = []
    for j, shard in enumerate(mine):
        lanes = pl.ds(shard * LANES, LANES)
        copies.append(
            [
                pltpu.make_async_copy(src, dst, sems.at[4 * j + n])
                for n, (src, dst) in enumerate(
                    (
                        (wo_in.at[lanes, :], wo.at[j]),
                        (v_in.at[:, lanes], v.at[j]),
                        (p_in.at[shard], p.at[j]),
                        (q_in.at[shard], q.at[j, used]),
                    )
                )
            ]
        )
    for n in range(4):
        for group in copies:
            group[n].start()

    def settle(n):
        for group in copies:
            group[n].wait()

    logits = sum(part[...] for part in parts[1:]) + parts[0][...]
    sign = sign_ref[...]
    factor = sign / (1.0 + jnp.exp(sign * (logits[0:1] - logits[1:2])))
    delta[...] = jnp.broadcast_to(factor, (128, factor.shape[1])).T
    tail = pl.ds(pl.multiple_of(blocks * size, size), win)
    for j in range(len(mine)):
        dm[j, tail, :] = jnp.zeros((win, LANES), BF16)
    settle(0)

    def carry_back(blk):
        at = block_rows(blk, size)
        arrival(blk).wait()
        for j in range(len(mine)):
            dm[j, at, :] = dot_nt(d_res[at, :], wo[j]).astype(BF16)

    loop(carry_back)
    settle(1)

    def attend(img, at, count, first):
        for j in range(len(mine)):
            vals = head_blocks(v[j, pl.ds(img * head, head), :], heads, head)
            d_att[j, pl.ds(at, win), :cols] = dot_nt(dm[j, pl.ds(at, win), :], vals)

    windows(ints, images, rows, attend, True)
    settle(2)

    def soften(blk):
        at = block_rows(blk, size)
        weight = delta[block_rows(blk, SB), :]
        weight = jnp.broadcast_to(weight[:, None, :], (SB, rows, 128)).reshape(size, 128)[:, :1]
        for j in range(len(mine)):
            prob = p[j, at, :cols]
            grad = d_att[j, at, :cols]
            inner = head_sum(grad * prob, head)
            weighted = prob * weight
            ds[j, at, :cols] = (weighted * (grad - inner)).astype(BF16)
            pd[j, at, :cols] = weighted.astype(BF16)

    loop(soften)
    settle(3)
    for j in range(len(mine)):
        q[j, tail, :] = jnp.zeros((win, LANES), BF16)
    lane_head = iota((head, LANES), 1) // head
    place = iota((win, cols), 0)

    def diagonal(block):
        total = block[:head]
        for h in range(1, heads):
            total = jnp.where(lane_head == h, block[h * head : (h + 1) * head], total)
        return total[:, :cols]

    def outer(img, at, count, first):
        own = place < count
        here = pl.ds(at, win)
        zero = jnp.zeros((win, cols), BF16)
        for j in range(len(mine)):
            dk = diagonal(dot_tn(jnp.where(own, ds[j, here, :cols], zero), q[j, here, :]))
            dv = diagonal(dot_tn(jnp.where(own, pd[j, here, :cols], zero), dm[j, here, :]))
            term = jnp.concatenate([dk, dv], axis=-1)
            if first:
                acc[j, img * head : (img + 1) * head, :] = term
            else:
                acc[j, pl.ds(pl.multiple_of(img * head, head), head), :] += term

    windows(ints, images, rows, outer, False)
    for j, out_ref in enumerate(outs):
        total = acc[j]
        for a in arrived:
            total = total + a[...].astype(F32)
        out_ref[...] = total.astype(out_ref.dtype)


def whole(a):
    return pl.BlockSpec(a.shape, lambda *_: (0,) * a.ndim)


def local(
    images, query_states, neg_caption, neg_image, cross_query, cross_kv, cross_out, norm_gain,
    itm_weight,
):
    pair_count, patches, vis = images.shape
    queries, width = query_states.shape[1:]
    cols = cross_query.shape[1]
    head = width // HEADS
    scale = 1.0 / head**0.5
    groups = lax.axis_size("dp")
    shards = lax.axis_size("mp")
    dp, mp = lax.axis_index("dp"), lax.axis_index("mp")
    core = dp % NC
    rows = queries // shards
    half = width // 2

    def around(x, by):
        return lax.ppermute(x, "mp", [(i, (i + by) % shards) for i in range(shards)])

    def shift(x, by_z, by_x, by_core):
        moves = []
        for i in range(groups):
            z, x_, c = i // (NX * NC), i // NC % NX, i % NC
            to = ((z + by_z) % NZ * NX + (x_ + by_x) % NX) * NC + (c + by_core) % NC
            moves.append((i, to))
        return lax.ppermute(x, "dp", moves)

    own_rows = lax.dynamic_slice_in_dim(query_states, mp * rows, rows, 1)
    packed = jnp.concatenate([own_rows[:, :, :half], own_rows[:, :, half:]], axis=1)
    pool = lax.all_gather(packed[:GATHERED], "dp", axis=0, tiled=True)
    halves = [
        jnp.concatenate([cross_kv[0].T, cross_query.T], axis=1),
        jnp.concatenate([cross_kv[1].T, cross_out], axis=1),
    ]
    brought = jnp.where(core == 0, halves[0], halves[1])
    got = [around(brought, shards - s) for s in range(1, shards)]
    number = jnp.stack([neg_image // 32, neg_image % 32], axis=-1).astype(BF16)
    number = jnp.pad(number, ((0, 2 * rows - pair_count), (0, half - 2)))
    part = jnp.concatenate([packed[GATHERED:], number[None]], axis=0)
    units = part.shape[0]
    line = jnp.concatenate([part] + [shift(part, 0, -d, 0) for d in range(1, NX)], axis=0)
    up, down = [line], [line]
    for step in range(NZ // 2 - 1):
        if step == 2:
            up[-1], down[-1], *got = lax.optimization_barrier((up[-1], down[-1], *got))
        up.append(shift(up[-1], -1, 0, 0))
        down.append(shift(down[-1], 1, 0, 0))
    cut = NX // 2 * units
    across = [shift(up[-1][:cut], -1, 0, 0), shift(down[-1][cut:], 1, 0, 0)]
    carried = jnp.concatenate(up + across + down[:0:-1], axis=0)
    carried_other = shift(carried, 0, 0, 1)
    numbers = [x.reshape(-1, units, 2 * rows, half) for x in (carried, carried_other)]

    swap = [shift(g, 0, 0, 1) for g in got]
    flat = images.reshape(pair_count * patches, vis)
    params = pltpu.CompilerParams(vmem_limit_bytes=56 * 2**20)
    smem = pl.BlockSpec(memory_space=pltpu.SMEM)
    anywhere = pl.BlockSpec(memory_space=pl.ANY)
    vmem = pl.BlockSpec(memory_space=pltpu.VMEM)
    tall = shards * LANES
    out_rows = vis // groups
    pad_rows = (out_rows + 1 + 7) // 8 * 8
    chips = groups // NC
    shapes = [
        (pair_count * patches, tall), (pair_count * patches, tall), (tall, width), (tall, width),
        (groups * pad_rows, pair_count * patches),
    ]
    keys, values, wq, wo, spread = pl.pallas_call(
        functools.partial(project_kernel, shards=shards, cols=cols, vis=vis, out_rows=out_rows),
        in_specs=[smem] + [anywhere] * (1 + 2 * shards),
        out_specs=[anywhere] * 5,
        scratch_shapes=[
            pltpu.VMEM(flat.shape, BF16),
            pltpu.VMEM((shards, LANES, vis + width), BF16),
            pltpu.VMEM((shards, LANES, vis + width), BF16),
            pltpu.VMEM(shapes[0], BF16),
            pltpu.VMEM(shapes[1], BF16),
            pltpu.VMEM(shapes[4], BF16),
            pltpu.SemaphoreType.DMA((1 + 2 * shards,)),
            pltpu.SemaphoreType.DMA((1 + 4 * shards,)),
        ],
        out_shape=[jax.ShapeDtypeStruct(shape, BF16) for shape in shapes],
        compiler_params=params,
        cost_estimate=pl.CostEstimate(
            flops=4 * 10**10, bytes_accessed=20 * 10**6, transcendentals=0
        ),
        name="project",
    )(core.astype(I32).reshape(1), flat, *halves, *got, *swap)

    most = pair_count * (2 + CE - 1) + 2 * groups
    n_slots = -(-(most + WIN - CE) // SB) * SB
    n_rows = n_slots * rows
    n_lanes = -(-n_slots // 128) * 128
    ints, sign, hit = pl.pallas_call(
        plan_kernel,
        in_specs=[
            smem, anywhere, anywhere, vmem,
        ],
        out_specs=[vmem] * 3,
        scratch_shapes=[
            pltpu.VMEM((NC, groups // NC, 2 * rows, 128), BF16),
            pltpu.SemaphoreType.DMA((NC,)),
        ],
        out_shape=[
            jax.ShapeDtypeStruct((8, n_slots), I32),
            jax.ShapeDtypeStruct((1, n_lanes), F32),
            jax.ShapeDtypeStruct((groups * pair_count, n_slots), BF16),
        ],
        compiler_params=params,
        name="plan",
    )(dp.astype(I32).reshape(1), *numbers, neg_caption.reshape(-1, 1))

    fold = norm_gain / queries
    const = jnp.stack([fold * itm_weight[:, 0], fold * (itm_weight[:, 1] - itm_weight[:, 0])])
    q_rows, prob, d_res, log_part = pl.pallas_call(
        functools.partial(forward_kernel, head=head, scale=scale),
        in_specs=[smem] + [anywhere] * 7 + [vmem],
        out_specs=[anywhere] * 3 + [vmem],
        scratch_shapes=[
            pltpu.VMEM((n_slots, 2 * rows, half), BF16),
            pltpu.VMEM(wq.shape, BF16),
            pltpu.VMEM(keys.shape, BF16),
            pltpu.VMEM(values.shape, BF16),
            pltpu.VMEM(wo.shape, BF16),
            pltpu.VMEM((shards, n_rows, LANES), BF16),
            pltpu.VMEM((shards, n_rows, LANES), F32),
            pltpu.VMEM((shards, n_rows, LANES), BF16),
            pltpu.VMEM((n_rows, shards * LANES), BF16),
            pltpu.VMEM((n_rows, width), BF16),
            pltpu.VMEM((n_lanes, 128), F32),
            pltpu.SemaphoreType.DMA((n_slots // SB,)),
            pltpu.SemaphoreType.DMA((4,)),
            pltpu.SemaphoreType.DMA((3,)),
        ],
        out_shape=[
            jax.ShapeDtypeStruct((shards, n_rows, LANES), BF16),
            jax.ShapeDtypeStruct((shards, n_rows, LANES), F32),
            jax.ShapeDtypeStruct((n_rows, width), BF16),
            jax.ShapeDtypeStruct((8, n_lanes), F32),
        ],
        compiler_params=params,
        name="forward",
    )(ints, pool, carried, carried_other, wq, keys, values, wo, const)

    parts = [log_part] + [around(log_part, shards - s) for s in range(1, shards)]
    logits = jnp.zeros((2, n_slots), F32)
    for m in range(shards):
        for s in range(shards):
            logits = logits + jnp.where((mp + s) % shards == m, parts[s][:2, :n_slots], 0.0)
    logits = jnp.where(sign[:, :n_slots] != 0.0, logits, 0.0)

    def backward(mine, arrived=(), kind=BF16):
        shape = (pair_count * patches, 2 * cols)
        slack = n_rows + WIN * rows
        n = len(mine)
        return pl.pallas_call(
            functools.partial(
                backward_kernel, mine=mine, arrivals=len(arrived), head=head,
                heads=HEADS // shards, rows=rows, terms=shards,
            ),
            in_specs=[smem] + [vmem] * (1 + shards) + [anywhere] * 5 + [vmem] * len(arrived),
            out_specs=[vmem] * n,
            scratch_shapes=[
                pltpu.VMEM((n_rows, width), BF16),
                pltpu.VMEM((n, LANES, width), BF16),
                pltpu.VMEM((n, pair_count * patches, LANES), BF16),
                pltpu.VMEM((n, n_rows, LANES), F32),
                pltpu.VMEM((n, slack, LANES), BF16),
                pltpu.VMEM((n, slack, LANES), BF16),
                pltpu.VMEM((n, slack, LANES), F32),
                pltpu.VMEM((n, slack, LANES), BF16),
                pltpu.VMEM((n, slack, LANES), BF16),
                pltpu.VMEM((n,) + shape, F32),
                pltpu.VMEM((n_lanes, 128), F32),
                pltpu.SemaphoreType.DMA((4 * n,)),
                pltpu.SemaphoreType.DMA((n_slots // SB,)),
            ],
            out_shape=[jax.ShapeDtypeStruct(shape, kind)] * n,
            compiler_params=params,
            cost_estimate=pl.CostEstimate(flops=10**6, bytes_accessed=10**4, transcendentals=0),
            name="backward",
        )(ints, sign, *parts, d_res, wo, values, prob, q_rows, *arrived)

    two = around(backward((2,))[0], 2)
    one, three = backward((1, 3))
    one, three = around(one, 1), around(three, 3)
    own = backward((0,), (two,), F32)[0]
    d_kv = (own + one.astype(F32) + three.astype(F32)).astype(BF16)

    logit_hi = logits.astype(BF16)
    logit_lo = (logits - logit_hi.astype(F32)).astype(BF16)
    four = jnp.concatenate([logit_hi, logit_lo], axis=0)
    home = dot_nt(hit, four).astype(BF16)
    home = jnp.pad(
        home.reshape(groups, 1, 4 * pair_count),
        ((0, 0), (out_rows, pad_rows - out_rows - 1), (0, 2 * cols - 4 * pair_count)),
    )
    home, d_kv = lax.optimization_barrier((home, d_kv))
    grad = dot(spread, d_kv).reshape(groups, pad_rows, 2 * cols)
    over = shift((grad[chips:] + home[chips:]).astype(BF16), 0, 0, 1)
    leaving = (grad[:chips] + home[:chips] + over).astype(BF16)
    alike = [[chip * NC + c for chip in range(chips)] for c in range(NC)]
    arrived = lax.all_to_all(
        leaving, "dp", split_axis=0, concat_axis=0, tiled=True, axis_index_groups=alike
    )
    summed = jnp.sum(arrived.astype(F32), axis=0)
    grad_part = jnp.transpose(summed[:out_rows].reshape(out_rows, 2, cols), (1, 0, 2))
    back = summed[out_rows, : 4 * pair_count].reshape(pair_count, 2, 2)
    pushed_logits = back[:, 0] + back[:, 1]
    image = jnp.arange(pair_count, dtype=I32)[:, None]
    own_logits = []
    for j in range(2):
        here = ((ints[1:2] == image) & (ints[2:3] == j))[:, None, :]
        own_logits.append(jnp.sum(jnp.where(here, logits[None], 0.0), axis=-1))
    return (jnp.stack(own_logits + [pushed_logits]), grad_part)


def solution(mesh):
    return jax.shard_map(
        local,
        mesh=mesh,
        in_specs=(
            P("dp", None, None),
            P("dp", None, None),
            P("dp"),
            P("dp"),
            P(None, "mp"),
            P(None, None, "mp"),
            P("mp", None),
            P(),
            P(),
        ),
        out_specs=(P(None, "dp", None), P(None, "dp", "mp")),
        check_vma=False,
    )
```

```python
import functools

import jax
import jax.numpy as jnp
from jax import lax
from jax.experimental import pallas as pl
from jax.experimental.pallas import tpu as pltpu
from jax.sharding import PartitionSpec as P

HEADS = 12
EPS = 1e-06
CE = 2
SB = 32
WIN = 16
LANES = 256
NZ, NX, NC = 8, 4, 2
GATHERED = 11
BF16 = jnp.bfloat16
F32 = jnp.float32
I32 = jnp.int32


def dot(a, b):
    return jnp.dot(a, b, preferred_element_type=F32)


def dot_nt(a, b):
    return lax.dot_general(a, b, (((1,), (1,)), ((), ())), preferred_element_type=F32)


def dot_tn(a, b):
    return lax.dot_general(a, b, (((0,), (0,)), ((), ())), preferred_element_type=F32)


def iota(shape, axis):
    return lax.broadcasted_iota(I32, shape, axis)


def head_blocks(rows, heads, head):
    lane_head = iota(rows.shape, 1) // head
    zero = jnp.zeros_like(rows)
    return jnp.concatenate([jnp.where(lane_head == h, rows, zero) for h in range(heads)], axis=0)


def head_sum(values, head):
    width = values.shape[-1]
    same = iota((width, width), 0) // head == iota((width, width), 1) // head
    ones = jnp.where(same, 1.0, 0.0).astype(BF16)
    upper = values.astype(BF16)
    lower = (values - upper.astype(F32)).astype(BF16)
    return dot(upper, ones) + dot(lower, ones)


def plan_kernel(dp_ref, mine_in, other_in, neg_ref, ints_out, sign_out, hit_out, held, sems):
    images = neg_ref.shape[0]
    copies = [
        pltpu.make_async_copy(
            source.at[:, source.shape[1] - 1, :, pl.ds(0, 128)], held.at[j], sems.at[j]
        )
        for j, source in enumerate((mine_in, other_in))
    ]
    for copy in copies:
        copy.start()
    total = hit_out.shape[0]
    slots = ints_out.shape[1]
    dp = dp_ref[0]
    z, x, c = lax.div(dp, NX * NC), lax.rem(lax.div(dp, NC), NX), lax.rem(dp, NC)
    base = dp * images
    place = iota((total, 1), 0)

    def digit(value, by, size):
        return lax.rem(lax.div(value, jnp.full_like(value, by)), jnp.full_like(value, size))

    def ahead(start, steps, size):
        to = start + steps
        return jnp.where(to >= size, to - size, to)

    block = ahead(z, digit(place, images * NX, NZ), NZ) * NX
    block = (block + ahead(x, digit(place, images, NX), NX)) * NC
    block = block + ahead(c, digit(place, images * NX * NZ, NC), NC)
    number = block * images + digit(place, 1, images)
    for copy in copies:
        copy.wait()
    ids = held[...].astype(F32).reshape(total, 128)
    ids = (ids[:, :1] * 32 + ids[:, 1:2]).astype(I32)
    own = (ids - base) == iota((total, images), 1)
    ones = jnp.where(own, 1.0, 0.0)
    below = jnp.where(iota((128, 128), 0) >= iota((128, 128), 1), 1.0, 0.0).astype(BF16)
    count_row = jnp.zeros((1, images), F32)
    upto = []
    for j in range(total // 128):
        piece = ones[128 * j : 128 * (j + 1)]
        upto.append(dot(below, piece.astype(BF16)) + count_row)
        count_row = count_row + jnp.sum(piece, axis=0, keepdims=True)
    upto = jnp.concatenate(upto, axis=0)
    diagonal = iota((images, images), 0) == iota((images, images), 1)
    count_col = jnp.sum(jnp.where(diagonal, count_row, 0.0), axis=1, keepdims=True)

    def chunks_of(count):
        return lax.div(count.astype(I32) + (2 + CE - 1), jnp.full(count.shape, CE, I32))

    chunks_row, chunks_col = chunks_of(count_row), chunks_of(count_col)
    before = iota((images, images), 0) < iota((images, images), 1)
    after = iota((images, images), 0) > iota((images, images), 1)
    first_row = jnp.sum(jnp.where(before, chunks_col, 0), axis=0, keepdims=True)
    first_col = jnp.sum(jnp.where(after, chunks_row, 0), axis=1, keepdims=True)
    n_chunks = jnp.sum(chunks_row, axis=1, keepdims=True)
    slot_of = jnp.sum(
        jnp.where(own, (first_row * CE + 1).astype(F32) + upto, 0.0), axis=1, keepdims=True
    ).astype(I32)
    slot = iota((1, slots), 1)
    chunk = lax.div(slot, jnp.full(slot.shape, CE, I32))
    img = jnp.sum(jnp.where(chunk >= first_col, 1, 0), axis=0, keepdims=True) - 1
    at_img = img == iota((images, slots), 0)
    pos = slot - CE * jnp.sum(jnp.where(at_img, first_col, 0), axis=0, keepdims=True)
    negative = jnp.sum(jnp.where(at_img, neg_ref[...], 0), axis=0, keepdims=True)
    hit = (slot_of == slot) & (pos >= 2)
    pushed = jnp.sum(jnp.where(hit, number + 1, 0), axis=0, keepdims=True)
    used = (chunk < n_chunks) & ((pos < 2) | (pushed > 0))
    cap = jnp.where(pos == 0, base + img, jnp.where(pos == 1, negative, pushed - 1))
    local = digit(cap, 1, images)
    block = digit(cap, images, total)
    by_z = digit(block, NX * NC, NZ) - z
    by_x = digit(block, NC, NX) - x
    by_z = jnp.where(by_z < 0, by_z + NZ, by_z)
    by_x = jnp.where(by_x < 0, by_x + NX, by_x)
    gathered = local < GATHERED
    carried = (by_z * NX + by_x) * (images - GATHERED + 1) + local - GATHERED
    unit = jnp.where(gathered, block * GATHERED + local, carried)
    kind = jnp.where(gathered, 0, jnp.where(digit(block, 1, NC) == c, 1, 2))
    unit = jnp.where(used, unit, 0)
    kind = jnp.where(used, kind, 0)
    most = jnp.max(count_row, axis=1, keepdims=True).astype(I32) + 2
    row = iota((8, slots), 0)
    lane = iota((images, slots), 0) == iota((images, slots), 1)
    start = jnp.sum(jnp.where(lane, first_col * CE, 0), axis=0, keepdims=True)
    count = jnp.sum(jnp.where(lane, count_col.astype(I32) + 2, 0), axis=0, keepdims=True)
    ints = n_chunks
    for at, values in enumerate((unit, img, pos, n_chunks, start, count, kind, most)):
        ints = jnp.where(row == at, values, ints)
    ints_out[...] = ints
    sign_out[...] = jnp.zeros_like(sign_out)
    sign_out[:, :slots] = jnp.where(used, jnp.where(pos == 0, -1.0, 1.0), 0.0)
    chips = total // images // NC
    half = digit(place, images * chips, NC)
    number = digit(place, images, chips) * NC + ahead(c, half, NC)
    number = number * images + digit(place, 1, images)
    home = (number == cap) & used & (pos >= 2)
    hit_out[...] = jnp.where(home, 1.0, 0.0).astype(BF16)


def blocks_of(ints):
    return lax.div(ints[3, 0] * CE + (SB - 1), SB)


def windows(ints, images, rows, act, extra_first):
    def extra():
        def one(img, carry):
            count = ints[5, img]

            def more(w, carry):
                at = pl.multiple_of((ints[4, img] + w * WIN) * rows, CE * rows)
                act(img, at, (count - w * WIN) * rows, False)
                return carry

            return lax.fori_loop(1, lax.div(count + (WIN - 1), WIN), more, carry)

        @pl.when(ints[7, 0] > WIN)
        def _():
            lax.fori_loop(0, images, one, 0)

    if extra_first:
        extra()
    for img in range(images):
        at = pl.multiple_of(ints[4, img] * rows, CE * rows)
        act(img, at, ints[5, img] * rows, True)
    if not extra_first:
        extra()


def block_rows(blk, size):
    return pl.ds(pl.multiple_of(blk * size, size), size)


def project_kernel(core, flat_in, first_in, second_in, *rest, shards, cols, vis, out_rows):
    got, swap = rest[: shards - 1], rest[shards - 1 : 2 * shards - 2]
    k_out, v_out, wq_out, wo_out, spread_out = rest[2 * shards - 2 : 2 * shards + 3]
    flat, first, second, k, v, spread, sems, sem_o = rest[2 * shards + 3 :]
    count = flat.shape[0]
    side = core[0]
    pltpu.make_async_copy(flat_in, flat, sems.at[0]).start()
    own = pl.ds(0, cols)

    def landing(j, s):
        return (first, second)[j].at[s, own], sems.at[1 + 2 * s + j]

    for j, source in enumerate((first_in, second_in)):
        pltpu.make_async_copy(source, *landing(j, 0)).start()
    for s in range(1, shards):
        for j in range(NC):

            @pl.when(side == j)
            def _():
                pltpu.make_async_copy(got[s - 1], *landing(j, s)).start()

            @pl.when(side != j)
            def _():
                pltpu.make_async_copy(swap[s - 1], *landing(j, s)).start()

    pad = jnp.zeros((LANES - cols, first.shape[2]), BF16)
    for s in range(shards):
        first[s, cols:, :] = pad
        second[s, cols:, :] = pad
    pltpu.make_async_copy(flat_in, flat, sems.at[0]).wait()
    leaving = []

    def leave(source, target):
        copy = pltpu.make_async_copy(source, target, sem_o.at[len(leaving)])
        copy.start()
        leaving.append(copy)

    step = vis // NZ
    slot = spread.shape[0] // (NZ * NX * NC)
    half = spread.shape[0] // NC
    for z in range(NZ):
        low = step * z // 128 * 128
        window = -(-(step * z + step - low) // 128) * 128
        row, lane = iota((NX * NC * slot, window), 0), iota((NX * NC * slot, window), 1)
        inner = row % slot
        kind = (row // (NX * slot) + side) % NC
        goal = (row // slot % NX * NC + kind) * out_rows + inner + (step * z - low)
        chosen = jnp.where((lane == goal) & (inner < out_rows), 1.0, 0.0).astype(BF16)
        moved = dot_nt(chosen, flat[:, low : low + window]).astype(BF16)
        for c in range(NC):
            part = slice(c * half + z * NX * slot, c * half + (z + 1) * NX * slot)
            spread[part, :] = moved[c * NX * slot : (c + 1) * NX * slot]
    leave(spread, spread_out)
    for s in range(shards):
        lanes = slice(s * LANES, (s + 1) * LANES)
        for j, (held, kept, out, other) in enumerate(
            ((first, k, k_out, wq_out), (second, v, v_out, wo_out))
        ):
            pltpu.make_async_copy(first_in, *landing(j, s)).wait()
            leave(held.at[s, :, pl.ds(vis, held.shape[2] - vis)], other.at[pl.ds(s * LANES, LANES)])
            for n in range(0, count, 512):
                kept[n : n + 512, lanes] = dot_nt(flat[n : n + 512], held[s, :, :vis]).astype(BF16)
            leave(kept.at[:, pl.ds(s * LANES, LANES)], out.at[:, pl.ds(s * LANES, LANES)])
    for copy in leaving:
        copy.wait()


def forward_kernel(
    ints, pool, carried, carried_other, wq_in, k_in, v_in, wo_in, const_ref, q_out, p_out, d_out, log_out,
    xbuf, wq, k, v, wo, q, p, half, mixed, d_res, logs, sem_x, sem_w, sem_o, *, head, scale,
):
    width = wo.shape[1]
    shards = wq.shape[0] // LANES
    heads = HEADS // shards
    cols = heads * head
    images = k.shape[0] // head
    rows = xbuf.shape[1] // 2
    size = SB * rows
    win = WIN * rows
    blocks = blocks_of(ints)
    weights = [
        pltpu.make_async_copy(src, dst, sem_w.at[j])
        for j, (src, dst) in enumerate(((wq_in, wq), (k_in, k), (v_in, v), (wo_in, wo)))
    ]
    for copy in weights:
        copy.start()

    def fetch(blk):
        def one(j, carry):
            slot = blk * SB + j
            for at, source in enumerate((pool, carried, carried_other)):

                @pl.when(ints[6, slot] == at)
                def _():
                    pltpu.make_async_copy(
                        source.at[ints[0, slot]], xbuf.at[slot], sem_x.at[blk]
                    ).start()

            return carry

        lax.fori_loop(0, SB, one, 0, unroll=4)

    def fetched(blk):
        here = xbuf.at[block_rows(blk, SB)]
        pltpu.make_async_copy(pool.at[pl.ds(0, SB)], here, sem_x.at[blk]).wait()

    def results(blk, s):
        at = block_rows(blk, size)
        return [
            pltpu.make_async_copy(q.at[s, at], q_out.at[s, at], sem_o.at[0]),
            pltpu.make_async_copy(p.at[s, at], p_out.at[s, at], sem_o.at[1]),
        ]

    def gradient(blk):
        at = block_rows(blk, size)
        return pltpu.make_async_copy(d_res.at[at], d_out.at[at], sem_o.at[2])

    def loop(body):
        def one(blk, carry):
            body(blk)
            return carry

        lax.fori_loop(0, blocks, one, 0)

    loop(fetch)
    weights[0].wait()

    def take(blk):
        x16 = xbuf[block_rows(blk, SB)].astype(F32)
        return jnp.concatenate([x16[:, :rows], x16[:, rows:]], axis=-1).reshape(size, width)

    def queries(blk):
        fetched(blk)
        got = (dot_nt(take(blk).astype(BF16), wq[...]) * scale).astype(BF16)
        for s in range(shards):
            q[s, block_rows(blk, size), :] = got[:, s * LANES : (s + 1) * LANES]

    loop(queries)
    weights[1].wait()

    def score(img, at, count, first):
        for s in range(shards):
            keys = k[pl.ds(img * head, head), s * LANES : (s + 1) * LANES]
            p[s, pl.ds(at, win), :cols] = dot_nt(
                q[s, pl.ds(at, win), :], head_blocks(keys, heads, head)
            )

    windows(ints, images, rows, score, True)

    def soften(blk):
        at = block_rows(blk, size)
        for s in range(shards):
            raised = jnp.exp(p[s, at, :cols])
            prob = raised / head_sum(raised, head)
            p[s, at, :cols] = prob
            half[s, at, :cols] = prob.astype(BF16)
            for copy in results(blk, s):
                copy.start()

    loop(soften)
    weights[2].wait()

    def mix(img, at, count, first):
        for s in range(shards):
            lanes = slice(s * LANES, (s + 1) * LANES)
            vals = head_blocks(v[pl.ds(img * head, head), lanes], heads, head)
            mixed[pl.ds(at, win), lanes] = dot(half[s, pl.ds(at, win), :cols], vals).astype(BF16)

    windows(ints, images, rows, mix, True)
    weights[3].wait()
    scaled = const_ref[1:2]
    flat = scaled - jnp.mean(scaled, axis=-1, keepdims=True)

    def finish(blk):
        at = block_rows(blk, size)
        residual = take(blk) + dot(mixed[at, :], wo[...])
        centred = residual - jnp.mean(residual, axis=-1, keepdims=True)
        variance = jnp.mean(centred * centred, axis=-1, keepdims=True)
        inverse = 1.0 / jnp.sqrt(variance + EPS)
        unit = centred * inverse
        none = jnp.sum(unit * const_ref[0:1], axis=-1, keepdims=True)
        gap = jnp.sum(unit * scaled, axis=-1, keepdims=True)
        both = jnp.where(iota((size, 128), 1) == 0, none, none + gap)
        logs[block_rows(blk, SB), :] = jnp.sum(both.reshape(SB, rows, 128), axis=1)
        d_res[at, :] = (inverse * (flat - unit * (gap / width))).astype(BF16)
        gradient(blk).start()

    loop(finish)
    log_out[...] = logs[...].T[: log_out.shape[0]]

    def settle(blk):
        for s in range(shards):
            for copy in results(blk, s):
                copy.wait()
        gradient(blk).wait()

    loop(settle)


def backward_kernel(
    ints, sign_ref, *rest, mine, arrivals, head, heads, rows, terms
):
    parts, rest = rest[:terms], rest[terms:]
    d_in, wo_in, v_in, p_in, q_in = rest[:5]
    arrived, rest = rest[5 : 5 + arrivals], rest[5 + arrivals :]
    outs, rest = rest[: len(mine)], rest[len(mine) :]
    d_res, wo, v, p, q, dm, d_att, ds, pd, acc, delta, sems, sem_d = rest
    cols = heads * head
    images = v.shape[1] // head
    size = SB * rows
    win = WIN * rows
    blocks = blocks_of(ints)
    used = pl.ds(0, q.shape[1] - win)

    def loop(body):
        def one(blk, carry):
            body(blk)
            return carry

        lax.fori_loop(0, blocks, one, 0)

    def arrival(blk):
        at = block_rows(blk, size)
        return pltpu.make_async_copy(d_in.at[at], d_res.at[at], sem_d.at[blk])

    loop(lambda blk: arrival(blk).start())
    copies = []
    for j, shard in enumerate(mine):
        lanes = pl.ds(shard * LANES, LANES)
        copies.append(
            [
                pltpu.make_async_copy(src, dst, sems.at[4 * j + n])
                for n, (src, dst) in enumerate(
                    (
                        (wo_in.at[lanes, :], wo.at[j]),
                        (v_in.at[:, lanes], v.at[j]),
                        (p_in.at[shard], p.at[j]),
                        (q_in.at[shard], q.at[j, used]),
                    )
                )
            ]
        )
    for n in range(4):
        for group in copies:
            group[n].start()

    def settle(n):
        for group in copies:
            group[n].wait()

    logits = sum(part[...] for part in parts[1:]) + parts[0][...]
    sign = sign_ref[...]
    factor = sign / (1.0 + jnp.exp(sign * (logits[0:1] - logits[1:2])))
    delta[...] = jnp.broadcast_to(factor, (128, factor.shape[1])).T
    tail = pl.ds(pl.multiple_of(blocks * size, size), win)
    for j in range(len(mine)):
        dm[j, tail, :] = jnp.zeros((win, LANES), BF16)
    settle(0)

    def carry_back(blk):
        at = block_rows(blk, size)
        arrival(blk).wait()
        for j in range(len(mine)):
            dm[j, at, :] = dot_nt(d_res[at, :], wo[j]).astype(BF16)

    loop(carry_back)
    settle(1)

    def attend(img, at, count, first):
        for j in range(len(mine)):
            vals = head_blocks(v[j, pl.ds(img * head, head), :], heads, head)
            d_att[j, pl.ds(at, win), :cols] = dot_nt(dm[j, pl.ds(at, win), :], vals)

    windows(ints, images, rows, attend, True)
    settle(2)

    def soften(blk):
        at = block_rows(blk, size)
        weight = delta[block_rows(blk, SB), :]
        weight = jnp.broadcast_to(weight[:, None, :], (SB, rows, 128)).reshape(size, 128)[:, :1]
        for j in range(len(mine)):
            prob = p[j, at, :cols]
            grad = d_att[j, at, :cols]
            inner = head_sum(grad * prob, head)
            weighted = prob * weight
            ds[j, at, :cols] = (weighted * (grad - inner)).astype(BF16)
            pd[j, at, :cols] = weighted.astype(BF16)

    loop(soften)
    settle(3)
    for j in range(len(mine)):
        q[j, tail, :] = jnp.zeros((win, LANES), BF16)
    lane_head = iota((head, LANES), 1) // head
    place = iota((win, cols), 0)

    def diagonal(block):
        total = block[:head]
        for h in range(1, heads):
            total = jnp.where(lane_head == h, block[h * head : (h + 1) * head], total)
        return total[:, :cols]

    def outer(img, at, count, first):
        own = place < count
        here = pl.ds(at, win)
        zero = jnp.zeros((win, cols), BF16)
        for j in range(len(mine)):
            dk = diagonal(dot_tn(jnp.where(own, ds[j, here, :cols], zero), q[j, here, :]))
            dv = diagonal(dot_tn(jnp.where(own, pd[j, here, :cols], zero), dm[j, here, :]))
            term = jnp.concatenate([dk, dv], axis=-1)
            if first:
                acc[j, img * head : (img + 1) * head, :] = term
            else:
                acc[j, pl.ds(pl.multiple_of(img * head, head), head), :] += term

    windows(ints, images, rows, outer, False)
    for j, out_ref in enumerate(outs):
        total = acc[j]
        for a in arrived:
            total = total + a[...].astype(F32)
        out_ref[...] = total.astype(out_ref.dtype)


def whole(a):
    return pl.BlockSpec(a.shape, lambda *_: (0,) * a.ndim)


def local(
    images, query_states, neg_caption, neg_image, cross_query, cross_kv, cross_out, norm_gain,
    itm_weight,
):
    pair_count, patches, vis = images.shape
    queries, width = query_states.shape[1:]
    cols = cross_query.shape[1]
    head = width // HEADS
    scale = 1.0 / head**0.5
    groups = lax.axis_size("dp")
    shards = lax.axis_size("mp")
    dp, mp = lax.axis_index("dp"), lax.axis_index("mp")
    core = dp % NC
    rows = queries // shards
    half = width // 2

    def around(x, by):
        return lax.ppermute(x, "mp", [(i, (i + by) % shards) for i in range(shards)])

    def shift(x, by_z, by_x, by_core):
        moves = []
        for i in range(groups):
            z, x_, c = i // (NX * NC), i // NC % NX, i % NC
            to = ((z + by_z) % NZ * NX + (x_ + by_x) % NX) * NC + (c + by_core) % NC
            moves.append((i, to))
        return lax.ppermute(x, "dp", moves)

    own_rows = lax.dynamic_slice_in_dim(query_states, mp * rows, rows, 1)
    packed = jnp.concatenate([own_rows[:, :, :half], own_rows[:, :, half:]], axis=1)
    pool = lax.all_gather(packed[:GATHERED], "dp", axis=0, tiled=True)
    halves = [
        jnp.concatenate([cross_kv[0].T, cross_query.T], axis=1),
        jnp.concatenate([cross_kv[1].T, cross_out], axis=1),
    ]
    brought = jnp.where(core == 0, halves[0], halves[1])
    got = [around(brought, shards - s) for s in range(1, shards)]
    number = jnp.stack([neg_image // 32, neg_image % 32], axis=-1).astype(BF16)
    number = jnp.pad(number, ((0, 2 * rows - pair_count), (0, half - 2)))
    part = jnp.concatenate([packed[GATHERED:], number[None]], axis=0)
    units = part.shape[0]
    line = jnp.concatenate([part] + [shift(part, 0, -d, 0) for d in range(1, NX)], axis=0)
    up, down = [line], [line]
    for step in range(NZ // 2 - 1):
        if step == 2:
            up[-1], down[-1], *got[:2] = lax.optimization_barrier((up[-1], down[-1], *got[:2]))
        up.append(shift(up[-1], -1, 0, 0))
        down.append(shift(down[-1], 1, 0, 0))
    up[-1], down[-1], got[2] = lax.optimization_barrier((up[-1], down[-1], got[2]))
    cut = NX // 2 * units
    across = [shift(up[-1][:cut], -1, 0, 0), shift(down[-1][cut:], 1, 0, 0)]
    carried = jnp.concatenate(up + across + down[:0:-1], axis=0)
    carried_other = shift(carried, 0, 0, 1)
    numbers = [x.reshape(-1, units, 2 * rows, half) for x in (carried, carried_other)]

    swap = [shift(g, 0, 0, 1) for g in got]
    flat = images.reshape(pair_count * patches, vis)
    params = pltpu.CompilerParams(vmem_limit_bytes=56 * 2**20)
    smem = pl.BlockSpec(memory_space=pltpu.SMEM)
    anywhere = pl.BlockSpec(memory_space=pl.ANY)
    vmem = pl.BlockSpec(memory_space=pltpu.VMEM)
    tall = shards * LANES
    out_rows = vis // groups
    pad_rows = (out_rows + 1 + 7) // 8 * 8
    chips = groups // NC
    shapes = [
        (pair_count * patches, tall), (pair_count * patches, tall), (tall, width), (tall, width),
        (groups * pad_rows, pair_count * patches),
    ]
    keys, values, wq, wo, spread = pl.pallas_call(
        functools.partial(project_kernel, shards=shards, cols=cols, vis=vis, out_rows=out_rows),
        in_specs=[smem] + [anywhere] * (1 + 2 * shards),
        out_specs=[anywhere] * 5,
        scratch_shapes=[
            pltpu.VMEM(flat.shape, BF16),
            pltpu.VMEM((shards, LANES, vis + width), BF16),
            pltpu.VMEM((shards, LANES, vis + width), BF16),
            pltpu.VMEM(shapes[0], BF16),
            pltpu.VMEM(shapes[1], BF16),
            pltpu.VMEM(shapes[4], BF16),
            pltpu.SemaphoreType.DMA((1 + 2 * shards,)),
            pltpu.SemaphoreType.DMA((1 + 4 * shards,)),
        ],
        out_shape=[jax.ShapeDtypeStruct(shape, BF16) for shape in shapes],
        compiler_params=params,
        cost_estimate=pl.CostEstimate(
            flops=4 * 10**10, bytes_accessed=20 * 10**6, transcendentals=0
        ),
        name="project",
    )(core.astype(I32).reshape(1), flat, *halves, *got, *swap)

    most = pair_count * (2 + CE - 1) + 2 * groups
    n_slots = -(-(most + WIN - CE) // SB) * SB
    n_rows = n_slots * rows
    n_lanes = -(-n_slots // 128) * 128
    ints, sign, hit = pl.pallas_call(
        plan_kernel,
        in_specs=[
            smem, anywhere, anywhere, vmem,
        ],
        out_specs=[vmem] * 3,
        scratch_shapes=[
            pltpu.VMEM((NC, groups // NC, 2 * rows, 128), BF16),
            pltpu.SemaphoreType.DMA((NC,)),
        ],
        out_shape=[
            jax.ShapeDtypeStruct((8, n_slots), I32),
            jax.ShapeDtypeStruct((1, n_lanes), F32),
            jax.ShapeDtypeStruct((groups * pair_count, n_slots), BF16),
        ],
        compiler_params=params,
        name="plan",
    )(dp.astype(I32).reshape(1), *numbers, neg_caption.reshape(-1, 1))

    fold = norm_gain / queries
    const = jnp.stack([fold * itm_weight[:, 0], fold * (itm_weight[:, 1] - itm_weight[:, 0])])
    q_rows, prob, d_res, log_part = pl.pallas_call(
        functools.partial(forward_kernel, head=head, scale=scale),
        in_specs=[smem] + [anywhere] * 7 + [vmem],
        out_specs=[anywhere] * 3 + [vmem],
        scratch_shapes=[
            pltpu.VMEM((n_slots, 2 * rows, half), BF16),
            pltpu.VMEM(wq.shape, BF16),
            pltpu.VMEM(keys.shape, BF16),
            pltpu.VMEM(values.shape, BF16),
            pltpu.VMEM(wo.shape, BF16),
            pltpu.VMEM((shards, n_rows, LANES), BF16),
            pltpu.VMEM((shards, n_rows, LANES), F32),
            pltpu.VMEM((shards, n_rows, LANES), BF16),
            pltpu.VMEM((n_rows, shards * LANES), BF16),
            pltpu.VMEM((n_rows, width), BF16),
            pltpu.VMEM((n_lanes, 128), F32),
            pltpu.SemaphoreType.DMA((n_slots // SB,)),
            pltpu.SemaphoreType.DMA((4,)),
            pltpu.SemaphoreType.DMA((3,)),
        ],
        out_shape=[
            jax.ShapeDtypeStruct((shards, n_rows, LANES), BF16),
            jax.ShapeDtypeStruct((shards, n_rows, LANES), F32),
            jax.ShapeDtypeStruct((n_rows, width), BF16),
            jax.ShapeDtypeStruct((8, n_lanes), F32),
        ],
        compiler_params=params,
        name="forward",
    )(ints, pool, carried, carried_other, wq, keys, values, wo, const)

    parts = [log_part] + [around(log_part, shards - s) for s in range(1, shards)]
    logits = jnp.zeros((2, n_slots), F32)
    for m in range(shards):
        for s in range(shards):
            logits = logits + jnp.where((mp + s) % shards == m, parts[s][:2, :n_slots], 0.0)
    logits = jnp.where(sign[:, :n_slots] != 0.0, logits, 0.0)

    def backward(mine, arrived=(), kind=BF16):
        shape = (pair_count * patches, 2 * cols)
        slack = n_rows + WIN * rows
        n = len(mine)
        return pl.pallas_call(
            functools.partial(
                backward_kernel, mine=mine, arrivals=len(arrived), head=head,
                heads=HEADS // shards, rows=rows, terms=shards,
            ),
            in_specs=[smem] + [vmem] * (1 + shards) + [anywhere] * 5 + [vmem] * len(arrived),
            out_specs=[vmem] * n,
            scratch_shapes=[
                pltpu.VMEM((n_rows, width), BF16),
                pltpu.VMEM((n, LANES, width), BF16),
                pltpu.VMEM((n, pair_count * patches, LANES), BF16),
                pltpu.VMEM((n, n_rows, LANES), F32),
                pltpu.VMEM((n, slack, LANES), BF16),
                pltpu.VMEM((n, slack, LANES), BF16),
                pltpu.VMEM((n, slack, LANES), F32),
                pltpu.VMEM((n, slack, LANES), BF16),
                pltpu.VMEM((n, slack, LANES), BF16),
                pltpu.VMEM((n,) + shape, F32),
                pltpu.VMEM((n_lanes, 128), F32),
                pltpu.SemaphoreType.DMA((4 * n,)),
                pltpu.SemaphoreType.DMA((n_slots // SB,)),
            ],
            out_shape=[jax.ShapeDtypeStruct(shape, kind)] * n,
            compiler_params=params,
            cost_estimate=pl.CostEstimate(flops=10**6, bytes_accessed=10**4, transcendentals=0),
            name="backward",
        )(ints, sign, *parts, d_res, wo, values, prob, q_rows, *arrived)

    two = around(backward((2,))[0], 2)
    one, three = backward((1, 3))
    one, three = around(one, 1), around(three, 3)
    own = backward((0,), (two,), F32)[0]
    d_kv = (own + one.astype(F32) + three.astype(F32)).astype(BF16)

    logit_hi = logits.astype(BF16)
    logit_lo = (logits - logit_hi.astype(F32)).astype(BF16)
    four = jnp.concatenate([logit_hi, logit_lo], axis=0)
    home = dot_nt(hit, four).astype(BF16)
    home = jnp.pad(
        home.reshape(groups, 1, 4 * pair_count),
        ((0, 0), (out_rows, pad_rows - out_rows - 1), (0, 2 * cols - 4 * pair_count)),
    )
    home, d_kv = lax.optimization_barrier((home, d_kv))
    grad = dot(spread, d_kv).reshape(groups, pad_rows, 2 * cols)
    over = shift((grad[chips:] + home[chips:]).astype(BF16), 0, 0, 1)
    leaving = (grad[:chips] + home[:chips] + over).astype(BF16)
    alike = [[chip * NC + c for chip in range(chips)] for c in range(NC)]
    arrived = lax.all_to_all(
        leaving, "dp", split_axis=0, concat_axis=0, tiled=True, axis_index_groups=alike
    )
    summed = jnp.sum(arrived.astype(F32), axis=0)
    grad_part = jnp.transpose(summed[:out_rows].reshape(out_rows, 2, cols), (1, 0, 2))
    back = summed[out_rows, : 4 * pair_count].reshape(pair_count, 2, 2)
    pushed_logits = back[:, 0] + back[:, 1]
    image = jnp.arange(pair_count, dtype=I32)[:, None]
    own_logits = []
    for j in range(2):
        here = ((ints[1:2] == image) & (ints[2:3] == j))[:, None, :]
        own_logits.append(jnp.sum(jnp.where(here, logits[None], 0.0), axis=-1))
    return (jnp.stack(own_logits + [pushed_logits]), grad_part)


def solution(mesh):
    return jax.shard_map(
        local,
        mesh=mesh,
        in_specs=(
            P("dp", None, None),
            P("dp", None, None),
            P("dp"),
            P("dp"),
            P(None, "mp"),
            P(None, None, "mp"),
            P("mp", None),
            P(),
            P(),
        ),
        out_specs=(P(None, "dp", None), P(None, "dp", "mp")),
        check_vma=False,
    )
```

```python
import functools

import jax
import jax.numpy as jnp
from jax import lax
from jax.experimental import pallas as pl
from jax.experimental.pallas import tpu as pltpu
from jax.sharding import PartitionSpec as P

HEADS = 12
EPS = 1e-06
CE = 2
SB = 32
WIN = 16
LANES = 256
NZ, NX, NC = 8, 4, 2
GATHERED = 12
BF16 = jnp.bfloat16
F32 = jnp.float32
I32 = jnp.int32


def dot(a, b):
    return jnp.dot(a, b, preferred_element_type=F32)


def dot_nt(a, b):
    return lax.dot_general(a, b, (((1,), (1,)), ((), ())), preferred_element_type=F32)


def dot_tn(a, b):
    return lax.dot_general(a, b, (((0,), (0,)), ((), ())), preferred_element_type=F32)


def iota(shape, axis):
    return lax.broadcasted_iota(I32, shape, axis)


def head_blocks(rows, heads, head):
    lane_head = iota(rows.shape, 1) // head
    zero = jnp.zeros_like(rows)
    return jnp.concatenate([jnp.where(lane_head == h, rows, zero) for h in range(heads)], axis=0)


def head_sum(values, head):
    width = values.shape[-1]
    same = iota((width, width), 0) // head == iota((width, width), 1) // head
    ones = jnp.where(same, 1.0, 0.0).astype(BF16)
    upper = values.astype(BF16)
    lower = (values - upper.astype(F32)).astype(BF16)
    return dot(upper, ones) + dot(lower, ones)


def plan_kernel(dp_ref, mine_in, other_in, neg_ref, ints_out, sign_out, hit_out, held, sems):
    images = neg_ref.shape[0]
    copies = [
        pltpu.make_async_copy(
            source.at[:, source.shape[1] - 1, :, pl.ds(0, 128)], held.at[j], sems.at[j]
        )
        for j, source in enumerate((mine_in, other_in))
    ]
    for copy in copies:
        copy.start()
    total = hit_out.shape[0]
    slots = ints_out.shape[1]
    dp = dp_ref[0]
    z, x, c = lax.div(dp, NX * NC), lax.rem(lax.div(dp, NC), NX), lax.rem(dp, NC)
    base = dp * images
    place = iota((total, 1), 0)

    def digit(value, by, size):
        return lax.rem(lax.div(value, jnp.full_like(value, by)), jnp.full_like(value, size))

    def ahead(start, steps, size):
        to = start + steps
        return jnp.where(to >= size, to - size, to)

    block = ahead(z, digit(place, images * NX, NZ), NZ) * NX
    block = (block + ahead(x, digit(place, images, NX), NX)) * NC
    block = block + ahead(c, digit(place, images * NX * NZ, NC), NC)
    number = block * images + digit(place, 1, images)
    for copy in copies:
        copy.wait()
    ids = held[...].astype(F32).reshape(total, 128)
    ids = (ids[:, :1] * 32 + ids[:, 1:2]).astype(I32)
    own = (ids - base) == iota((total, images), 1)
    ones = jnp.where(own, 1.0, 0.0)
    below = jnp.where(iota((128, 128), 0) >= iota((128, 128), 1), 1.0, 0.0).astype(BF16)
    count_row = jnp.zeros((1, images), F32)
    upto = []
    for j in range(total // 128):
        piece = ones[128 * j : 128 * (j + 1)]
        upto.append(dot(below, piece.astype(BF16)) + count_row)
        count_row = count_row + jnp.sum(piece, axis=0, keepdims=True)
    upto = jnp.concatenate(upto, axis=0)
    diagonal = iota((images, images), 0) == iota((images, images), 1)
    count_col = jnp.sum(jnp.where(diagonal, count_row, 0.0), axis=1, keepdims=True)

    def chunks_of(count):
        return lax.div(count.astype(I32) + (2 + CE - 1), jnp.full(count.shape, CE, I32))

    chunks_row, chunks_col = chunks_of(count_row), chunks_of(count_col)
    before = iota((images, images), 0) < iota((images, images), 1)
    after = iota((images, images), 0) > iota((images, images), 1)
    first_row = jnp.sum(jnp.where(before, chunks_col, 0), axis=0, keepdims=True)
    first_col = jnp.sum(jnp.where(after, chunks_row, 0), axis=1, keepdims=True)
    n_chunks = jnp.sum(chunks_row, axis=1, keepdims=True)
    slot_of = jnp.sum(
        jnp.where(own, (first_row * CE + 1).astype(F32) + upto, 0.0), axis=1, keepdims=True
    ).astype(I32)
    slot = iota((1, slots), 1)
    chunk = lax.div(slot, jnp.full(slot.shape, CE, I32))
    img = jnp.sum(jnp.where(chunk >= first_col, 1, 0), axis=0, keepdims=True) - 1
    at_img = img == iota((images, slots), 0)
    pos = slot - CE * jnp.sum(jnp.where(at_img, first_col, 0), axis=0, keepdims=True)
    negative = jnp.sum(jnp.where(at_img, neg_ref[...], 0), axis=0, keepdims=True)
    hit = (slot_of == slot) & (pos >= 2)
    pushed = jnp.sum(jnp.where(hit, number + 1, 0), axis=0, keepdims=True)
    used = (chunk < n_chunks) & ((pos < 2) | (pushed > 0))
    cap = jnp.where(pos == 0, base + img, jnp.where(pos == 1, negative, pushed - 1))
    local = digit(cap, 1, images)
    block = digit(cap, images, total)
    by_z = digit(block, NX * NC, NZ) - z
    by_x = digit(block, NC, NX) - x
    by_z = jnp.where(by_z < 0, by_z + NZ, by_z)
    by_x = jnp.where(by_x < 0, by_x + NX, by_x)
    gathered = local < GATHERED
    carried = (by_z * NX + by_x) * (images - GATHERED + 1) + local - GATHERED
    unit = jnp.where(gathered, block * GATHERED + local, carried)
    kind = jnp.where(gathered, 0, jnp.where(digit(block, 1, NC) == c, 1, 2))
    unit = jnp.where(used, unit, 0)
    kind = jnp.where(used, kind, 0)
    most = jnp.max(count_row, axis=1, keepdims=True).astype(I32) + 2
    row = iota((8, slots), 0)
    lane = iota((images, slots), 0) == iota((images, slots), 1)
    start = jnp.sum(jnp.where(lane, first_col * CE, 0), axis=0, keepdims=True)
    count = jnp.sum(jnp.where(lane, count_col.astype(I32) + 2, 0), axis=0, keepdims=True)
    ints = n_chunks
    for at, values in enumerate((unit, img, pos, n_chunks, start, count, kind, most)):
        ints = jnp.where(row == at, values, ints)
    ints_out[...] = ints
    sign_out[...] = jnp.zeros_like(sign_out)
    sign_out[:, :slots] = jnp.where(used, jnp.where(pos == 0, -1.0, 1.0), 0.0)
    chips = total // images // NC
    half = digit(place, images * chips, NC)
    number = digit(place, images, chips) * NC + ahead(c, half, NC)
    number = number * images + digit(place, 1, images)
    home = (number == cap) & used & (pos >= 2)
    hit_out[...] = jnp.where(home, 1.0, 0.0).astype(BF16)


def blocks_of(ints):
    return lax.div(ints[3, 0] * CE + (SB - 1), SB)


def windows(ints, images, rows, act, extra_first):
    def extra():
        def one(img, carry):
            count = ints[5, img]

            def more(w, carry):
                at = pl.multiple_of((ints[4, img] + w * WIN) * rows, CE * rows)
                act(img, at, (count - w * WIN) * rows, False)
                return carry

            return lax.fori_loop(1, lax.div(count + (WIN - 1), WIN), more, carry)

        @pl.when(ints[7, 0] > WIN)
        def _():
            lax.fori_loop(0, images, one, 0)

    if extra_first:
        extra()
    for img in range(images):
        at = pl.multiple_of(ints[4, img] * rows, CE * rows)
        act(img, at, ints[5, img] * rows, True)
    if not extra_first:
        extra()


def block_rows(blk, size):
    return pl.ds(pl.multiple_of(blk * size, size), size)


def project_kernel(core, flat_in, first_in, second_in, *rest, shards, cols, vis, out_rows):
    got, swap = rest[: shards - 1], rest[shards - 1 : 2 * shards - 2]
    k_out, v_out, wq_out, wo_out, spread_out = rest[2 * shards - 2 : 2 * shards + 3]
    flat, first, second, k, v, spread, sems, sem_o = rest[2 * shards + 3 :]
    count = flat.shape[0]
    side = core[0]
    pltpu.make_async_copy(flat_in, flat, sems.at[0]).start()
    own = pl.ds(0, cols)

    def landing(j, s):
        return (first, second)[j].at[s, own], sems.at[1 + 2 * s + j]

    for j, source in enumerate((first_in, second_in)):
        pltpu.make_async_copy(source, *landing(j, 0)).start()
    for s in range(1, shards):
        for j in range(NC):

            @pl.when(side == j)
            def _():
                pltpu.make_async_copy(got[s - 1], *landing(j, s)).start()

            @pl.when(side != j)
            def _():
                pltpu.make_async_copy(swap[s - 1], *landing(j, s)).start()

    pad = jnp.zeros((LANES - cols, first.shape[2]), BF16)
    for s in range(shards):
        first[s, cols:, :] = pad
        second[s, cols:, :] = pad
    pltpu.make_async_copy(flat_in, flat, sems.at[0]).wait()
    leaving = []

    def leave(source, target):
        copy = pltpu.make_async_copy(source, target, sem_o.at[len(leaving)])
        copy.start()
        leaving.append(copy)

    step = vis // NZ
    slot = spread.shape[0] // (NZ * NX * NC)
    half = spread.shape[0] // NC
    for z in range(NZ):
        low = step * z // 128 * 128
        window = -(-(step * z + step - low) // 128) * 128
        row, lane = iota((NX * NC * slot, window), 0), iota((NX * NC * slot, window), 1)
        inner = row % slot
        kind = (row // (NX * slot) + side) % NC
        goal = (row // slot % NX * NC + kind) * out_rows + inner + (step * z - low)
        chosen = jnp.where((lane == goal) & (inner < out_rows), 1.0, 0.0).astype(BF16)
        moved = dot_nt(chosen, flat[:, low : low + window]).astype(BF16)
        for c in range(NC):
            part = slice(c * half + z * NX * slot, c * half + (z + 1) * NX * slot)
            spread[part, :] = moved[c * NX * slot : (c + 1) * NX * slot]
    leave(spread, spread_out)
    for s in range(shards):
        lanes = slice(s * LANES, (s + 1) * LANES)
        for j, (held, kept, out, other) in enumerate(
            ((first, k, k_out, wq_out), (second, v, v_out, wo_out))
        ):
            pltpu.make_async_copy(first_in, *landing(j, s)).wait()
            leave(held.at[s, :, pl.ds(vis, held.shape[2] - vis)], other.at[pl.ds(s * LANES, LANES)])
            for n in range(0, count, 512):
                kept[n : n + 512, lanes] = dot_nt(flat[n : n + 512], held[s, :, :vis]).astype(BF16)
            leave(kept.at[:, pl.ds(s * LANES, LANES)], out.at[:, pl.ds(s * LANES, LANES)])
    for copy in leaving:
        copy.wait()


def forward_kernel(
    ints, pool, carried, carried_other, wq_in, k_in, v_in, wo_in, const_ref, q_out, p_out, d_out, log_out,
    xbuf, wq, k, v, wo, q, p, half, mixed, d_res, logs, sem_x, sem_w, sem_o, *, head, scale,
):
    width = wo.shape[1]
    shards = wq.shape[0] // LANES
    heads = HEADS // shards
    cols = heads * head
    images = k.shape[0] // head
    rows = xbuf.shape[1] // 2
    size = SB * rows
    win = WIN * rows
    blocks = blocks_of(ints)
    weights = [
        pltpu.make_async_copy(src, dst, sem_w.at[j])
        for j, (src, dst) in enumerate(((wq_in, wq), (k_in, k), (v_in, v), (wo_in, wo)))
    ]
    for copy in weights:
        copy.start()

    def fetch(blk):
        def one(j, carry):
            slot = blk * SB + j
            for at, source in enumerate((pool, carried, carried_other)):

                @pl.when(ints[6, slot] == at)
                def _():
                    pltpu.make_async_copy(
                        source.at[ints[0, slot]], xbuf.at[slot], sem_x.at[blk]
                    ).start()

            return carry

        lax.fori_loop(0, SB, one, 0, unroll=4)

    def fetched(blk):
        here = xbuf.at[block_rows(blk, SB)]
        pltpu.make_async_copy(pool.at[pl.ds(0, SB)], here, sem_x.at[blk]).wait()

    def results(blk, s):
        at = block_rows(blk, size)
        return [
            pltpu.make_async_copy(q.at[s, at], q_out.at[s, at], sem_o.at[0]),
            pltpu.make_async_copy(p.at[s, at], p_out.at[s, at], sem_o.at[1]),
        ]

    def gradient(blk):
        at = block_rows(blk, size)
        return pltpu.make_async_copy(d_res.at[at], d_out.at[at], sem_o.at[2])

    def loop(body):
        def one(blk, carry):
            body(blk)
            return carry

        lax.fori_loop(0, blocks, one, 0)

    loop(fetch)
    weights[0].wait()

    def take(blk):
        x16 = xbuf[block_rows(blk, SB)].astype(F32)
        return jnp.concatenate([x16[:, :rows], x16[:, rows:]], axis=-1).reshape(size, width)

    def queries(blk):
        fetched(blk)
        got = (dot_nt(take(blk).astype(BF16), wq[...]) * scale).astype(BF16)
        for s in range(shards):
            q[s, block_rows(blk, size), :] = got[:, s * LANES : (s + 1) * LANES]

    loop(queries)
    weights[1].wait()

    def score(img, at, count, first):
        for s in range(shards):
            keys = k[pl.ds(img * head, head), s * LANES : (s + 1) * LANES]
            p[s, pl.ds(at, win), :cols] = dot_nt(
                q[s, pl.ds(at, win), :], head_blocks(keys, heads, head)
            )

    windows(ints, images, rows, score, True)

    def soften(blk):
        at = block_rows(blk, size)
        for s in range(shards):
            raised = jnp.exp(p[s, at, :cols])
            prob = raised / head_sum(raised, head)
            p[s, at, :cols] = prob
            half[s, at, :cols] = prob.astype(BF16)
            for copy in results(blk, s):
                copy.start()

    loop(soften)
    weights[2].wait()

    def mix(img, at, count, first):
        for s in range(shards):
            lanes = slice(s * LANES, (s + 1) * LANES)
            vals = head_blocks(v[pl.ds(img * head, head), lanes], heads, head)
            mixed[pl.ds(at, win), lanes] = dot(half[s, pl.ds(at, win), :cols], vals).astype(BF16)

    windows(ints, images, rows, mix, True)
    weights[3].wait()
    scaled = const_ref[1:2]
    flat = scaled - jnp.mean(scaled, axis=-1, keepdims=True)

    def finish(blk):
        at = block_rows(blk, size)
        residual = take(blk) + dot(mixed[at, :], wo[...])
        centred = residual - jnp.mean(residual, axis=-1, keepdims=True)
        variance = jnp.mean(centred * centred, axis=-1, keepdims=True)
        inverse = 1.0 / jnp.sqrt(variance + EPS)
        unit = centred * inverse
        none = jnp.sum(unit * const_ref[0:1], axis=-1, keepdims=True)
        gap = jnp.sum(unit * scaled, axis=-1, keepdims=True)
        both = jnp.where(iota((size, 128), 1) == 0, none, none + gap)
        logs[block_rows(blk, SB), :] = jnp.sum(both.reshape(SB, rows, 128), axis=1)
        d_res[at, :] = (inverse * (flat - unit * (gap / width))).astype(BF16)
        gradient(blk).start()

    loop(finish)
    log_out[...] = logs[...].T[: log_out.shape[0]]

    def settle(blk):
        for s in range(shards):
            for copy in results(blk, s):
                copy.wait()
        gradient(blk).wait()

    loop(settle)


def backward_kernel(
    ints, sign_ref, *rest, mine, arrivals, head, heads, rows, terms
):
    parts, rest = rest[:terms], rest[terms:]
    d_in, wo_in, v_in, p_in, q_in = rest[:5]
    arrived, rest = rest[5 : 5 + arrivals], rest[5 + arrivals :]
    outs, rest = rest[: len(mine)], rest[len(mine) :]
    d_res, wo, v, p, q, dm, d_att, ds, pd, acc, delta, sems, sem_d = rest
    cols = heads * head
    images = v.shape[1] // head
    size = SB * rows
    win = WIN * rows
    blocks = blocks_of(ints)
    used = pl.ds(0, q.shape[1] - win)

    def loop(body):
        def one(blk, carry):
            body(blk)
            return carry

        lax.fori_loop(0, blocks, one, 0)

    def arrival(blk):
        at = block_rows(blk, size)
        return pltpu.make_async_copy(d_in.at[at], d_res.at[at], sem_d.at[blk])

    loop(lambda blk: arrival(blk).start())
    copies = []
    for j, shard in enumerate(mine):
        lanes = pl.ds(shard * LANES, LANES)
        copies.append(
            [
                pltpu.make_async_copy(src, dst, sems.at[4 * j + n])
                for n, (src, dst) in enumerate(
                    (
                        (wo_in.at[lanes, :], wo.at[j]),
                        (v_in.at[:, lanes], v.at[j]),
                        (p_in.at[shard], p.at[j]),
                        (q_in.at[shard], q.at[j, used]),
                    )
                )
            ]
        )
    for n in range(4):
        for group in copies:
            group[n].start()

    def settle(n):
        for group in copies:
            group[n].wait()

    logits = sum(part[...] for part in parts[1:]) + parts[0][...]
    sign = sign_ref[...]
    factor = sign / (1.0 + jnp.exp(sign * (logits[0:1] - logits[1:2])))
    delta[...] = jnp.broadcast_to(factor, (128, factor.shape[1])).T
    tail = pl.ds(pl.multiple_of(blocks * size, size), win)
    for j in range(len(mine)):
        dm[j, tail, :] = jnp.zeros((win, LANES), BF16)
    settle(0)

    def carry_back(blk):
        at = block_rows(blk, size)
        arrival(blk).wait()
        for j in range(len(mine)):
            dm[j, at, :] = dot_nt(d_res[at, :], wo[j]).astype(BF16)

    loop(carry_back)
    settle(1)

    def attend(img, at, count, first):
        for j in range(len(mine)):
            vals = head_blocks(v[j, pl.ds(img * head, head), :], heads, head)
            d_att[j, pl.ds(at, win), :cols] = dot_nt(dm[j, pl.ds(at, win), :], vals)

    windows(ints, images, rows, attend, True)
    settle(2)

    def soften(blk):
        at = block_rows(blk, size)
        weight = delta[block_rows(blk, SB), :]
        weight = jnp.broadcast_to(weight[:, None, :], (SB, rows, 128)).reshape(size, 128)[:, :1]
        for j in range(len(mine)):
            prob = p[j, at, :cols]
            grad = d_att[j, at, :cols]
            inner = head_sum(grad * prob, head)
            weighted = prob * weight
            ds[j, at, :cols] = (weighted * (grad - inner)).astype(BF16)
            pd[j, at, :cols] = weighted.astype(BF16)

    loop(soften)
    settle(3)
    for j in range(len(mine)):
        q[j, tail, :] = jnp.zeros((win, LANES), BF16)
    lane_head = iota((head, LANES), 1) // head
    place = iota((win, cols), 0)

    def diagonal(block):
        total = block[:head]
        for h in range(1, heads):
            total = jnp.where(lane_head == h, block[h * head : (h + 1) * head], total)
        return total[:, :cols]

    def outer(img, at, count, first):
        own = place < count
        here = pl.ds(at, win)
        zero = jnp.zeros((win, cols), BF16)
        for j in range(len(mine)):
            dk = diagonal(dot_tn(jnp.where(own, ds[j, here, :cols], zero), q[j, here, :]))
            dv = diagonal(dot_tn(jnp.where(own, pd[j, here, :cols], zero), dm[j, here, :]))
            term = jnp.concatenate([dk, dv], axis=-1)
            if first:
                acc[j, img * head : (img + 1) * head, :] = term
            else:
                acc[j, pl.ds(pl.multiple_of(img * head, head), head), :] += term

    windows(ints, images, rows, outer, False)
    for j, out_ref in enumerate(outs):
        total = acc[j]
        for a in arrived:
            total = total + a[...].astype(F32)
        out_ref[...] = total.astype(out_ref.dtype)


def whole(a):
    return pl.BlockSpec(a.shape, lambda *_: (0,) * a.ndim)


def local(
    images, query_states, neg_caption, neg_image, cross_query, cross_kv, cross_out, norm_gain,
    itm_weight,
):
    pair_count, patches, vis = images.shape
    queries, width = query_states.shape[1:]
    cols = cross_query.shape[1]
    head = width // HEADS
    scale = 1.0 / head**0.5
    groups = lax.axis_size("dp")
    shards = lax.axis_size("mp")
    dp, mp = lax.axis_index("dp"), lax.axis_index("mp")
    core = dp % NC
    rows = queries // shards
    half = width // 2

    def around(x, by):
        return lax.ppermute(x, "mp", [(i, (i + by) % shards) for i in range(shards)])

    def shift(x, by_z, by_x, by_core):
        moves = []
        for i in range(groups):
            z, x_, c = i // (NX * NC), i // NC % NX, i % NC
            to = ((z + by_z) % NZ * NX + (x_ + by_x) % NX) * NC + (c + by_core) % NC
            moves.append((i, to))
        return lax.ppermute(x, "dp", moves)

    own_rows = lax.dynamic_slice_in_dim(query_states, mp * rows, rows, 1)
    packed = jnp.concatenate([own_rows[:, :, :half], own_rows[:, :, half:]], axis=1)
    pool = lax.all_gather(packed[:GATHERED], "dp", axis=0, tiled=True)
    number = jnp.stack([neg_image // 32, neg_image % 32], axis=-1).astype(BF16)
    number = jnp.pad(number, ((0, 2 * rows - pair_count), (0, half - 2)))
    part = jnp.concatenate([packed[GATHERED:], number[None]], axis=0)
    units = part.shape[0]
    line = jnp.concatenate([part] + [shift(part, 0, -d, 0) for d in range(1, NX)], axis=0)
    up, down = [line], [line]
    for _ in range(NZ // 2 - 1):
        up.append(shift(up[-1], -1, 0, 0))
        down.append(shift(down[-1], 1, 0, 0))
    cut = NX // 2 * units
    across = [shift(up[-1][:cut], -1, 0, 0), shift(down[-1][cut:], 1, 0, 0)]
    carried = jnp.concatenate(up + across + down[:0:-1], axis=0)
    carried_other = shift(carried, 0, 0, 1)
    numbers = [x.reshape(-1, units, 2 * rows, half) for x in (carried, carried_other)]

    halves = [
        jnp.concatenate([cross_kv[0].T, cross_query.T], axis=1),
        jnp.concatenate([cross_kv[1].T, cross_out], axis=1),
    ]
    brought = jnp.where(core == 0, halves[0], halves[1])
    got = [around(brought, shards - s) for s in range(1, shards)]
    swap = [shift(g, 0, 0, 1) for g in got]
    flat = images.reshape(pair_count * patches, vis)
    params = pltpu.CompilerParams(vmem_limit_bytes=56 * 2**20)
    smem = pl.BlockSpec(memory_space=pltpu.SMEM)
    anywhere = pl.BlockSpec(memory_space=pl.ANY)
    vmem = pl.BlockSpec(memory_space=pltpu.VMEM)
    tall = shards * LANES
    out_rows = vis // groups
    pad_rows = (out_rows + 1 + 7) // 8 * 8
    chips = groups // NC
    shapes = [
        (pair_count * patches, tall), (pair_count * patches, tall), (tall, width), (tall, width),
        (groups * pad_rows, pair_count * patches),
    ]
    keys, values, wq, wo, spread = pl.pallas_call(
        functools.partial(project_kernel, shards=shards, cols=cols, vis=vis, out_rows=out_rows),
        in_specs=[smem] + [anywhere] * (1 + 2 * shards),
        out_specs=[anywhere] * 5,
        scratch_shapes=[
            pltpu.VMEM(flat.shape, BF16),
            pltpu.VMEM((shards, LANES, vis + width), BF16),
            pltpu.VMEM((shards, LANES, vis + width), BF16),
            pltpu.VMEM(shapes[0], BF16),
            pltpu.VMEM(shapes[1], BF16),
            pltpu.VMEM(shapes[4], BF16),
            pltpu.SemaphoreType.DMA((1 + 2 * shards,)),
            pltpu.SemaphoreType.DMA((1 + 4 * shards,)),
        ],
        out_shape=[jax.ShapeDtypeStruct(shape, BF16) for shape in shapes],
        compiler_params=params,
        cost_estimate=pl.CostEstimate(
            flops=4 * 10**10, bytes_accessed=20 * 10**6, transcendentals=0
        ),
        name="project",
    )(core.astype(I32).reshape(1), flat, *halves, *got, *swap)

    most = pair_count * (2 + CE - 1) + 2 * groups
    n_slots = -(-(most + WIN - CE) // SB) * SB
    n_rows = n_slots * rows
    n_lanes = -(-n_slots // 128) * 128
    ints, sign, hit = pl.pallas_call(
        plan_kernel,
        in_specs=[
            smem, anywhere, anywhere, vmem,
        ],
        out_specs=[vmem] * 3,
        scratch_shapes=[
            pltpu.VMEM((NC, groups // NC, 2 * rows, 128), BF16),
            pltpu.SemaphoreType.DMA((NC,)),
        ],
        out_shape=[
            jax.ShapeDtypeStruct((8, n_slots), I32),
            jax.ShapeDtypeStruct((1, n_lanes), F32),
            jax.ShapeDtypeStruct((groups * pair_count, n_slots), BF16),
        ],
        compiler_params=params,
        name="plan",
    )(dp.astype(I32).reshape(1), *numbers, neg_caption.reshape(-1, 1))

    fold = norm_gain / queries
    const = jnp.stack([fold * itm_weight[:, 0], fold * (itm_weight[:, 1] - itm_weight[:, 0])])
    q_rows, prob, d_res, log_part = pl.pallas_call(
        functools.partial(forward_kernel, head=head, scale=scale),
        in_specs=[smem] + [anywhere] * 7 + [vmem],
        out_specs=[anywhere] * 3 + [vmem],
        scratch_shapes=[
            pltpu.VMEM((n_slots, 2 * rows, half), BF16),
            pltpu.VMEM(wq.shape, BF16),
            pltpu.VMEM(keys.shape, BF16),
            pltpu.VMEM(values.shape, BF16),
            pltpu.VMEM(wo.shape, BF16),
            pltpu.VMEM((shards, n_rows, LANES), BF16),
            pltpu.VMEM((shards, n_rows, LANES), F32),
            pltpu.VMEM((shards, n_rows, LANES), BF16),
            pltpu.VMEM((n_rows, shards * LANES), BF16),
            pltpu.VMEM((n_rows, width), BF16),
            pltpu.VMEM((n_lanes, 128), F32),
            pltpu.SemaphoreType.DMA((n_slots // SB,)),
            pltpu.SemaphoreType.DMA((4,)),
            pltpu.SemaphoreType.DMA((3,)),
        ],
        out_shape=[
            jax.ShapeDtypeStruct((shards, n_rows, LANES), BF16),
            jax.ShapeDtypeStruct((shards, n_rows, LANES), F32),
            jax.ShapeDtypeStruct((n_rows, width), BF16),
            jax.ShapeDtypeStruct((8, n_lanes), F32),
        ],
        compiler_params=params,
        name="forward",
    )(ints, pool, carried, carried_other, wq, keys, values, wo, const)

    parts = [log_part] + [around(log_part, shards - s) for s in range(1, shards)]
    logits = jnp.zeros((2, n_slots), F32)
    for m in range(shards):
        for s in range(shards):
            logits = logits + jnp.where((mp + s) % shards == m, parts[s][:2, :n_slots], 0.0)
    logits = jnp.where(sign[:, :n_slots] != 0.0, logits, 0.0)

    def backward(mine, arrived=(), kind=BF16):
        shape = (pair_count * patches, 2 * cols)
        slack = n_rows + WIN * rows
        n = len(mine)
        return pl.pallas_call(
            functools.partial(
                backward_kernel, mine=mine, arrivals=len(arrived), head=head,
                heads=HEADS // shards, rows=rows, terms=shards,
            ),
            in_specs=[smem] + [vmem] * (1 + shards) + [anywhere] * 5 + [vmem] * len(arrived),
            out_specs=[vmem] * n,
            scratch_shapes=[
                pltpu.VMEM((n_rows, width), BF16),
                pltpu.VMEM((n, LANES, width), BF16),
                pltpu.VMEM((n, pair_count * patches, LANES), BF16),
                pltpu.VMEM((n, n_rows, LANES), F32),
                pltpu.VMEM((n, slack, LANES), BF16),
                pltpu.VMEM((n, slack, LANES), BF16),
                pltpu.VMEM((n, slack, LANES), F32),
                pltpu.VMEM((n, slack, LANES), BF16),
                pltpu.VMEM((n, slack, LANES), BF16),
                pltpu.VMEM((n,) + shape, F32),
                pltpu.VMEM((n_lanes, 128), F32),
                pltpu.SemaphoreType.DMA((4 * n,)),
                pltpu.SemaphoreType.DMA((n_slots // SB,)),
            ],
            out_shape=[jax.ShapeDtypeStruct(shape, kind)] * n,
            compiler_params=params,
            cost_estimate=pl.CostEstimate(flops=10**6, bytes_accessed=10**4, transcendentals=0),
            name="backward",
        )(ints, sign, *parts, d_res, wo, values, prob, q_rows, *arrived)

    two = around(backward((2,))[0], 2)
    one, three = backward((1, 3))
    one, three = around(one, 1), around(three, 3)
    own = backward((0,), (two,), F32)[0]
    d_kv = (own + one.astype(F32) + three.astype(F32)).astype(BF16)

    logit_hi = logits.astype(BF16)
    logit_lo = (logits - logit_hi.astype(F32)).astype(BF16)
    four = jnp.concatenate([logit_hi, logit_lo], axis=0)
    home = dot_nt(hit, four).astype(BF16)
    home = jnp.pad(
        home.reshape(groups, 1, 4 * pair_count),
        ((0, 0), (out_rows, pad_rows - out_rows - 1), (0, 2 * cols - 4 * pair_count)),
    )
    home, d_kv = lax.optimization_barrier((home, d_kv))
    grad = dot(spread, d_kv).reshape(groups, pad_rows, 2 * cols)
    over = shift((grad[chips:] + home[chips:]).astype(BF16), 0, 0, 1)
    leaving = (grad[:chips] + home[:chips] + over).astype(BF16)
    alike = [[chip * NC + c for chip in range(chips)] for c in range(NC)]
    arrived = lax.all_to_all(
        leaving, "dp", split_axis=0, concat_axis=0, tiled=True, axis_index_groups=alike
    )
    summed = jnp.sum(arrived.astype(F32), axis=0)
    grad_part = jnp.transpose(summed[:out_rows].reshape(out_rows, 2, cols), (1, 0, 2))
    back = summed[out_rows, : 4 * pair_count].reshape(pair_count, 2, 2)
    pushed_logits = back[:, 0] + back[:, 1]
    image = jnp.arange(pair_count, dtype=I32)[:, None]
    own_logits = []
    for j in range(2):
        here = ((ints[1:2] == image) & (ints[2:3] == j))[:, None, :]
        own_logits.append(jnp.sum(jnp.where(here, logits[None], 0.0), axis=-1))
    return (jnp.stack(own_logits + [pushed_logits]), grad_part)


def solution(mesh):
    return jax.shard_map(
        local,
        mesh=mesh,
        in_specs=(
            P("dp", None, None),
            P("dp", None, None),
            P("dp"),
            P("dp"),
            P(None, "mp"),
            P(None, None, "mp"),
            P("mp", None),
            P(),
            P(),
        ),
        out_specs=(P(None, "dp", None), P(None, "dp", "mp")),
        check_vma=False,
    )
```
